256 devices in a mesh: gx: 8 (over y, core), gy: 32 (over x, z).
Axes of the slice: x: 4, y: 4, z: 8, core: 2. Of those that a mesh axis runs over, the one named last changes fastest.
Arguments:
- inputs: bfloat16 [32, 64, 128, 128], P(None, 'gx', 'gy'), may hold values from -6 to 6
- cotangent: bfloat16 [32, 64, 128, 128], P(None, 'gx', 'gy'), may hold values from -6 to 6
- kernel: bfloat16 [3, 3, 3, 32, 32], replicated, may hold values from -0.21875 to 0.21875
- channel_bias: float32 [32], replicated, may hold values from -3 to 3
- spectral: bfloat16 [32, 32, 4096], replicated, may hold values from -3 to 3
Outputs:
- outputs: bfloat16 [32, 64, 128, 128], P(None, 'gx', 'gy')
- input_grad: bfloat16 [32, 64, 128, 128], P(None, 'gx', 'gy')
- spectral_grad: float32 [32, 32, 4096], P(None, None, ('gx', 'gy'))
- kernel_grad: float32 [3, 3, 3, 32, 32], replicated
- bias_grad: float32 [32], replicated
The draws below stay inside these ranges and needn't reach their ends.
All inputs are finite; a program needn't handle non-finite values.
Results may differ from the reference program's by a relative error of at most 0.005.
Values may be sent and summed in bfloat16 or wider, within the bound.
A program may use at most 128 MiB of HBM per device.

```python
import math
import jax
import jax.numpy as jnp
from jax import lax

C = 32
MODES = 16
NZ = 128
NX = 64
NY = 128


def shard_levels(own_key, shape, shards, smallest, top_value):
    def one(dim, shards_of):
        steps = jax.random.uniform(jax.random.fold_in(jax.random.fold_in(own_key, 6), dim), (shards_of,), jnp.float32, smallest / len(shards), top_value / len(shards))
        return jnp.repeat(jnp.exp(steps), shape[dim] // shards_of).reshape((-1,) + (1,) * (len(shape) - dim - 1))

    gain = one(*shards[0])
    for cut in shards[1:]:
        gain = gain * one(*cut)
    return gain


def scatter_about(rng, dims, width, limit, pieces=(), held_as=jnp.bfloat16):
    values = jax.random.normal(rng, dims, jnp.float32) * width
    if len(pieces) > 0:
        values = shard_levels(rng, dims, pieces, -0.22, 0.18) * values
    return jnp.clip(values, min=-limit, max=limit).astype(held_as)


def setup_inputs(seed: int = 0) -> dict:
    key_list = jax.random.split(jax.random.key(seed), 6)
    inputs = scatter_about(key_list[0], (C, NX, NY, NZ), 1.0, 6.0, ((1, 8), (2, 32)))
    cotangent = scatter_about(key_list[1], (C, NX, NY, NZ), 1.0, 6.0, ((1, 8), (2, 32)))
    kernel = scatter_about(key_list[2], (3, 3, 3, C, C), (27 * C) ** -0.5, 0.21875)
    channel_bias = scatter_about(key_list[3], (C,), 0.5, 3.0, (), jnp.float32)
    spectral = scatter_about(key_list[4], (C, C, MODES ** 3), 0.5, 3.0)
    return dict(inputs=inputs, cotangent=cotangent, kernel=kernel, channel_bias=channel_bias, spectral=spectral)


highest = lax.Precision.HIGHEST

def basis_rows(mode_count, cell_count, length, start_cell):
    mode_rows = jnp.arange(mode_count, dtype=jnp.int32)
    half_modes = mode_count // 2
    frequency = jnp.where(mode_rows < half_modes, mode_rows, mode_rows - half_modes + 1)
    positions = start_cell + jnp.arange(cell_count, dtype=jnp.int32)
    phase_index = frequency[:, None] * positions[None, :] % length
    angles = phase_index.astype(jnp.float32) * (2.0 * math.pi / length)
    return jnp.where((mode_rows < half_modes)[:, None], jnp.cos(angles), jnp.sin(angles))

def analyse(values, basis_x, basis_y, basis_z):
    partial_value = jnp.einsum('cxyz,rz->cxyr', values, basis_z, precision=highest)
    partial_value = jnp.einsum('cxyr,qy->cxqr', partial_value, basis_y, precision=highest)
    partial_value = jnp.einsum('cxqr,px->cpqr', partial_value, basis_x, precision=highest)
    return partial_value.reshape(partial_value.shape[0], -1)

def synthesise(coeff_rows, basis_x, basis_y, basis_z):
    mode_count = basis_x.shape[0]
    mode_grid = coeff_rows.reshape(coeff_rows.shape[0], mode_count, mode_count, mode_count)
    partial_value = jnp.einsum('opqr,px->oxqr', mode_grid, basis_x, precision=highest)
    partial_value = jnp.einsum('oxqr,qy->oxyr', partial_value, basis_y, precision=highest)
    return jnp.einsum('oxyr,rz->oxyz', partial_value, basis_z, precision=highest)

def convolve(values, kernel_f32):
    weights = jnp.transpose(kernel_f32, (3, 4, 0, 1, 2))
    result = lax.conv_general_dilated(values[None], weights, (1, 1, 1), [(1, 1), (1, 1), (1, 1)], dimension_numbers=('NCDHW', 'OIDHW', 'NCDHW'), precision=highest)
    return result[0]

def gelu_tanh(values):
    return jax.nn.gelu(values, approximate=True)

def reference(inputs, cotangent, kernel, channel_bias, spectral):
    channels, count_x, count_y, length_z = inputs.shape
    basis_x = basis_rows(MODES, count_x, count_x, 0)
    basis_y = basis_rows(MODES, count_y, count_y, 0)
    basis_z = basis_rows(MODES, length_z, length_z, 0)
    grid_scale = 1.0 / math.sqrt(count_x * count_y * length_z)
    mode_scale = 1.0 / math.sqrt(MODES ** 3)
    whole_grid = inputs.astype(jnp.float32)
    spectral_f32 = spectral.astype(jnp.float32)
    coeffs = analyse(whole_grid, basis_x, basis_y, basis_z) * grid_scale
    mixed_modes = jnp.einsum('ocm,cm->om', spectral_f32, coeffs, precision=highest)
    local_term, pullback = jax.vjp(convolve, whole_grid, kernel.astype(jnp.float32))
    preact = local_term + synthesise(mixed_modes, basis_x, basis_y, basis_z) * mode_scale
    preact = preact + channel_bias[:, None, None, None]
    outputs = gelu_tanh(preact).astype(jnp.bfloat16)
    slope_grad = jax.vjp(gelu_tanh, preact)[1](cotangent.astype(jnp.float32))[0]
    delta_grad = lax.optimization_barrier(slope_grad.astype(jnp.bfloat16))
    delta_f32 = delta_grad.astype(jnp.float32)
    conv_grad, kernel_sum = pullback(delta_f32)
    back_modes = analyse(delta_f32, basis_x, basis_y, basis_z) * mode_scale
    spectral_grad = back_modes[:, None, :] * coeffs[None, :, :]
    input_modes = jnp.einsum('ocm,om->cm', spectral_f32, back_modes, precision=highest)
    spectral_term = synthesise(input_modes, basis_x, basis_y, basis_z) * grid_scale
    input_grad = (conv_grad + spectral_term).astype(jnp.bfloat16)
    kernel_grad = kernel_sum * grid_scale
    bias_grad = lax.optimization_barrier(jnp.sum(delta_f32, axis=(1, 2, 3))) * grid_scale
    return (outputs, input_grad, spectral_grad, kernel_grad, bias_grad)
```

```python
import functools
import math

import jax
import jax.numpy as jnp
import numpy as np
from jax import lax
from jax.experimental import pallas as pl
from jax.experimental.pallas import tpu as pltpu
from jax.sharding import PartitionSpec as P

MESH = pl.DeviceIdType.MESH
MODES = 16
C = 32
BX, BY, NZ = 8, 4, 128
NX, NY = 64, 128
LANES = BY * NZ
WIDE = (BY + 2) * NZ
NEIGHBOURS = [(i, j) for i in (-1, 0, 1) for j in (-1, 0, 1) if (i, j) != (0, 0)]
GRID_SCALE = 1.0 / math.sqrt(NX * NY * NZ)
MODE_SCALE = 1.0 / math.sqrt(MODES**3)
KG_ROWS = 32
KG_SHARES = 9
f32, bf16 = jnp.float32, jnp.bfloat16
DOT_NT = (((1,), (1,)), ((), ()))
DOT_TN = (((0,), (0,)), ((), ()))
DOT_NN = (((1,), (0,)), ((), ()))


def basis(cells):
    rows = np.arange(MODES)
    frequency = np.where(rows < MODES // 2, rows, rows - MODES // 2 + 1)
    phase = frequency[:, None] * np.arange(cells)[None, :] % cells
    angles = phase * (2.0 * math.pi / cells)
    return np.where((rows < MODES // 2)[:, None], np.cos(angles), np.sin(angles)).astype(np.float32)


def split(array):
    high = array.astype(jnp.bfloat16)
    low = (array - high.astype(np.float32)).astype(jnp.bfloat16)
    return high, low


def tables():
    phi_x, phi_y, phi_z = basis(NX), basis(NY), basis(NZ)
    high, low = split(phi_z)
    z_analysis = np.concatenate([high, low], 0)
    z_synthesis = np.concatenate([high, high, low], 0)
    lanes = np.repeat(phi_y.reshape(MODES, 32, BY), C, axis=2)
    y_table = lanes.reshape(MODES, 2, 16, BY * C).transpose(2, 1, 0, 3)
    x_table = phi_x.T.reshape(-1)
    return z_analysis, z_synthesis, np.ascontiguousarray(y_table), np.ascontiguousarray(x_table)


def dot(a, b, dims):
    return lax.dot_general(a, b, dims, preferred_element_type=f32)


def kernel(
    x_hbm, ct_hbm, spec_hbm, wf_ref, wb_ref, bias_ref, za_ref, zs_ref, py_ref, px_ref,
    out_hbm, ig_hbm, sg_ref, kg_ref, bg_ref,
    xin, ctin, spec, flat, ct, acc, stk, dstk, dx, tbuf,
    sx, rx, sy, ry, sz, rz, ct_modes, coefs, mixed, mt, rzf,
    sxb, rxb, syb, ryb, szb, rzb,
    kgp, kr1, ks2, kr2, ks3, kr3,
    oflat, obf, ibf,
    dma_sem, halo_s, halo_r, xs, xr, ys, yr, zs, zr, k1s, k1r, k2s, k2r, k3s, k3r,
):
    a, b = lax.axis_index("gx"), lax.axis_index("gy")
    h, q = b // 16, lax.rem(b, 16)
    g = 2 * a + h

    load_x = pltpu.make_async_copy(x_hbm, xin, dma_sem.at[0])
    load_ct = pltpu.make_async_copy(ct_hbm, ctin, dma_sem.at[1])
    load_spec = pltpu.make_async_copy(
        spec_hbm.at[:, :, pl.ds(pl.multiple_of(g * 256, 256), 256)], spec, dma_sem.at[2]
    )
    load_x.start()
    load_ct.start()
    load_spec.start()

    def group_x(k):
        t = lax.rem(g + k, 16)
        return t, (t // 2, q + 16 * lax.rem(t, 2))

    def group_y(k):
        t = lax.rem(q + k, 16)
        return t, (a, t + 16 * h)

    def there(da, db):
        ok = None
        if da == 1:
            ok = a < 7
        if da == -1:
            ok = a > 0
        if db == 1:
            ok = (b < 31) if ok is None else ok & (b < 31)
        if db == -1:
            ok = (b > 0) if ok is None else ok & (b > 0)
        return ok

    barrier = pltpu.get_barrier_semaphore()

    def greet(k, carry):
        pl.semaphore_signal(barrier, inc=1, device_id=group_x(k)[1], device_id_type=MESH)
        pl.semaphore_signal(barrier, inc=1, device_id=group_y(k)[1], device_id_type=MESH)
        return carry

    lax.fori_loop(1, 16, greet, 0)
    awaited = 30
    for da, db in NEIGHBOURS:
        if db == 0:
            continue

        @pl.when(there(da, db))
        def _():
            pl.semaphore_signal(barrier, inc=1, device_id=(a + da, b + db), device_id_type=MESH)

        awaited = awaited + jnp.where(there(da, db), 1, 0)

    def x_copy(t, peer, src, buf, ssem, rsem):
        return pltpu.make_async_remote_copy(
            src_ref=src, dst_ref=buf.at[g], send_sem=ssem.at[t], recv_sem=rsem.at[g],
            device_id=peer, device_id_type=MESH,
        )

    def y_copy(t, peer, src, buf, ssem, rsem):
        return pltpu.make_async_remote_copy(
            src_ref=src, dst_ref=buf.at[q], send_sem=ssem.at[t], recv_sem=rsem.at[q],
            device_id=peer, device_id_type=MESH,
        )

    def arrived(t, peer, buf, ssem, rsem):
        pltpu.make_async_remote_copy(
            src_ref=buf.at[t], dst_ref=buf.at[t], send_sem=ssem.at[t], recv_sem=rsem.at[t],
            device_id=peer, device_id_type=MESH,
        ).wait_recv()

    def each(members, action):
        def step(k, carry):
            t, peer = members(k)
            action(t, peer)
            return carry

        lax.fori_loop(1, 16, step, 0)

    def halo_copy(index, field, n, da, db):
        sx_ = pl.ds(8, 1) if da == 1 else pl.ds(1, 1) if da == -1 else pl.ds(1, 8)
        dx_ = pl.ds(0, 1) if da == 1 else pl.ds(9, 1) if da == -1 else pl.ds(1, 8)
        sl = pl.ds(512, 128) if db == 1 else pl.ds(128, 128) if db == -1 else pl.ds(128, 512)
        dl = pl.ds(0, 128) if db == 1 else pl.ds(640, 128) if db == -1 else pl.ds(128, 512)
        return pltpu.make_async_remote_copy(
            src_ref=field.at[sx_, pl.ds(32, 32), sl], dst_ref=field.at[dx_, pl.ds(32, 32), dl],
            send_sem=halo_s.at[n, index], recv_sem=halo_r.at[n, index],
            device_id=(a + da, b + db), device_id_type=MESH,
        )

    def halo_start(field, n):
        for index, (da, db) in enumerate(NEIGHBOURS):

            @pl.when(there(da, db))
            def _():
                halo_copy(index, field, n, da, db).start()

    def halo_wait_recv(field, n):
        for index, (da, db) in enumerate(NEIGHBOURS):

            @pl.when(there(-da, -db))
            def _():
                halo_copy(index, field, n, da, db).wait_recv()

    def halo_wait_send(field, n):
        for index, (da, db) in enumerate(NEIGHBOURS):

            @pl.when(there(da, db))
            def _():
                halo_copy(index, field, n, da, db).wait_send()

    def zero_rim(field):
        @pl.when(a == 0)
        def _():
            field[0, 32:64, :] = jnp.zeros((C, WIDE), bf16)

        @pl.when(a == 7)
        def _():
            field[9, 32:64, :] = jnp.zeros((C, WIDE), bf16)

        @pl.when(b == 0)
        def _():
            for i in range(10):
                field[i, 32:64, 0:128] = jnp.zeros((C, NZ), bf16)

        @pl.when(b == 31)
        def _():
            for i in range(10):
                field[i, 32:64, 640:768] = jnp.zeros((C, NZ), bf16)

    def z_analyse(i, tiles):
        rows = jnp.concatenate(tiles, axis=0)
        both = dot(za_ref[...], rows, DOT_NT)
        tbuf[i] = both[:16] + both[16:]

    def x_partials(buf):
        rows = [tbuf[i] for i in range(BX)]

        def step(p, carry):
            total = px_ref[(a * 8) * 16 + p] * rows[0]
            for i in range(1, BX):
                total = total + px_ref[(a * 8 + i) * 16 + p] * rows[i]
            buf[p] = total.astype(bf16)
            return carry

        lax.fori_loop(0, 16, step, 0)

    def y_blocks(recv, send):
        for half in range(2):
            total = recv[half].astype(f32)
            for i in range(1, 8):
                total = total + recv[2 * i + half].astype(f32)
            send[half] = total.astype(bf16)

    def y_analyse(recv):
        def step(block, carry):
            result = list(carry)
            for half in range(2):
                value = recv[block, half].astype(f32)
                for m in range(MODES):
                    result[m] = result[m] + value * py_ref[block, half, pl.ds(m, 1), :]
            return tuple(result)

        start = tuple(jnp.zeros((16, 128), f32) for _ in range(MODES))
        return lax.fori_loop(0, 16, step, start)

    def to_columns(parts, scale):
        wide = jnp.transpose(jnp.concatenate(parts, axis=0))
        return (wide[0:32] + wide[32:64] + wide[64:96] + wide[96:128]) * scale

    def y_synthesise(modes, scale, send):
        tall = jnp.transpose(jnp.concatenate([modes * scale] * 4, axis=0))
        for half in range(2):
            total = py_ref[q, half, pl.ds(0, 1), :] * tall[0:16]
            for m in range(1, MODES):
                total = total + py_ref[q, half, pl.ds(m, 1), :] * tall[16 * m : 16 * m + 16]
            send[half] = total.astype(bf16)

    def x_z_synthesise(i):
        total = px_ref[(a * 8 + i) * 16] * rzf[0]
        for p in range(1, MODES):
            total = total + px_ref[(a * 8 + i) * 16 + p] * rzf[p]
        high = total.astype(bf16)
        low = (total - high.astype(f32)).astype(bf16)
        return dot(jnp.concatenate([high, low, high], axis=0), zs_ref[...], DOT_TN)

    lane = lax.broadcasted_iota(jnp.int32, (C, NZ), 1)

    def shift_rows(field, ones):
        def step(i, carry):
            for y in range(BY + 2):
                cells = slice(y * NZ, (y + 1) * NZ)
                value = field[i, 32:64, cells].astype(f32)
                before = jnp.where(lane == 0, 0.0, pltpu.roll(value, 1, 1))
                after = jnp.where(lane == NZ - 1, 0.0, pltpu.roll(value, NZ - 1, 1))
                field[i, 0:32, cells] = before.astype(bf16)
                field[i, 64:96, cells] = after.astype(bf16)
            return carry

        lax.fori_loop(0, 10, step, 0)

    def fill_ones(field):
        def step(i, carry):
            field[i, 96:128, :] = jnp.ones((32, WIDE), bf16)
            return carry

        lax.fori_loop(0, 10, step, 0)

    def convolve(field, weights):
        def step(i, carry):
            total = None
            for d in range(3):
                for e in range(3):
                    tap = (d * 3 + e) * 128
                    part = dot(
                        weights[:, tap : tap + 128], field[i + d, :, e * NZ : e * NZ + LANES], DOT_NN
                    )
                    total = part if total is None else total + part
            acc[i] = total
            return carry

        lax.fori_loop(0, BX, step, 0)

    def unflatten(source, write):
        def step(c, carry):
            flat[pl.ds(pl.multiple_of(c * 32, 32), 32), :] = source[c].astype(f32)
            return carry

        lax.fori_loop(0, C, step, 0)

        def step2(i, carry):
            tiles = [flat[pl.ds(i * BY + y, C, stride=32), :] for y in range(BY)]
            write(i, tiles)
            return carry

        lax.fori_loop(0, BX, step2, 0)

    def flatten(source, target):
        def step(c, carry):
            target[c] = source[pl.ds(pl.multiple_of(c * 32, 32), 32), :].astype(bf16)
            return carry

        lax.fori_loop(0, C, step, 0)

    load_x.wait()

    def write_x(i, tiles):
        tiles = [t.astype(bf16) for t in tiles]
        for y in range(BY):
            stk[i + 1, 32:64, (y + 1) * NZ : (y + 2) * NZ] = tiles[y]
        z_analyse(i, tiles)

    unflatten(xin, write_x)
    x_partials(sx)
    pl.semaphore_wait(barrier, awaited)
    each(group_x, lambda t, peer: x_copy(t, peer, sx.at[t], rx, xs.at[0], xr.at[0]).start())
    rx[g] = sx[g]
    halo_start(stk, 0)

    zero_rim(stk)
    fill_ones(stk)
    load_ct.wait()

    def write_ct(i, tiles):
        for y in range(BY):
            ct[i, :, y * NZ : (y + 1) * NZ] = tiles[y]

    unflatten(ctin, write_ct)
    for i in (0, 1, 10, 11):
        dx[i] = jnp.zeros((C, LANES), bf16)

    each(group_x, lambda t, peer: arrived(t, peer, rx, xs.at[0], xr.at[0]))
    y_blocks(rx, sy)
    each(group_y, lambda t, peer: y_copy(t, peer, sy, ry, ys.at[0], yr.at[0]).start())
    ry[q] = sy[...]

    halo_wait_recv(stk, 0)
    shift_rows(stk, True)
    convolve(stk, wf_ref)
    load_spec.wait()

    each(group_y, lambda t, peer: arrived(t, peer, ry, ys.at[0], yr.at[0]))
    parts = y_analyse(ry)
    for m in range(MODES):
        ct_modes[0, m] = parts[m]
    coefs[...] = to_columns(parts, GRID_SCALE)

    def mix(o, carry):
        mixed[pl.ds(o, 1), :] = jnp.sum(spec[o].astype(f32) * coefs[...], axis=0, keepdims=True)
        return carry

    lax.fori_loop(0, C, mix, 0)
    y_synthesise(mixed[...], MODE_SCALE, sz)
    each(group_x, lambda t, peer: x_copy(t, peer, sz.at[lax.rem(t, 2)], rz, zs.at[0], zr.at[0]).start())
    rz[g] = sz[h]
    each(group_x, lambda t, peer: arrived(t, peer, rz, zs.at[0], zr.at[0]))
    for p in range(MODES):
        rzf[p] = rz[p].astype(f32)

    root = math.sqrt(2.0 / math.pi)

    def point(i, carry):
        modes = x_z_synthesise(i)
        tiles = []
        for y in range(BY):
            cells = slice(y * NZ, (y + 1) * NZ)
            v = acc[i, :, cells] + modes[y * C : (y + 1) * C] + bias_ref[...]
            square = v * v
            t = jnp.tanh(root * (v + 0.044715 * (square * v)))
            half = 0.5 * (1.0 + t)
            slope = half + 0.5 * v * (1.0 - t * t) * (root * (1.0 + 3 * 0.044715 * square))
            oflat[pl.ds(i * BY + y, C, stride=32), :] = v * half
            delta = (ct[i, :, cells] * slope).astype(bf16)
            dstk[i + 1, 32:64, (y + 1) * NZ : (y + 2) * NZ] = delta
            dx[i + 2, :, cells] = delta
            tiles.append(delta)
        z_analyse(i, tiles)
        return carry

    lax.fori_loop(0, BX, point, 0)

    x_partials(sxb)
    each(group_x, lambda t, peer: x_copy(t, peer, sxb.at[t], rxb, xs.at[1], xr.at[1]).start())
    rxb[g] = sxb[g]
    halo_start(dstk, 1)

    zero_rim(dstk)
    fill_ones(dstk)
    flatten(oflat, obf)
    store_out = pltpu.make_async_copy(obf, out_hbm, dma_sem.at[3])
    store_out.start()

    kgp[...] = jnp.zeros((9, C, 128), f32)

    def kernel_step(i, carry):
        rows = jnp.concatenate([dx[i + 2], dx[i + 1], dx[i]], axis=0)
        for e in range(3):
            part = dot(rows, stk[i, :, e * NZ : e * NZ + LANES], DOT_NT)
            for d in range(3):
                kgp[e * 3 + d] += part[d * C : (d + 1) * C]
        return carry

    each(group_x, lambda t, peer: arrived(t, peer, rxb, xs.at[1], xr.at[1]))
    y_blocks(rxb, syb)
    each(group_y, lambda t, peer: y_copy(t, peer, syb, ryb, ys.at[1], yr.at[1]).start())
    ryb[q] = syb[...]

    lax.fori_loop(0, 10, kernel_step, 0)

    def k1_start(t, peer):
        @pl.when(t < KG_SHARES)
        def _():
            x_copy(t, peer, kgp.at[t], kr1, k1s, k1r).start()

    each(group_x, k1_start)

    halo_wait_recv(dstk, 1)
    shift_rows(dstk, False)
    convolve(dstk, wb_ref)

    @pl.when(g < KG_SHARES)
    def _():
        kr1[g] = kgp[g]
        each(group_x, lambda t, peer: arrived(t, peer, kr1, k1s, k1r))
        total = kr1[0]
        for i in range(1, 16):
            total = total + kr1[i]
        ks2[...] = total
        kr2[q] = total
        each(group_y, lambda t, peer: y_copy(t, peer, ks2, kr2, k2s, k2r).start())

    each(group_y, lambda t, peer: arrived(t, peer, ryb, ys.at[1], yr.at[1]))
    parts = y_analyse(ryb)
    for m in range(MODES):
        ct_modes[1, m] = parts[m]
    mixed[...] = to_columns(parts, MODE_SCALE)

    def mix_back(o, carry):
        return carry + spec[o].astype(f32) * mixed[pl.ds(o, 1), :]

    back = lax.fori_loop(0, C, mix_back, jnp.zeros((C, 256), f32))
    y_synthesise(back, GRID_SCALE, szb)
    each(group_x, lambda t, peer: x_copy(t, peer, szb.at[lax.rem(t, 2)], rzb, zs.at[1], zr.at[1]).start())
    rzb[g] = szb[h]

    @pl.when(g < KG_SHARES)
    def _():
        each(group_y, lambda t, peer: arrived(t, peer, kr2, k2s, k2r))
        total = kr2[0]
        for i in range(1, 16):
            total = total + kr2[i]
        total = total * GRID_SCALE
        ks3[...] = total
        kr3[g] = total
        each(group_x, lambda t, peer: x_copy(t, peer, ks3, kr3, k3s, k3r).start())

    def columns_of(n, scale):
        wide = jnp.transpose(ct_modes[n, q])
        return (wide[0:32] + wide[32:64] + wide[64:96] + wide[96:128]) * scale

    coef_part = columns_of(0, GRID_SCALE)
    back_part = columns_of(1, MODE_SCALE)
    for o in range(C):
        sg_ref[o] = coef_part * back_part[o : o + 1, :]

    each(group_x, lambda t, peer: arrived(t, peer, rzb, zs.at[1], zr.at[1]))
    for p in range(MODES):
        rzf[p] = rzb[p].astype(f32)

    store_out.wait()

    def last(i, carry):
        modes = x_z_synthesise(i)
        for y in range(BY):
            cells = slice(y * NZ, (y + 1) * NZ)
            oflat[pl.ds(i * BY + y, C, stride=32), :] = acc[i, :, cells] + modes[y * C : (y + 1) * C]
        return carry

    lax.fori_loop(0, BX, last, 0)
    flatten(oflat, ibf)
    store_ig = pltpu.make_async_copy(ibf, ig_hbm, dma_sem.at[4])
    store_ig.start()

    def k3_arrived(t, peer):
        @pl.when(t < KG_SHARES)
        def _():
            arrived(t, peer, kr3, k3s, k3r)

    each(group_x, k3_arrived)
    for d in range(3):
        for e in range(3):
            block = kr3[e * 3 + d]
            for f in range(3):
                moved = block if f == 0 else pltpu.roll(block, 128 - 32 * f, 1)
                kg_ref[(d * 3 + e) * 3 + f] = moved[:, 0:32]
    bg_ref[...] = jnp.transpose(kr3[4])[96:97, :]

    for n, (s, r, z) in enumerate(((sx, rx, sz), (sxb, rxb, szb))):
        zr_ = (rz, rzb)[n]
        y_s, y_r = ((sy, ry), (syb, ryb))[n]

        def left_x(t, peer):
            x_copy(t, peer, s.at[t], r, xs.at[n], xr.at[n]).wait_send()
            x_copy(t, peer, z.at[lax.rem(t, 2)], zr_, zs.at[n], zr.at[n]).wait_send()

        each(group_x, left_x)
        each(group_y, lambda t, peer: y_copy(t, peer, y_s, y_r, ys.at[n], yr.at[n]).wait_send())
    halo_wait_send(stk, 0)
    halo_wait_send(dstk, 1)

    def k1_left(t, peer):
        @pl.when(t < KG_SHARES)
        def _():
            x_copy(t, peer, kgp.at[t], kr1, k1s, k1r).wait_send()

    each(group_x, k1_left)

    @pl.when(g < KG_SHARES)
    def _():
        each(group_y, lambda t, peer: y_copy(t, peer, ks2, kr2, k2s, k2r).wait_send())
        each(group_x, lambda t, peer: x_copy(t, peer, ks3, kr3, k3s, k3r).wait_send())

    store_ig.wait()


def layer(inputs, cotangent, weights, channel_bias, spectral):
    z_analysis, z_synthesis, y_table, x_table = tables()
    x = inputs.reshape(C, BX * BY, NZ)
    ct = cotangent.reshape(C, BX * BY, NZ)
    pad = ((0, 0), (0, 0), (0, 32))
    forward = jnp.pad(weights.transpose(3, 0, 1, 2, 4).reshape(C, 9, 96), pad).reshape(C, 1152)
    flipped = weights[::-1, ::-1, ::-1]
    backward = jnp.pad(flipped.transpose(4, 0, 1, 2, 3).reshape(C, 9, 96), pad).reshape(C, 1152)
    any_space = pl.BlockSpec(memory_space=pl.ANY)
    vmem = pl.BlockSpec(memory_space=pltpu.VMEM)
    smem = pl.BlockSpec(memory_space=pltpu.SMEM)
    dma = pltpu.SemaphoreType.DMA
    V = pltpu.VMEM
    mode_bufs = [
        V((16, 16, 128), bf16), V((16, 16, 128), bf16),
        V((2, 16, 128), bf16), V((16, 2, 16, 128), bf16),
        V((2, 16, 128), bf16), V((16, 16, 128), bf16),
    ]
    outputs, input_grad, spectral_grad, kernel_grad, bias_grad = pl.pallas_call(
        kernel,
        out_shape=(
            jax.ShapeDtypeStruct((C, BX * BY, NZ), bf16),
            jax.ShapeDtypeStruct((C, BX * BY, NZ), bf16),
            jax.ShapeDtypeStruct((C, C, 16), f32),
            jax.ShapeDtypeStruct((27, C, C), f32),
            jax.ShapeDtypeStruct((1, C), f32),
        ),
        in_specs=[any_space] * 3 + [vmem] * 6 + [smem],
        out_specs=(any_space, any_space, vmem, vmem, vmem),
        scratch_shapes=[
            V((C, 32, NZ), bf16), V((C, 32, NZ), bf16), V((C, C, 256), bf16),
            V((C * 32, NZ), f32), V((BX, C, LANES), f32), V((BX, C, LANES), f32),
            V((10, 128, WIDE), bf16), V((10, 128, WIDE), bf16), V((12, C, LANES), bf16),
            V((BX, 16, 128), f32),
            *mode_bufs,
            V((2, MODES, 16, 128), f32), V((C, 256), f32), V((C, 256), f32),
            V((256, 128), f32), V((MODES, 16, 128), f32),
            *mode_bufs,
            V((9, KG_ROWS, 128), f32), V((16, KG_ROWS, 128), f32),
            V((KG_ROWS, 128), f32), V((16, KG_ROWS, 128), f32),
            V((KG_ROWS, 128), f32), V((16, KG_ROWS, 128), f32),
            V((C * 32, NZ), f32), V((C, 32, NZ), bf16), V((C, 32, NZ), bf16),
            dma((5,)), dma((2, 8)), dma((2, 8)),
            *[dma((2, 16))] * 6,
            *[dma((16,))] * 6,
        ],
        compiler_params=pltpu.CompilerParams(
            collective_id=0, has_side_effects=True, vmem_limit_bytes=40 * 2**20
        ),
        cost_estimate=pl.CostEstimate(flops=700_000_000, bytes_accessed=4_000_000, transcendentals=131072),
    )(
        x, ct, spectral, forward, backward,
        jnp.broadcast_to(channel_bias[:, None], (C, 128)),
        z_analysis, z_synthesis, y_table, x_table,
    )
    field = (C, BX, BY, NZ)
    return (
        outputs.reshape(field), input_grad.reshape(field), spectral_grad,
        kernel_grad.reshape(3, 3, 3, C, C), bias_grad.reshape(C),
    )


def solution(mesh):
    placed = (P(None, "gx", "gy", None), P(None, "gx", "gy", None), P(), P(), P())
    return jax.shard_map(
        layer,
        mesh=mesh,
        in_specs=placed,
        out_specs=(
            P(None, "gx", "gy", None),
            P(None, "gx", "gy", None),
            P(None, None, ("gx", "gy")),
            P(),
            P(),
        ),
        check_vma=False,
    )
```

```python
import functools
import math

import jax
import jax.numpy as jnp
import numpy as np
from jax import lax
from jax.experimental import pallas as pl
from jax.experimental.pallas import tpu as pltpu
from jax.sharding import PartitionSpec as P

MESH = pl.DeviceIdType.MESH
MODES = 16
C = 32
BX, BY, NZ = 8, 4, 128
NX, NY = 64, 128
LANES = BY * NZ
WIDE = (BY + 2) * NZ
NEIGHBOURS = [(i, j) for i in (-1, 0, 1) for j in (-1, 0, 1) if (i, j) != (0, 0)]
GRID_SCALE = 1.0 / math.sqrt(NX * NY * NZ)
MODE_SCALE = 1.0 / math.sqrt(MODES**3)
KG_ROWS = 16
KG_SHARES = 14
f32, bf16 = jnp.float32, jnp.bfloat16
DOT_NT = (((1,), (1,)), ((), ()))
DOT_TN = (((0,), (0,)), ((), ()))
DOT_NN = (((1,), (0,)), ((), ()))


def basis(cells):
    rows = np.arange(MODES)
    frequency = np.where(rows < MODES // 2, rows, rows - MODES // 2 + 1)
    phase = frequency[:, None] * np.arange(cells)[None, :] % cells
    angles = phase * (2.0 * math.pi / cells)
    return np.where((rows < MODES // 2)[:, None], np.cos(angles), np.sin(angles)).astype(np.float32)


def split(array):
    high = array.astype(jnp.bfloat16)
    low = (array - high.astype(np.float32)).astype(jnp.bfloat16)
    return high, low


def tables():
    phi_x, phi_y, phi_z = basis(NX), basis(NY), basis(NZ)
    high, low = split(phi_z)
    z_analysis = np.concatenate([high, low], 0)
    z_synthesis = np.concatenate([high, high, low], 0)
    lanes = np.repeat(phi_y.reshape(MODES, 32, BY), C, axis=2)
    y_table = lanes.transpose(1, 0, 2)
    x_table = phi_x.T.reshape(-1)
    return z_analysis, z_synthesis, np.ascontiguousarray(y_table), np.ascontiguousarray(x_table)


def dot(a, b, dims):
    return lax.dot_general(a, b, dims, preferred_element_type=f32)


def kernel(
    x_hbm, ct_hbm, spec_hbm, w_hbm, bias_hbm, za_hbm, zs_hbm, py_hbm, px_hbm,
    out_hbm, ig_hbm, sg_ref, kg_ref, bg_ref,
    w_raw, bias_row, za_ref, zs_ref, py_ref, px_ref, wf_ref, wb_ref, bias_ref,
    xin, ctin, spec, flat, ct, acc, stk, dstk, dx, tbuf,
    sx, rx, sy, ry, sz, rz, ct_modes, coefs, mixed,
    sxb, rxb, syb, ryb, szb, rzb,
    kgp, ks1, kr1, ks2, kr2, ks3, kr3,
    oflat, obf, ibf,
    dma_sem, halo_s, halo_r, xs, xr, ys, yr, zs, zr, k1s, k1r, k2s, k2r, k3s, k3r,
):
    a, b = lax.axis_index("gx"), lax.axis_index("gy")
    h, q = b // 16, lax.rem(b, 16)
    g = 2 * a + h
    partner = (3 - b // 8) * 8 + lax.rem(b, 8)

    load_x = pltpu.make_async_copy(x_hbm, xin, dma_sem.at[0])
    load_ct = pltpu.make_async_copy(ct_hbm, ctin, dma_sem.at[1])
    load_spec = pltpu.make_async_copy(
        spec_hbm.at[:, :, pl.ds(pl.multiple_of(g * 256, 256), 256)], spec, dma_sem.at[2]
    )
    load_x.start()
    small = [
        pltpu.make_async_copy(src, dst, dma_sem.at[5 + n])
        for n, (src, dst) in enumerate(
            ((za_hbm, za_ref), (px_hbm, px_ref), (w_hbm, w_raw), (bias_hbm, bias_row), (zs_hbm, zs_ref), (py_hbm, py_ref))
        )
    ]
    for load in small:
        load.start()
    load_ct.start()
    load_spec.start()

    def group_x(k):
        t = lax.rem(g + k, 16)
        return t, (t // 2, jnp.where(lax.rem(t, 2) == h, b, partner))

    def group_y(k):
        t = lax.rem(q + k, 16)
        return t, (a, t + 16 * h)

    def there(da, db):
        ok = None
        if da == 1:
            ok = a < 7
        if da == -1:
            ok = a > 0
        if db == 1:
            ok = (b < 31) if ok is None else ok & (b < 31)
        if db == -1:
            ok = (b > 0) if ok is None else ok & (b > 0)
        return ok

    barrier = pltpu.get_barrier_semaphore()

    def greet(k, carry):
        pl.semaphore_signal(barrier, inc=1, device_id=group_x(k)[1], device_id_type=MESH)
        pl.semaphore_signal(barrier, inc=1, device_id=group_y(k)[1], device_id_type=MESH)
        return carry

    lax.fori_loop(1, 16, greet, 0)
    awaited = 30
    for da, db in NEIGHBOURS:
        if db == 0:
            continue

        @pl.when(there(da, db))
        def _():
            pl.semaphore_signal(barrier, inc=1, device_id=(a + da, b + db), device_id_type=MESH)

        awaited = awaited + jnp.where(there(da, db), 1, 0)

    def x_copy(t, peer, src, buf, ssem, rsem):
        return pltpu.make_async_remote_copy(
            src_ref=src, dst_ref=buf.at[g], send_sem=ssem, recv_sem=rsem,
            device_id=peer, device_id_type=MESH,
        )

    def y_copy(t, peer, src, buf, ssem, rsem):
        return pltpu.make_async_remote_copy(
            src_ref=src, dst_ref=buf.at[q], send_sem=ssem, recv_sem=rsem,
            device_id=peer, device_id_type=MESH,
        )

    def all_of(buf, count, ssem, rsem):
        return pltpu.make_async_remote_copy(
            src_ref=buf.at[pl.ds(0, count)], dst_ref=buf.at[pl.ds(0, count)], send_sem=ssem, recv_sem=rsem,
            device_id=group_y(1)[1], device_id_type=MESH,
        )

    def each(members, action):
        def step(k, carry):
            t, peer = members(k)
            action(t, peer)
            return carry

        lax.fori_loop(1, 16, step, 0)

    def halo_copy(index, field, n, da, db):
        sx_ = pl.ds(8, 1) if da == 1 else pl.ds(1, 1) if da == -1 else pl.ds(1, 8)
        dx_ = pl.ds(0, 1) if da == 1 else pl.ds(9, 1) if da == -1 else pl.ds(1, 8)
        sl = pl.ds(512, 128) if db == 1 else pl.ds(128, 128) if db == -1 else pl.ds(128, 512)
        dl = pl.ds(0, 128) if db == 1 else pl.ds(640, 128) if db == -1 else pl.ds(128, 512)
        return pltpu.make_async_remote_copy(
            src_ref=field.at[sx_, pl.ds(32, 32), sl], dst_ref=field.at[dx_, pl.ds(32, 32), dl],
            send_sem=halo_s.at[n, index], recv_sem=halo_r.at[n, index],
            device_id=(a + da, b + db), device_id_type=MESH,
        )

    def halo_start(field, n):
        for index, (da, db) in enumerate(NEIGHBOURS):

            @pl.when(there(da, db))
            def _():
                halo_copy(index, field, n, da, db).start()

    def halo_wait_recv(field, n):
        for index, (da, db) in enumerate(NEIGHBOURS):

            @pl.when(there(-da, -db))
            def _():
                halo_copy(index, field, n, da, db).wait_recv()

    def halo_wait_send(field, n):
        for index, (da, db) in enumerate(NEIGHBOURS):

            @pl.when(there(da, db))
            def _():
                halo_copy(index, field, n, da, db).wait_send()

    def zero_rim(field):
        @pl.when(a == 0)
        def _():
            field[0, 32:64, :] = jnp.zeros((C, WIDE), bf16)

        @pl.when(a == 7)
        def _():
            field[9, 32:64, :] = jnp.zeros((C, WIDE), bf16)

        @pl.when(b == 0)
        def _():
            for i in range(10):
                field[i, 32:64, 0:128] = jnp.zeros((C, NZ), bf16)

        @pl.when(b == 31)
        def _():
            for i in range(10):
                field[i, 32:64, 640:768] = jnp.zeros((C, NZ), bf16)

    def z_analyse(i, tiles):
        rows = jnp.concatenate(tiles, axis=0)
        both = dot(za_ref[...], rows, DOT_NT)
        tbuf[i] = both[:16] + both[16:]

    def x_partials(buf):
        rows = [tbuf[i] for i in range(BX)]

        def step(p, carry):
            total = px_ref[(a * 8) * 16 + p] * rows[0]
            for i in range(1, BX):
                total = total + px_ref[(a * 8 + i) * 16 + p] * rows[i]
            buf[p] = total
            return carry

        lax.fori_loop(0, 16, step, 0, unroll=4)

    def y_blocks(recv, send):
        for half in range(2):
            total = recv[half]
            for i in range(1, 8):
                total = total + recv[2 * i + half]
            send[half] = total.astype(bf16)

    def block_of(member, half):
        return 16 * half + jnp.where(h == half, member, lax.rem(member + 8, 16))

    def y_analyse(recv):
        def step(block, carry):
            result = list(carry)
            for half in range(2):
                value = recv[block, half].astype(f32)
                place = block_of(block, half)
                for m in range(MODES):
                    result[m] = result[m] + value * py_ref[place, pl.ds(m, 1), :]
            return tuple(result)

        start = tuple(jnp.zeros((16, 128), f32) for _ in range(MODES))
        return lax.fori_loop(0, 16, step, start, unroll=2)

    def to_columns(parts, scale):
        wide = jnp.transpose(jnp.concatenate(parts, axis=0))
        return (wide[0:32] + wide[32:64] + wide[64:96] + wide[96:128]) * scale

    def y_synthesise(modes, scale, send):
        tall = jnp.transpose(jnp.concatenate([modes * scale] * 4, axis=0))
        for half in range(2):
            place = block_of(q, half)
            total = py_ref[place, pl.ds(0, 1), :] * tall[0:16]
            for m in range(1, MODES):
                total = total + py_ref[place, pl.ds(m, 1), :] * tall[16 * m : 16 * m + 16]
            send[half] = total

    def x_z_synthesise(i, recv):
        total = px_ref[(a * 8 + i) * 16] * recv[0]
        for p in range(1, MODES):
            total = total + px_ref[(a * 8 + i) * 16 + p] * recv[p]
        high = total.astype(bf16)
        low = (total - high.astype(f32)).astype(bf16)
        return dot(jnp.concatenate([high, low, high], axis=0), zs_ref[...], DOT_TN)

    lane = lax.broadcasted_iota(jnp.int32, (C, NZ), 1)

    def shift_rows(field, ones):
        def step(i, carry):
            for y in range(BY + 2):
                cells = slice(y * NZ, (y + 1) * NZ)
                value = field[i, 32:64, cells].astype(f32)
                before = jnp.where(lane == 0, 0.0, pltpu.roll(value, 1, 1))
                after = jnp.where(lane == NZ - 1, 0.0, pltpu.roll(value, NZ - 1, 1))
                field[i, 0:32, cells] = before.astype(bf16)
                field[i, 64:96, cells] = after.astype(bf16)
            return carry

        lax.fori_loop(0, 10, step, 0, unroll=2)

    def fill_ones(field):
        def step(i, carry):
            field[i, 96:128, :] = jnp.ones((32, WIDE), bf16)
            return carry

        lax.fori_loop(0, 10, step, 0)

    def convolve(field, weights):
        def step(i, carry):
            total = None
            for d in range(3):
                for e in range(3):
                    tap = (d * 3 + e) * 128
                    part = dot(
                        weights[:, tap : tap + 128], field[i + d, :, e * NZ : e * NZ + LANES], DOT_NN
                    )
                    total = part if total is None else total + part
            acc[i] = total
            return carry

        lax.fori_loop(0, BX, step, 0, unroll=2)

    def unflatten(source, write):
        def step(c, carry):
            flat[pl.ds(pl.multiple_of(c * 32, 32), 32), :] = source[c].astype(f32)
            return carry

        lax.fori_loop(0, C, step, 0, unroll=8)

        def step2(i, carry):
            tiles = [flat[pl.ds(i * BY + y, C, stride=32), :] for y in range(BY)]
            write(i, tiles)
            return carry

        lax.fori_loop(0, BX, step2, 0, unroll=4)

    def flatten(source, target):
        def step(c, carry):
            target[c] = source[pl.ds(pl.multiple_of(c * 32, 32), 32), :].astype(bf16)
            return carry

        lax.fori_loop(0, C, step, 0, unroll=8)

    def prepare_weights():
        row = lax.broadcasted_iota(jnp.int32, (C, 128), 0)
        column = lax.broadcasted_iota(jnp.int32, (C, 128), 1)
        place = [jnp.where(column == row + 32 * f, 1.0, 0.0).astype(bf16) for f in range(3)]
        for tap in range(9):
            total, back_total = None, None
            for f in range(3):
                part = dot(w_raw[tap * 3 + f], place[f], DOT_NN)
                total = part if total is None else total + part
                part = dot(w_raw[(8 - tap) * 3 + 2 - f], place[f], DOT_TN)
                back_total = part if back_total is None else back_total + part
            wf_ref[:, tap * 128 : tap * 128 + 128] = total.astype(bf16)
            wb_ref[:, tap * 128 : tap * 128 + 128] = back_total.astype(bf16)
        spread = jnp.where(column[:, :C] == row[:, :C], jnp.broadcast_to(bias_row[...], (C, C)), 0.0)
        bias_ref[...] = jnp.broadcast_to(jnp.sum(spread, axis=1, keepdims=True), (C, 128))

    load_x.wait()
    small[0].wait()
    small[1].wait()

    def write_x(i, tiles):
        tiles = [t.astype(bf16) for t in tiles]
        for y in range(BY):
            stk[i + 1, 32:64, (y + 1) * NZ : (y + 2) * NZ] = tiles[y]
        z_analyse(i, tiles)

    unflatten(xin, write_x)
    x_partials(sx)
    pl.semaphore_wait(barrier, awaited)
    each(group_x, lambda t, peer: x_copy(t, peer, sx.at[t], rx, xs.at[0], xr.at[0]).start())
    rx[g] = sx[g]
    halo_start(stk, 0)

    zero_rim(stk)
    fill_ones(stk)
    for load in small[2:]:
        load.wait()
    prepare_weights()
    load_ct.wait()

    def write_ct(i, tiles):
        for y in range(BY):
            ct[i, :, y * NZ : (y + 1) * NZ] = tiles[y]

    unflatten(ctin, write_ct)
    for i in (0, 1, 10, 11):
        dx[i] = jnp.zeros((C, LANES), bf16)

    all_of(rx, 15, xs.at[0], xr.at[0]).wait_recv()
    y_blocks(rx, sy)
    each(group_y, lambda t, peer: y_copy(t, peer, sy, ry, ys.at[0], yr.at[0]).start())
    ry[q] = sy[...]

    halo_wait_recv(stk, 0)
    shift_rows(stk, True)
    convolve(stk, wf_ref)
    load_spec.wait()

    all_of(ry, 15, ys.at[0], yr.at[0]).wait_recv()
    parts = y_analyse(ry)
    for m in range(MODES):
        ct_modes[0, m] = parts[m]
    coefs[...] = to_columns(parts, GRID_SCALE)

    def mix(o, carry):
        mixed[pl.ds(o, 1), :] = jnp.sum(spec[o].astype(f32) * coefs[...], axis=0, keepdims=True)
        return carry

    lax.fori_loop(0, C, mix, 0, unroll=4)
    y_synthesise(mixed[...], MODE_SCALE, sz)
    each(group_x, lambda t, peer: x_copy(t, peer, sz.at[lax.rem(t, 2)], rz, zs.at[0], zr.at[0]).start())
    rz[g] = sz[h]
    all_of(rz, 15, zs.at[0], zr.at[0]).wait_recv()

    root = math.sqrt(2.0 / math.pi)

    def point(i, carry):
        modes = x_z_synthesise(i, rz)
        tiles = []
        for y in range(BY):
            cells = slice(y * NZ, (y + 1) * NZ)
            v = acc[i, :, cells] + modes[y * C : (y + 1) * C] + bias_ref[...]
            square = v * v
            t = jnp.tanh(root * (v + 0.044715 * (square * v)))
            half = 0.5 * (1.0 + t)
            slope = half + 0.5 * v * (1.0 - t * t) * (root * (1.0 + 3 * 0.044715 * square))
            oflat[pl.ds(i * BY + y, C, stride=32), :] = v * half
            delta = (ct[i, :, cells] * slope).astype(bf16)
            dstk[i + 1, 32:64, (y + 1) * NZ : (y + 2) * NZ] = delta
            dx[i + 2, :, cells] = delta
            tiles.append(delta)
        z_analyse(i, tiles)
        return carry

    lax.fori_loop(0, BX, point, 0, unroll=4)

    x_partials(sxb)
    each(group_x, lambda t, peer: x_copy(t, peer, sxb.at[t], rxb, xs.at[1], xr.at[1]).start())
    rxb[g] = sxb[g]
    halo_start(dstk, 1)

    zero_rim(dstk)
    fill_ones(dstk)
    flatten(oflat, obf)
    store_out = pltpu.make_async_copy(obf, out_hbm, dma_sem.at[3])
    store_out.start()

    kgp[...] = jnp.zeros((9, C, 128), f32)

    def kernel_step(i, carry):
        rows = jnp.concatenate([dx[i + 2], dx[i + 1], dx[i]], axis=0)
        for e in range(3):
            part = dot(rows, stk[i, :, e * NZ : e * NZ + LANES], DOT_NT)
            for d in range(3):
                kgp[e * 3 + d] += part[d * C : (d + 1) * C]
        return carry

    lax.fori_loop(0, 10, kernel_step, 0)

    for n in range(7):
        block = kgp[n]
        if n < 6:
            block = jnp.where(lane >= 96, pltpu.roll(kgp[7 + n // 3], 96 - 32 * (n % 3), 1), block)
        ks1[2 * n] = block[0:16].astype(bf16)
        ks1[2 * n + 1] = block[16:32].astype(bf16)
    def k1_start(t, peer):
        @pl.when(t < KG_SHARES)
        def _():
            x_copy(t, peer, ks1.at[t], kr1, k1s, k1r).start()

    each(group_x, k1_start)

    all_of(rxb, 15, xs.at[1], xr.at[1]).wait_recv()
    y_blocks(rxb, syb)
    each(group_y, lambda t, peer: y_copy(t, peer, syb, ryb, ys.at[1], yr.at[1]).start())
    ryb[q] = syb[...]

    halo_wait_recv(dstk, 1)
    shift_rows(dstk, False)
    convolve(dstk, wb_ref)

    @pl.when(g < KG_SHARES)
    def _():
        all_of(kr1, 15, k1s, k1r).wait_recv()
        kr1[g] = ks1[g]
        total = kr1[0].astype(f32)
        for i in range(1, 16):
            total = total + kr1[i].astype(f32)
        ks2[...] = total.astype(bf16)
        kr2[q] = total.astype(bf16)
        each(group_y, lambda t, peer: y_copy(t, peer, ks2, kr2, k2s, k2r).start())

    all_of(ryb, 15, ys.at[1], yr.at[1]).wait_recv()
    parts = y_analyse(ryb)
    for m in range(MODES):
        ct_modes[1, m] = parts[m]
    mixed[...] = to_columns(parts, MODE_SCALE)

    def mix_back(o, carry):
        return carry + spec[o].astype(f32) * mixed[pl.ds(o, 1), :]

    back = lax.fori_loop(0, C, mix_back, jnp.zeros((C, 256), f32), unroll=4)
    y_synthesise(back, GRID_SCALE, szb)
    each(group_x, lambda t, peer: x_copy(t, peer, szb.at[lax.rem(t, 2)], rzb, zs.at[1], zr.at[1]).start())
    rzb[g] = szb[h]

    @pl.when(g < KG_SHARES)
    def _():
        all_of(kr2, 15, k2s, k2r).wait_recv()
        total = kr2[0].astype(f32)
        for i in range(1, 16):
            total = total + kr2[i].astype(f32)
        total = total * GRID_SCALE
        ks3[...] = total
        kr3[g] = total
        each(group_x, lambda t, peer: x_copy(t, peer, ks3, kr3, k3s, k3r).start())

    coef_rows = ct_modes[0, q]
    coef_rows = coef_rows + pltpu.roll(coef_rows, 64, 1)
    coef_rows = (coef_rows + pltpu.roll(coef_rows, 32, 1)) * GRID_SCALE
    wide = jnp.transpose(ct_modes[1, q])
    back_columns = jnp.transpose(wide[0:32] + wide[32:64] + wide[64:96] + wide[96:128]) * MODE_SCALE
    for o in range(C):
        sg_ref[o] = (coef_rows * back_columns[:, o : o + 1])[:, 0:32]

    all_of(rzb, 15, zs.at[1], zr.at[1]).wait_recv()

    store_out.wait()

    def last(i, carry):
        modes = x_z_synthesise(i, rzb)
        for y in range(BY):
            cells = slice(y * NZ, (y + 1) * NZ)
            oflat[pl.ds(i * BY + y, C, stride=32), :] = acc[i, :, cells] + modes[y * C : (y + 1) * C]
        return carry

    lax.fori_loop(0, BX, last, 0, unroll=4)
    flatten(oflat, ibf)
    store_ig = pltpu.make_async_copy(ibf, ig_hbm, dma_sem.at[4])
    store_ig.start()

    def in_shares(has, has_not):
        pl.when(g < KG_SHARES)(has)
        pl.when(g >= KG_SHARES)(has_not)

    in_shares(
        lambda: all_of(kr3, KG_SHARES - 1, k3s, k3r).wait_recv(),
        lambda: all_of(kr3, KG_SHARES, k3s, k3r).wait_recv(),
    )
    blocks = [jnp.concatenate([kr3[2 * n], kr3[2 * n + 1]], axis=0) for n in range(7)]
    for d in range(3):
        for e in range(3):
            for f in range(3):
                n, offset = e * 3 + d, 32 * f
                if n >= 7:
                    n, offset = (n - 7) * 3 + f, 96
                moved = blocks[n] if offset == 0 else pltpu.roll(blocks[n], 128 - offset, 1)
                kg_ref[(d * 3 + e) * 3 + f] = moved[:, 0:32]
    bg_ref[...] = jnp.transpose(blocks[6])[96:97, :]

    for n in range(2):
        all_of((rx, rxb)[n], 15, xs.at[n], xr.at[n]).wait_send()
        all_of((rz, rzb)[n], 15, zs.at[n], zr.at[n]).wait_send()
        all_of((ry, ryb)[n], 15, ys.at[n], yr.at[n]).wait_send()
    halo_wait_send(stk, 0)
    halo_wait_send(dstk, 1)
    in_shares(
        lambda: all_of(kr1, KG_SHARES - 1, k1s, k1r).wait_send(),
        lambda: all_of(kr1, KG_SHARES, k1s, k1r).wait_send(),
    )

    @pl.when(g < KG_SHARES)
    def _():
        all_of(kr2, 15, k2s, k2r).wait_send()
        all_of(kr3, 15, k3s, k3r).wait_send()

    store_ig.wait()


def hand_over(*refs):
    sources, targets, held, load_sem, store_sem = refs[:5], refs[5:10], refs[10:15], refs[15], refs[16]
    loads = [pltpu.make_async_copy(sources[n], held[n], load_sem.at[n]) for n in range(5)]
    stores = [pltpu.make_async_copy(held[n], targets[n], store_sem.at[n]) for n in range(5)]
    for load in loads:
        load.start()
    for load, store in zip(loads, stores):
        load.wait()
        store.start()
    for store in stores:
        store.wait()


def layer(inputs, cotangent, weights, channel_bias, spectral):
    z_analysis, z_synthesis, y_table, x_table = tables()
    x = inputs.reshape(C, BX * BY, NZ)
    ct = cotangent.reshape(C, BX * BY, NZ)
    any_space = pl.BlockSpec(memory_space=pl.ANY)
    vmem = pl.BlockSpec(memory_space=pltpu.VMEM)
    dma = pltpu.SemaphoreType.DMA
    V = pltpu.VMEM
    mode_bufs = [
        V((16, 16, 128), f32), V((16, 16, 128), f32),
        V((2, 16, 128), bf16), V((16, 2, 16, 128), bf16),
        V((2, 16, 128), f32), V((16, 16, 128), f32),
    ]
    results = pl.pallas_call(
        kernel,
        out_shape=(
            jax.ShapeDtypeStruct((C, BX * BY, NZ), bf16),
            jax.ShapeDtypeStruct((C, BX * BY, NZ), bf16),
            jax.ShapeDtypeStruct((C, 16, C), f32),
            jax.ShapeDtypeStruct((27, C, C), f32),
            jax.ShapeDtypeStruct((1, C), f32),
        ),
        in_specs=[pl.BlockSpec(memory_space=pltpu.HBM)] * 9,
        out_specs=(any_space, any_space, vmem, vmem, vmem),
        scratch_shapes=[
            V((27, C, C), bf16), V((1, C), f32), V((32, 128), bf16), V((48, 128), bf16),
            V((32, MODES, 128), f32), pltpu.SMEM((NX * MODES,), f32),
            V((C, 1152), bf16), V((C, 1152), bf16), V((C, 128), f32),
            V((C, 32, NZ), bf16), V((C, 32, NZ), bf16), V((C, C, 256), bf16),
            V((C * 32, NZ), f32), V((BX, C, LANES), f32), V((BX, C, LANES), f32),
            V((10, 128, WIDE), bf16), V((10, 128, WIDE), bf16), V((12, C, LANES), bf16),
            V((BX, 16, 128), f32),
            *mode_bufs,
            V((2, MODES, 16, 128), f32), V((C, 256), f32), V((C, 256), f32),

            *mode_bufs,
            V((9, C, 128), f32), V((KG_SHARES, KG_ROWS, 128), bf16), V((16, KG_ROWS, 128), bf16),
            V((KG_ROWS, 128), bf16), V((16, KG_ROWS, 128), bf16),
            V((KG_ROWS, 128), f32), V((16, KG_ROWS, 128), f32),
            V((C * 32, NZ), f32), V((C, 32, NZ), bf16), V((C, 32, NZ), bf16),
            dma((11,)), dma((2, 8)), dma((2, 8)),
            *[dma((2,))] * 6,
            *[dma] * 6,
        ],
        compiler_params=pltpu.CompilerParams(
            collective_id=0, has_side_effects=True, vmem_limit_bytes=60 * 2**20
        ),
        cost_estimate=pl.CostEstimate(flops=700_000_000, bytes_accessed=4_000_000, transcendentals=131072),
    )(
        x, ct, spectral, weights.reshape(27, C, C),
        channel_bias.reshape(1, C),
        z_analysis, z_synthesis, y_table, x_table,
    )
    outputs, input_grad, spectral_grad, kernel_grad, bias_grad = pl.pallas_call(
        hand_over,
        out_shape=tuple(jax.ShapeDtypeStruct(r.shape, r.dtype) for r in results),
        in_specs=[any_space] * 5,
        out_specs=(any_space,) * 5,
        scratch_shapes=[*[V(r.shape, r.dtype) for r in results], dma((5,)), dma((5,))],
        compiler_params=pltpu.CompilerParams(vmem_limit_bytes=60 * 2**20),
    )(*results)
    field = (C, BX, BY, NZ)
    return (
        outputs.reshape(field), input_grad.reshape(field), spectral_grad.transpose(0, 2, 1),
        kernel_grad.reshape(3, 3, 3, C, C), bias_grad.reshape(C),
    )


def solution(mesh):
    placed = (P(None, "gx", "gy", None), P(None, "gx", "gy", None), P(), P(), P())
    return jax.shard_map(
        layer,
        mesh=mesh,
        in_specs=placed,
        out_specs=(
            P(None, "gx", "gy", None),
            P(None, "gx", "gy", None),
            P(None, None, ("gx", "gy")),
            P(),
            P(),
        ),
        check_vma=False,
    )
```

```python
import functools
import math

import jax
import jax.numpy as jnp
import numpy as np
from jax import lax
from jax.experimental import pallas as pl
from jax.experimental.pallas import tpu as pltpu
from jax.sharding import PartitionSpec as P

MESH = pl.DeviceIdType.MESH
MODES = 16
C = 32
BX, BY, NZ = 8, 4, 128
NX, NY = 64, 128
LANES = BY * NZ
WIDE = (BY + 2) * NZ
NEIGHBOURS = [(i, j) for i in (-1, 0, 1) for j in (-1, 0, 1) if (i, j) != (0, 0)]
GRID_SCALE = 1.0 / math.sqrt(NX * NY * NZ)
MODE_SCALE = 1.0 / math.sqrt(MODES**3)
KG_ROWS = 16
KG_SHARES = 14
f32, bf16 = jnp.float32, jnp.bfloat16
DOT_NT = (((1,), (1,)), ((), ()))
DOT_TN = (((0,), (0,)), ((), ()))
DOT_NN = (((1,), (0,)), ((), ()))


def basis(cells):
    rows = np.arange(MODES)
    frequency = np.where(rows < MODES // 2, rows, rows - MODES // 2 + 1)
    phase = frequency[:, None] * np.arange(cells)[None, :] % cells
    angles = phase * (2.0 * math.pi / cells)
    return np.where((rows < MODES // 2)[:, None], np.cos(angles), np.sin(angles)).astype(np.float32)


def split(array):
    high = array.astype(jnp.bfloat16)
    low = (array - high.astype(np.float32)).astype(jnp.bfloat16)
    return high, low


def tables():
    phi_x, phi_y, phi_z = basis(NX), basis(NY), basis(NZ)
    high, low = split(phi_z)
    z_analysis = np.concatenate([high, low], 0)
    z_synthesis = np.concatenate([high, high, low], 0)
    lanes = np.repeat(phi_y.reshape(MODES, 32, BY), C, axis=2)
    y_table = lanes.transpose(1, 0, 2)
    x_table = phi_x.T.reshape(-1)
    return z_analysis, z_synthesis, np.ascontiguousarray(y_table), np.ascontiguousarray(x_table)


def dot(a, b, dims):
    return lax.dot_general(a, b, dims, preferred_element_type=f32)


def x_z_synthesise(cell, recv, px_ref, zs_ref):
    total = px_ref[cell * 16] * recv[0]
    for p in range(1, MODES):
        total = total + px_ref[cell * 16 + p] * recv[p]
    high = total.astype(bf16)
    low = (total - high.astype(f32)).astype(bf16)
    return dot(jnp.concatenate([high, low, high], axis=0), zs_ref[...], DOT_TN)


def kernel(
    x_hbm, ct_hbm, spec_hbm, w_hbm, bias_hbm, za_hbm, zs_hbm, py_hbm, px_hbm,
    out_hbm, acc_hbm, sg_hbm, rzb, kr3,
    w_raw, bias_row, za_ref, zs_ref, py_ref, px_ref, wf_ref, wb_ref, bias_ref,
    xin, ctin, spec, flat, ct, acc, stk, dstk, dx, tbuf,
    sx, rx, sy, ry, sz, rz, ct_modes, coefs, mixed,
    sxb, rxb, syb, ryb, szb,
    kgt, ks1, kr1, ks2, kr2, ks3, sg_ref,
    oflat, obf,
    dma_sem, halo_s, halo_r, xs, xr, ys, yr, zs, zr, k1s, k1r, k2s, k2r, k3s, k3r,
):
    a, b = lax.axis_index("gx"), lax.axis_index("gy")
    h, q = b // 16, lax.rem(b, 16)
    g = 2 * a + h
    partner = (3 - b // 8) * 8 + lax.rem(b, 8)

    def group_x(k):
        rank, other, core = k // 4, lax.rem(k // 2, 2), lax.rem(k, 2)
        steps = jnp.where(rank == 1, 3, jnp.where(rank == 0, 0, rank - 1))
        ta = 2 * lax.rem(a // 2 + steps, 4) + lax.rem(a + core, 2)
        th = lax.rem(h + other, 2)
        return 2 * ta + th, (ta, jnp.where(other == 0, b, partner))

    def group_y(k):
        rank, other = k // 2, lax.rem(k, 2)
        steps = jnp.where(lax.rem(rank, 2) == 1, (rank + 1) // 2, 8 - rank // 2)
        t = 8 * lax.rem(q // 8 + other, 2) + lax.rem(lax.rem(q, 8) + steps, 8)
        return t, (a, t + 16 * h)

    def each(members, action):
        def step(n, carry):
            t, peer = members(15 - n)
            action(t, peer)
            return carry

        lax.fori_loop(0, 15, step, 0, unroll=True)

    def there(da, db):
        ok = None
        if da == 1:
            ok = a < 7
        if da == -1:
            ok = a > 0
        if db == 1:
            ok = (b < 31) if ok is None else ok & (b < 31)
        if db == -1:
            ok = (b > 0) if ok is None else ok & (b > 0)
        return ok

    barrier = pltpu.get_barrier_semaphore()

    def greet(t, peer):
        pl.semaphore_signal(barrier, inc=1, device_id=peer, device_id_type=MESH)

    each(group_y, greet)
    each(group_x, greet)
    awaited = 30
    for da, db in NEIGHBOURS:
        if db == 0:
            continue

        @pl.when(there(da, db))
        def _():
            pl.semaphore_signal(barrier, inc=1, device_id=(a + da, b + db), device_id_type=MESH)

        awaited = awaited + jnp.where(there(da, db), 1, 0)

    load_x = pltpu.make_async_copy(x_hbm, xin, dma_sem.at[0])
    load_ct = pltpu.make_async_copy(ct_hbm, ctin, dma_sem.at[1])
    load_spec = pltpu.make_async_copy(
        spec_hbm.at[:, :, pl.ds(pl.multiple_of(g * 256, 256), 256)], spec, dma_sem.at[2]
    )
    load_x.start()
    small = [
        pltpu.make_async_copy(src, dst, dma_sem.at[5 + n])
        for n, (src, dst) in enumerate(
            ((za_hbm, za_ref), (px_hbm, px_ref), (w_hbm, w_raw), (bias_hbm, bias_row), (zs_hbm, zs_ref), (py_hbm, py_ref))
        )
    ]
    for load in small:
        load.start()
    load_ct.start()
    load_spec.start()

    def x_copy(t, peer, src, buf, ssem, rsem):
        return pltpu.make_async_remote_copy(
            src_ref=src, dst_ref=buf.at[g], send_sem=ssem, recv_sem=rsem,
            device_id=peer, device_id_type=MESH,
        )

    def y_copy(t, peer, src, buf, ssem, rsem):
        return pltpu.make_async_remote_copy(
            src_ref=src, dst_ref=buf.at[q], send_sem=ssem, recv_sem=rsem,
            device_id=peer, device_id_type=MESH,
        )

    def all_of(buf, count, ssem, rsem):
        return pltpu.make_async_remote_copy(
            src_ref=buf.at[pl.ds(0, count)], dst_ref=buf.at[pl.ds(0, count)], send_sem=ssem, recv_sem=rsem,
            device_id=group_y(1)[1], device_id_type=MESH,
        )

    def halo_copy(index, field, n, da, db):
        sx_ = pl.ds(8, 1) if da == 1 else pl.ds(1, 1) if da == -1 else pl.ds(1, 8)
        dx_ = pl.ds(0, 1) if da == 1 else pl.ds(9, 1) if da == -1 else pl.ds(1, 8)
        sl = pl.ds(512, 128) if db == 1 else pl.ds(128, 128) if db == -1 else pl.ds(128, 512)
        dl = pl.ds(0, 128) if db == 1 else pl.ds(640, 128) if db == -1 else pl.ds(128, 512)
        return pltpu.make_async_remote_copy(
            src_ref=field.at[sx_, pl.ds(32, 32), sl], dst_ref=field.at[dx_, pl.ds(32, 32), dl],
            send_sem=halo_s.at[n, index], recv_sem=halo_r.at[n, index],
            device_id=(a + da, b + db), device_id_type=MESH,
        )

    def halo_start(field, n):
        for index, (da, db) in enumerate(NEIGHBOURS):

            @pl.when(there(da, db))
            def _():
                halo_copy(index, field, n, da, db).start()

    def halo_wait_recv(field, n):
        for index, (da, db) in enumerate(NEIGHBOURS):

            @pl.when(there(-da, -db))
            def _():
                halo_copy(index, field, n, da, db).wait_recv()

    def halo_wait_send(field, n):
        for index, (da, db) in enumerate(NEIGHBOURS):

            @pl.when(there(da, db))
            def _():
                halo_copy(index, field, n, da, db).wait_send()

    def zero_rim(field):
        @pl.when(a == 0)
        def _():
            field[0, 32:64, :] = jnp.zeros((C, WIDE), bf16)

        @pl.when(a == 7)
        def _():
            field[9, 32:64, :] = jnp.zeros((C, WIDE), bf16)

        @pl.when(b == 0)
        def _():
            for i in range(10):
                field[i, 32:64, 0:128] = jnp.zeros((C, NZ), bf16)

        @pl.when(b == 31)
        def _():
            for i in range(10):
                field[i, 32:64, 640:768] = jnp.zeros((C, NZ), bf16)

    def z_analyse(i, tiles):
        rows = jnp.concatenate(tiles, axis=0)
        both = dot(za_ref[...], rows, DOT_NT)
        tbuf[i] = both[:16] + both[16:]

    def x_partials(buf):
        rows = [tbuf[i] for i in range(BX)]

        def step(p, carry):
            total = px_ref[(a * 8) * 16 + p] * rows[0]
            for i in range(1, BX):
                total = total + px_ref[(a * 8 + i) * 16 + p] * rows[i]
            buf[p] = total
            return carry

        lax.fori_loop(0, 16, step, 0, unroll=4)

    def y_blocks(recv, send):
        for half in range(2):
            total = recv[half]
            for i in range(1, 8):
                total = total + recv[2 * i + half]
            send[half] = total.astype(bf16)

    def block_of(member, half):
        return 16 * half + jnp.where(h == half, member, lax.rem(member + 8, 16))

    def y_analyse(recv):
        def step(block, carry):
            result = list(carry)
            for half in range(2):
                value = recv[block, half].astype(f32)
                place = block_of(block, half)
                for m in range(MODES):
                    result[m] = result[m] + value * py_ref[place, pl.ds(m, 1), :]
            return tuple(result)

        start = tuple(jnp.zeros((16, 128), f32) for _ in range(MODES))
        return lax.fori_loop(0, 16, step, start, unroll=2)

    def to_columns(parts, scale):
        wide = jnp.transpose(jnp.concatenate(parts, axis=0))
        return (wide[0:32] + wide[32:64] + wide[64:96] + wide[96:128]) * scale

    def y_synthesise(modes, scale, send):
        tall = jnp.transpose(jnp.concatenate([modes * scale] * 4, axis=0))
        for half in range(2):
            place = block_of(q, half)
            total = py_ref[place, pl.ds(0, 1), :] * tall[0:16]
            for m in range(1, MODES):
                total = total + py_ref[place, pl.ds(m, 1), :] * tall[16 * m : 16 * m + 16]
            send[half] = total

    lane = lax.broadcasted_iota(jnp.int32, (C, NZ), 1)

    def shift_rows(field, ones):
        def step(i, carry):
            for y in range(BY + 2):
                cells = slice(y * NZ, (y + 1) * NZ)
                value = field[i, 32:64, cells].astype(f32)
                before = jnp.where(lane == 0, 0.0, pltpu.roll(value, 1, 1))
                after = jnp.where(lane == NZ - 1, 0.0, pltpu.roll(value, NZ - 1, 1))
                field[i, 0:32, cells] = before.astype(bf16)
                field[i, 64:96, cells] = after.astype(bf16)
            return carry

        lax.fori_loop(0, 10, step, 0, unroll=2)

    def fill_ones(field):
        def step(i, carry):
            field[i, 96:128, :] = jnp.ones((32, WIDE), bf16)
            return carry

        lax.fori_loop(0, 10, step, 0)

    def convolve(field, weights):
        def step(i, carry):
            total = None
            for d in range(3):
                for e in range(3):
                    tap = (d * 3 + e) * 128
                    part = dot(
                        weights[:, tap : tap + 128], field[i + d, :, e * NZ : e * NZ + LANES], DOT_NN
                    )
                    total = part if total is None else total + part
            acc[i] = total
            return carry

        lax.fori_loop(0, BX, step, 0, unroll=2)

    def unflatten(source, write):
        def step(c, carry):
            flat[pl.ds(pl.multiple_of(c * 32, 32), 32), :] = source[c].astype(f32)
            return carry

        lax.fori_loop(0, C, step, 0, unroll=8)

        def step2(i, carry):
            tiles = [flat[pl.ds(i * BY + y, C, stride=32), :] for y in range(BY)]
            write(i, tiles)
            return carry

        lax.fori_loop(0, BX, step2, 0, unroll=4)

    def flatten(source, target):
        def step(c, carry):
            target[c] = source[pl.ds(pl.multiple_of(c * 32, 32), 32), :].astype(bf16)
            return carry

        lax.fori_loop(0, C, step, 0, unroll=8)

    def prepare_weights():
        row = lax.broadcasted_iota(jnp.int32, (C, 128), 0)
        column = lax.broadcasted_iota(jnp.int32, (C, 128), 1)
        place = [jnp.where(column == row + 32 * f, 1.0, 0.0).astype(bf16) for f in range(3)]
        for tap in range(9):
            total, back_total = None, None
            for f in range(3):
                part = dot(w_raw[tap * 3 + f], place[f], DOT_NN)
                total = part if total is None else total + part
                part = dot(w_raw[(8 - tap) * 3 + 2 - f], place[f], DOT_TN)
                back_total = part if back_total is None else back_total + part
            wf_ref[:, tap * 128 : tap * 128 + 128] = total.astype(bf16)
            wb_ref[:, tap * 128 : tap * 128 + 128] = back_total.astype(bf16)
        spread = jnp.where(column[:, :C] == row[:, :C], jnp.broadcast_to(bias_row[...], (C, C)), 0.0)
        bias_ref[...] = jnp.broadcast_to(jnp.sum(spread, axis=1, keepdims=True), (C, 128))

    load_x.wait()
    small[0].wait()
    small[1].wait()

    def write_x(i, tiles):
        tiles = [t.astype(bf16) for t in tiles]
        for y in range(BY):
            stk[i + 1, 32:64, (y + 1) * NZ : (y + 2) * NZ] = tiles[y]
        z_analyse(i, tiles)

    unflatten(xin, write_x)
    x_partials(sx)
    pl.semaphore_wait(barrier, awaited)
    each(group_x, lambda t, peer: x_copy(t, peer, sx.at[t], rx, xs.at[0], xr.at[0]).start())
    rx[g] = sx[g]
    halo_start(stk, 0)

    zero_rim(stk)
    fill_ones(stk)
    for load in small[2:]:
        load.wait()
    prepare_weights()
    load_ct.wait()

    def write_ct(i, tiles):
        for y in range(BY):
            ct[i, :, y * NZ : (y + 1) * NZ] = tiles[y]

    unflatten(ctin, write_ct)
    for i in (0, 1, 10, 11):
        dx[i] = jnp.zeros((C, LANES), bf16)

    all_of(rx, 15, xs.at[0], xr.at[0]).wait_recv()
    y_blocks(rx, sy)
    each(group_y, lambda t, peer: y_copy(t, peer, sy, ry, ys.at[0], yr.at[0]).start())
    ry[q] = sy[...]

    halo_wait_recv(stk, 0)
    shift_rows(stk, True)
    convolve(stk, wf_ref)
    load_spec.wait()

    all_of(ry, 15, ys.at[0], yr.at[0]).wait_recv()
    parts = y_analyse(ry)
    for m in range(MODES):
        ct_modes[0, m] = parts[m]
    coefs[...] = to_columns(parts, GRID_SCALE)

    def mix(o, carry):
        mixed[pl.ds(o, 1), :] = jnp.sum(spec[o].astype(f32) * coefs[...], axis=0, keepdims=True)
        return carry

    lax.fori_loop(0, C, mix, 0, unroll=4)
    y_synthesise(mixed[...], MODE_SCALE, sz)
    each(group_x, lambda t, peer: x_copy(t, peer, sz.at[lax.rem(t, 2)], rz, zs.at[0], zr.at[0]).start())
    rz[g] = sz[h]
    all_of(rz, 15, zs.at[0], zr.at[0]).wait_recv()

    root = math.sqrt(2.0 / math.pi)

    def point(i, carry):
        modes = x_z_synthesise(a * 8 + i, rz, px_ref, zs_ref)
        tiles = []
        for y in range(BY):
            cells = slice(y * NZ, (y + 1) * NZ)
            v = acc[i, :, cells] + modes[y * C : (y + 1) * C] + bias_ref[...]
            square = v * v
            t = jnp.tanh(root * (v + 0.044715 * (square * v)))
            half = 0.5 * (1.0 + t)
            slope = half + 0.5 * v * (1.0 - t * t) * (root * (1.0 + 3 * 0.044715 * square))
            oflat[pl.ds(i * BY + y, C, stride=32), :] = v * half
            delta = (ct[i, :, cells] * slope).astype(bf16)
            dstk[i + 1, 32:64, (y + 1) * NZ : (y + 2) * NZ] = delta
            dx[i + 2, :, cells] = delta
            tiles.append(delta)
        z_analyse(i, tiles)
        return carry

    lax.fori_loop(0, BX, point, 0, unroll=True)

    x_partials(sxb)
    each(group_x, lambda t, peer: x_copy(t, peer, sxb.at[t], rxb, xs.at[1], xr.at[1]).start())
    rxb[g] = sxb[g]
    halo_start(dstk, 1)

    zero_rim(dstk)
    fill_ones(dstk)
    flatten(oflat, obf)
    store_out = pltpu.make_async_copy(obf, out_hbm, dma_sem.at[3])
    store_out.start()

    kgt[...] = jnp.zeros((3 * 128, 128), f32)

    def kernel_step(i, carry):
        shifted = [dx[i + 2], dx[i + 1], dx[i], jnp.zeros((C, LANES), bf16)]
        windows = [stk[i, :, e * NZ : e * NZ + LANES] for e in range(3)]
        kgt[...] += dot(jnp.concatenate(windows, axis=0), jnp.concatenate(shifted, axis=0), DOT_NT)
        return carry

    lax.fori_loop(0, 10, kernel_step, 0, unroll=2)
    columns = [jnp.transpose(kgt[128 * e : 128 * e + 128]) for e in range(3)]
    kgp = [columns[e][32 * d : 32 * d + 32] for e in range(3) for d in range(3)]

    for n in range(7):
        block = kgp[n]
        if n < 6:
            block = jnp.where(lane >= 96, pltpu.roll(kgp[7 + n // 3], 96 - 32 * (n % 3), 1), block)
        ks1[2 * n] = block[0:16].astype(bf16)
        ks1[2 * n + 1] = block[16:32].astype(bf16)
    def k1_start(t, peer):
        @pl.when(t < KG_SHARES)
        def _():
            x_copy(t, peer, ks1.at[t], kr1, k1s, k1r).start()

    each(group_x, k1_start)

    all_of(rxb, 15, xs.at[1], xr.at[1]).wait_recv()
    y_blocks(rxb, syb)
    each(group_y, lambda t, peer: y_copy(t, peer, syb, ryb, ys.at[1], yr.at[1]).start())
    ryb[q] = syb[...]

    halo_wait_recv(dstk, 1)
    shift_rows(dstk, False)
    convolve(dstk, wb_ref)
    store_acc = pltpu.make_async_copy(acc, acc_hbm, dma_sem.at[4])
    store_acc.start()

    @pl.when(g < KG_SHARES)
    def _():
        all_of(kr1, 15, k1s, k1r).wait_recv()
        kr1[g] = ks1[g]
        total = kr1[0].astype(f32)
        for i in range(1, 16):
            total = total + kr1[i].astype(f32)
        ks2[...] = total.astype(bf16)
        kr2[q] = total.astype(bf16)
        each(group_y, lambda t, peer: y_copy(t, peer, ks2, kr2, k2s, k2r).start())

    all_of(ryb, 15, ys.at[1], yr.at[1]).wait_recv()
    parts = y_analyse(ryb)
    for m in range(MODES):
        ct_modes[1, m] = parts[m]
    mixed[...] = to_columns(parts, MODE_SCALE)

    def mix_back(o, carry):
        return carry + spec[o].astype(f32) * mixed[pl.ds(o, 1), :]

    back = lax.fori_loop(0, C, mix_back, jnp.zeros((C, 256), f32), unroll=4)
    y_synthesise(back, GRID_SCALE, szb)
    each(group_x, lambda t, peer: x_copy(t, peer, szb.at[lax.rem(t, 2)], rzb, zs.at[1], zr.at[1]).start())
    keep_z = pltpu.make_async_copy(szb.at[h], rzb.at[g], dma_sem.at[11])
    keep_z.start()

    @pl.when(g < KG_SHARES)
    def _():
        all_of(kr2, 15, k2s, k2r).wait_recv()
        total = kr2[0].astype(f32)
        for i in range(1, 16):
            total = total + kr2[i].astype(f32)
        total = total * GRID_SCALE
        ks3[...] = total
        pltpu.make_async_copy(ks3, kr3.at[g], dma_sem.at[12]).start()
        each(group_x, lambda t, peer: x_copy(t, peer, ks3, kr3, k3s, k3r).start())

    coef_rows = ct_modes[0, q]
    coef_rows = coef_rows + pltpu.roll(coef_rows, 64, 1)
    coef_rows = (coef_rows + pltpu.roll(coef_rows, 32, 1)) * GRID_SCALE
    wide = jnp.transpose(ct_modes[1, q])
    back_columns = jnp.transpose(wide[0:32] + wide[32:64] + wide[64:96] + wide[96:128]) * MODE_SCALE
    for o in range(C):
        sg_ref[o] = (coef_rows * back_columns[:, o : o + 1])[:, 0:32]

    store_sg = pltpu.make_async_copy(sg_ref, sg_hbm, dma_sem.at[13])
    store_sg.start()

    for n in range(2):
        all_of((rx, rxb)[n], 15, xs.at[n], xr.at[n]).wait_send()
        all_of((rz, rzb)[n], 15, zs.at[n], zr.at[n]).wait_send()
        all_of((ry, ryb)[n], 15, ys.at[n], yr.at[n]).wait_send()
    halo_wait_send(stk, 0)
    halo_wait_send(dstk, 1)
    def in_shares(has, has_not):
        pl.when(g < KG_SHARES)(has)
        pl.when(g >= KG_SHARES)(has_not)

    in_shares(
        lambda: all_of(kr1, KG_SHARES - 1, k1s, k1r).wait_send(),
        lambda: all_of(kr1, KG_SHARES, k1s, k1r).wait_send(),
    )

    @pl.when(g < KG_SHARES)
    def _():
        all_of(kr2, 15, k2s, k2r).wait_send()
        all_of(rx, 15, k3s, k3r).wait_send()

    @pl.when(g < KG_SHARES)
    def _():
        pltpu.make_async_copy(ks3, kr3.at[g], dma_sem.at[12]).wait()

    store_out.wait()
    store_acc.wait()
    store_sg.wait()
    keep_z.wait()
    in_shares(
        lambda: all_of(kr3, KG_SHARES - 1, k3s, k3r).wait_recv(),
        lambda: all_of(kr3, KG_SHARES, k3s, k3r).wait_recv(),
    )
    all_of(rzb, 15, zs.at[1], zr.at[1]).wait_recv()


def finish(
    out_in, acc_in, sg_in, rz_in, kr_in, zs_in, px_in,
    out_hbm, ig_hbm, sg_hbm, kg_hbm, bg_ref,
    out_v, acc, sg_v, rz, kr, zs_ref, px_ref, flat, ig, kg, load_sem, store_sem,
):
    a = lax.axis_index("gx")
    pairs = ((rz_in, rz), (px_in, px_ref), (zs_in, zs_ref), (acc_in, acc), (kr_in, kr), (out_in, out_v), (sg_in, sg_v))
    loads = [pltpu.make_async_copy(src, dst, load_sem.at[n]) for n, (src, dst) in enumerate(pairs)]
    stores = [
        pltpu.make_async_copy(src, dst, store_sem.at[n])
        for n, (src, dst) in enumerate(((out_v, out_hbm), (sg_v, sg_hbm), (ig, ig_hbm), (kg, kg_hbm)))
    ]
    for load in loads:
        load.start()
    for load in loads[:4]:
        load.wait()

    def last(i, carry):
        modes = x_z_synthesise(a * 8 + i, rz, px_ref, zs_ref)
        for y in range(BY):
            cells = slice(y * NZ, (y + 1) * NZ)
            flat[pl.ds(i * BY + y, C, stride=32), :] = acc[i, :, cells] + modes[y * C : (y + 1) * C]
        return carry

    lax.fori_loop(0, BX, last, 0, unroll=True)

    def narrow(c, carry):
        ig[c] = flat[pl.ds(pl.multiple_of(c * 32, 32), 32), :].astype(bf16)
        return carry

    lax.fori_loop(0, C, narrow, 0, unroll=8)
    stores[2].start()
    loads[5].wait()
    stores[0].start()
    loads[6].wait()
    stores[1].start()
    loads[4].wait()
    blocks = [jnp.concatenate([kr[2 * n], kr[2 * n + 1]], axis=0) for n in range(7)]
    for d in range(3):
        for e in range(3):
            for f in range(3):
                n, offset = e * 3 + d, 32 * f
                if n >= 7:
                    n, offset = (n - 7) * 3 + f, 96
                moved = blocks[n] if offset == 0 else pltpu.roll(blocks[n], 128 - offset, 1)
                kg[(d * 3 + e) * 3 + f] = moved[:, 0:32]
    stores[3].start()
    bg_ref[...] = jnp.transpose(blocks[6])[96:97, :]
    for store in stores:
        store.wait()


def layer(inputs, cotangent, weights, channel_bias, spectral):
    z_analysis, z_synthesis, y_table, x_table = tables()
    x = inputs.reshape(C, BX * BY, NZ)
    ct = cotangent.reshape(C, BX * BY, NZ)
    any_space = pl.BlockSpec(memory_space=pl.ANY)
    vmem = pl.BlockSpec(memory_space=pltpu.VMEM)
    dma = pltpu.SemaphoreType.DMA
    V = pltpu.VMEM
    mode_bufs = [
        V((16, 16, 128), f32), V((16, 16, 128), f32),
        V((2, 16, 128), bf16), V((16, 2, 16, 128), bf16),
        V((2, 16, 128), f32), V((16, 16, 128), f32),
    ]
    results = pl.pallas_call(
        kernel,
        out_shape=(
            jax.ShapeDtypeStruct((C, BX * BY, NZ), bf16),
            jax.ShapeDtypeStruct((BX, C, LANES), f32),
            jax.ShapeDtypeStruct((C, 16, C), f32),
            jax.ShapeDtypeStruct((16, 16, 128), f32),
            jax.ShapeDtypeStruct((KG_SHARES, KG_ROWS, 128), f32),
        ),
        in_specs=[pl.BlockSpec(memory_space=pltpu.HBM)] * 9,
        out_specs=(any_space,) * 5,
        scratch_shapes=[
            V((27, C, C), bf16), V((1, C), f32), V((32, 128), bf16), V((48, 128), bf16),
            V((32, MODES, 128), f32), pltpu.SMEM((NX * MODES,), f32),
            V((C, 1152), bf16), V((C, 1152), bf16), V((C, 128), f32),
            V((C, 32, NZ), bf16), V((C, 32, NZ), bf16), V((C, C, 256), bf16),
            V((C * 32, NZ), f32), V((BX, C, LANES), f32), V((BX, C, LANES), f32),
            V((10, 128, WIDE), bf16), V((10, 128, WIDE), bf16), V((12, C, LANES), bf16),
            V((BX, 16, 128), f32),
            *mode_bufs,
            V((2, MODES, 16, 128), f32), V((C, 256), f32), V((C, 256), f32),

            *mode_bufs[:5],
            V((3 * 128, 128), f32), V((KG_SHARES, KG_ROWS, 128), bf16), V((16, KG_ROWS, 128), bf16),
            V((KG_ROWS, 128), bf16), V((16, KG_ROWS, 128), bf16),
            V((KG_ROWS, 128), f32), V((C, 16, C), f32),
            V((C * 32, NZ), f32), V((C, 32, NZ), bf16),
            dma((14,)), dma((2, 8)), dma((2, 8)),
            *[dma((2,))] * 6,
            *[dma] * 6,
        ],
        compiler_params=pltpu.CompilerParams(
            collective_id=0, has_side_effects=True, vmem_limit_bytes=60 * 2**20
        ),
        cost_estimate=pl.CostEstimate(flops=700_000_000, bytes_accessed=4_000_000, transcendentals=131072),
    )(
        x, ct, spectral, weights.reshape(27, C, C),
        channel_bias.reshape(1, C),
        z_analysis, z_synthesis, y_table, x_table,
    )
    block = (C, BX * BY, NZ)
    outputs, input_grad, spectral_grad, kernel_grad, bias_grad = pl.pallas_call(
        finish,
        out_shape=(
            jax.ShapeDtypeStruct(block, bf16),
            jax.ShapeDtypeStruct(block, bf16),
            jax.ShapeDtypeStruct((C, 16, C), f32),
            jax.ShapeDtypeStruct((27, C, C), f32),
            jax.ShapeDtypeStruct((1, C), f32),
        ),
        in_specs=[any_space] * 7,
        out_specs=(any_space,) * 4 + (vmem,),
        scratch_shapes=[
            *[V(r.shape, r.dtype) for r in results],
            V((48, 128), bf16), pltpu.SMEM((NX * MODES,), f32),
            V((C * 32, NZ), f32), V(block, bf16), V((27, C, C), f32),
            dma((7,)), dma((4,)),
        ],
        compiler_params=pltpu.CompilerParams(vmem_limit_bytes=60 * 2**20),
    )(*results, z_synthesis, x_table)
    field = (C, BX, BY, NZ)
    return (
        outputs.reshape(field), input_grad.reshape(field), spectral_grad.transpose(0, 2, 1),
        kernel_grad.reshape(3, 3, 3, C, C), bias_grad.reshape(C),
    )


def solution(mesh):
    placed = (P(None, "gx", "gy", None), P(None, "gx", "gy", None), P(), P(), P())
    return jax.shard_map(
        layer,
        mesh=mesh,
        in_specs=placed,
        out_specs=(
            P(None, "gx", "gy", None),
            P(None, "gx", "gy", None),
            P(None, None, ("gx", "gy")),
            P(),
            P(),
        ),
        check_vma=False,
    )
```

```python
import functools
import math

import jax
import jax.numpy as jnp
import numpy as np
from jax import lax
from jax.experimental import pallas as pl
from jax.experimental.pallas import tpu as pltpu
from jax.sharding import PartitionSpec as P

MESH = pl.DeviceIdType.MESH
MODES = 16
C = 32
BX, BY, NZ = 8, 4, 128
NX, NY = 64, 128
LANES = BY * NZ
WIDE = (BY + 2) * NZ
NEIGHBOURS = [(i, j) for i in (-1, 0, 1) for j in (-1, 0, 1) if (i, j) != (0, 0)]
GRID_SCALE = 1.0 / math.sqrt(NX * NY * NZ)
MODE_SCALE = 1.0 / math.sqrt(MODES**3)
Y_CLASSES = ((1, 6), (6, 10), (10, 14), (14, 16))
KG_ROWS = 16
KG_SHARES = 14
f32, bf16 = jnp.float32, jnp.bfloat16
DOT_NT = (((1,), (1,)), ((), ()))
DOT_TN = (((0,), (0,)), ((), ()))
DOT_NN = (((1,), (0,)), ((), ()))


def basis(cells):
    rows = np.arange(MODES)
    frequency = np.where(rows < MODES // 2, rows, rows - MODES // 2 + 1)
    phase = frequency[:, None] * np.arange(cells)[None, :] % cells
    angles = phase * (2.0 * math.pi / cells)
    return np.where((rows < MODES // 2)[:, None], np.cos(angles), np.sin(angles)).astype(np.float32)


def split(array):
    high = array.astype(jnp.bfloat16)
    low = (array - high.astype(np.float32)).astype(jnp.bfloat16)
    return high, low


def tables():
    phi_x, phi_y, phi_z = basis(NX), basis(NY), basis(NZ)
    high, low = split(phi_z)
    z_analysis = np.concatenate([high, low], 0)
    z_synthesis = np.concatenate([high, high, low], 0)
    lanes = np.repeat(phi_y.reshape(MODES, 32, BY), C, axis=2)
    y_table = lanes.transpose(1, 0, 2)
    x_table = phi_x.T.reshape(-1)
    return z_analysis, z_synthesis, np.ascontiguousarray(y_table), np.ascontiguousarray(x_table)


def dot(a, b, dims):
    return lax.dot_general(a, b, dims, preferred_element_type=f32)


def x_z_synthesise(cell, recv, px_ref, zs_ref):
    total = px_ref[cell * 16] * recv[0]
    for p in range(1, MODES):
        total = total + px_ref[cell * 16 + p] * recv[p]
    high = total.astype(bf16)
    low = (total - high.astype(f32)).astype(bf16)
    return dot(jnp.concatenate([high, low, high], axis=0), zs_ref[...], DOT_TN)


def kernel(
    x_hbm, ct_hbm, spec_hbm, w_hbm, bias_hbm, za_hbm, zs_hbm, py_hbm, px_hbm,
    out_hbm, ig_hbm, sg_hbm, kr3,
    w_raw, bias_row, za_ref, zs_ref, py_ref, px_ref, wf_ref, wb_ref, bias_ref,
    xin, ctin, spec, flat, ct, acc, stk, dstk, dx, tbuf,
    sx, rx, sy, ry, sz, rz, ct_modes, coefs, mixed,
    sxb, rxb, syb, ryb, szb, rzb,
    ks1, kr1, ks2, kr2, ks3, sg_ref,
    oflat, obf, ibf,
    ready, dma_sem, halo_s, halo_r, xs, xr, ys, yr, zs, zr, k1s, k1r, k2s, k2r, k3s, k3r,
):
    a, b = lax.axis_index("gx"), lax.axis_index("gy")
    h, q = b // 16, lax.rem(b, 16)
    g = 2 * a + h
    partner = (3 - b // 8) * 8 + lax.rem(b, 8)

    def group_x(k):
        rank, other, core = k // 4, lax.rem(k // 2, 2), lax.rem(k, 2)
        steps = jnp.where(rank == 1, 3, jnp.where(rank == 0, 0, rank - 1))
        ta = 2 * lax.rem(a // 2 + steps, 4) + lax.rem(a + core, 2)
        th = lax.rem(h + other, 2)
        return 2 * ta + th, (ta, jnp.where(other == 0, b, partner))

    def group_y(k):
        rank, other = k // 2, lax.rem(k, 2)
        steps = jnp.where(lax.rem(rank, 2) == 1, (rank + 1) // 2, 8 - rank // 2)
        t = 8 * lax.rem(q // 8 + other, 2) + lax.rem(lax.rem(q, 8) + steps, 8)
        return t, (a, t + 16 * h)

    def each(members, action, count=15):
        def step(n, carry):
            action(count - n, *members(count - n))
            return carry

        lax.fori_loop(0, count, step, 0, unroll=True)

    def there(da, db):
        ok = None
        if da == 1:
            ok = a < 7
        if da == -1:
            ok = a > 0
        if db == 1:
            ok = (b < 31) if ok is None else ok & (b < 31)
        if db == -1:
            ok = (b > 0) if ok is None else ok & (b > 0)
        return ok

    barrier = pltpu.get_barrier_semaphore()

    def greet(k, t, peer):
        pl.semaphore_signal(barrier, inc=1, device_id=peer, device_id_type=MESH)

    each(group_x, greet)
    each(group_y, greet, 9)
    awaited = 24
    for da, db in NEIGHBOURS:
        if db == 0:
            continue

        @pl.when(there(da, db))
        def _():
            pl.semaphore_signal(barrier, inc=1, device_id=(a + da, b + db), device_id_type=MESH)

        awaited = awaited + jnp.where(there(da, db), 1, 0)

    load_x = pltpu.make_async_copy(x_hbm, xin, dma_sem.at[0])
    load_ct = pltpu.make_async_copy(ct_hbm, ctin, dma_sem.at[1])
    load_spec = pltpu.make_async_copy(
        spec_hbm.at[:, :, pl.ds(pl.multiple_of(g * 256, 256), 256)], spec, dma_sem.at[2]
    )
    load_x.start()
    small = [
        pltpu.make_async_copy(src, dst, dma_sem.at[5 + n])
        for n, (src, dst) in enumerate(
            ((za_hbm, za_ref), (px_hbm, px_ref), (w_hbm, w_raw), (bias_hbm, bias_row), (zs_hbm, zs_ref), (py_hbm, py_ref))
        )
    ]
    for load in small:
        load.start()
    load_ct.start()
    load_spec.start()

    def x_copy(t, peer, src, buf, ssem, rsem):
        return pltpu.make_async_remote_copy(
            src_ref=src, dst_ref=buf.at[g], send_sem=ssem, recv_sem=rsem,
            device_id=peer, device_id_type=MESH,
        )

    def y_copy(t, peer, src, buf, ssem, rsem):
        return pltpu.make_async_remote_copy(
            src_ref=src, dst_ref=buf.at[q], send_sem=ssem, recv_sem=rsem,
            device_id=peer, device_id_type=MESH,
        )

    def all_of(buf, count, ssem, rsem):
        return pltpu.make_async_remote_copy(
            src_ref=buf.at[pl.ds(0, count)], dst_ref=buf.at[pl.ds(0, count)], send_sem=ssem, recv_sem=rsem,
            device_id=group_y(1)[1], device_id_type=MESH,
        )

    def halo_copy(index, field, n, da, db):
        sx_ = pl.ds(8, 1) if da == 1 else pl.ds(1, 1) if da == -1 else pl.ds(1, 8)
        dx_ = pl.ds(0, 1) if da == 1 else pl.ds(9, 1) if da == -1 else pl.ds(1, 8)
        sl = pl.ds(512, 128) if db == 1 else pl.ds(128, 128) if db == -1 else pl.ds(128, 512)
        dl = pl.ds(0, 128) if db == 1 else pl.ds(640, 128) if db == -1 else pl.ds(128, 512)
        return pltpu.make_async_remote_copy(
            src_ref=field.at[sx_, pl.ds(32, 32), sl], dst_ref=field.at[dx_, pl.ds(32, 32), dl],
            send_sem=halo_s.at[n, index], recv_sem=halo_r.at[n, index],
            device_id=(a + da, b + db), device_id_type=MESH,
        )

    def halo_start(field, n):
        for index, (da, db) in enumerate(NEIGHBOURS):

            @pl.when(there(da, db))
            def _():
                halo_copy(index, field, n, da, db).start()

    def halo_wait_recv(field, n):
        for index, (da, db) in enumerate(NEIGHBOURS):

            @pl.when(there(-da, -db))
            def _():
                halo_copy(index, field, n, da, db).wait_recv()

    def halo_wait_send(field, n):
        for index, (da, db) in enumerate(NEIGHBOURS):

            @pl.when(there(da, db))
            def _():
                halo_copy(index, field, n, da, db).wait_send()

    def zero_rim(field):
        @pl.when(a == 0)
        def _():
            field[0, 32:64, :] = jnp.zeros((C, WIDE), bf16)

        @pl.when(a == 7)
        def _():
            field[9, 32:64, :] = jnp.zeros((C, WIDE), bf16)

        @pl.when(b == 0)
        def _():
            for i in range(10):
                field[i, 32:64, 0:128] = jnp.zeros((C, NZ), bf16)

        @pl.when(b == 31)
        def _():
            for i in range(10):
                field[i, 32:64, 640:768] = jnp.zeros((C, NZ), bf16)

    def z_analyse(i, tiles):
        rows = jnp.concatenate(tiles, axis=0)
        both = dot(za_ref[...], rows, DOT_NT)
        tbuf[i] = both[:16] + both[16:]

    def x_partials(buf):
        rows = [tbuf[i] for i in range(BX)]

        def step(p, carry):
            total = px_ref[(a * 8) * 16 + p] * rows[0]
            for i in range(1, BX):
                total = total + px_ref[(a * 8 + i) * 16 + p] * rows[i]
            buf[p] = total
            return carry

        lax.fori_loop(0, 16, step, 0, unroll=4)

    def y_blocks(recv, send):
        for half in range(2):
            total = recv[half]
            for i in range(1, 8):
                total = total + recv[2 * i + half]
            send[half] = total.astype(bf16)

    def block_of(member, half):
        return 16 * half + jnp.where(h == half, member, lax.rem(member + 8, 16))

    def y_analyse(recv, n):
        def step(k, carry):
            result = list(carry)
            block = group_y(k)[0]
            for half in range(2):
                value = recv[block, half].astype(f32)
                place = block_of(block, half)
                for m in range(MODES):
                    result[m] = result[m] + value * py_ref[place, pl.ds(m, 1), :]
            return tuple(result)

        result = step(0, tuple(jnp.zeros((16, 128), f32) for _ in range(MODES)))
        for near, (low, high) in enumerate(Y_CLASSES):
            all_of(recv, high - low, ys.at[n], yr.at[n, near]).wait_recv()
            result = lax.fori_loop(low, high, step, result, unroll=True)
        return result

    def y_class(k):
        return jnp.where(k < 6, 0, jnp.where(k < 10, 1, jnp.where(k < 14, 2, 3)))

    def to_columns(parts, scale):
        wide = jnp.transpose(jnp.concatenate(parts, axis=0))
        return (wide[0:32] + wide[32:64] + wide[64:96] + wide[96:128]) * scale

    def y_synthesise(modes, scale, send):
        tall = jnp.transpose(jnp.concatenate([modes * scale] * 4, axis=0))
        for half in range(2):
            place = block_of(q, half)
            total = py_ref[place, pl.ds(0, 1), :] * tall[0:16]
            for m in range(1, MODES):
                total = total + py_ref[place, pl.ds(m, 1), :] * tall[16 * m : 16 * m + 16]
            send[half] = total

    lane = lax.broadcasted_iota(jnp.int32, (C, NZ), 1)

    def shift_rows(field, ones):
        def step(i, carry):
            for y in range(BY + 2):
                cells = slice(y * NZ, (y + 1) * NZ)
                value = field[i, 32:64, cells].astype(f32)
                before = jnp.where(lane == 0, 0.0, pltpu.roll(value, 1, 1))
                after = jnp.where(lane == NZ - 1, 0.0, pltpu.roll(value, NZ - 1, 1))
                field[i, 0:32, cells] = before.astype(bf16)
                field[i, 64:96, cells] = after.astype(bf16)
            return carry

        lax.fori_loop(0, 10, step, 0, unroll=2)

    def fill_ones(field):
        def step(i, carry):
            field[i, 96:128, :] = jnp.ones((32, WIDE), bf16)
            return carry

        lax.fori_loop(0, 10, step, 0)

    def convolve(field, weights):
        def step(i, carry):
            total = None
            for d in range(3):
                for e in range(3):
                    tap = (d * 3 + e) * 128
                    part = dot(
                        weights[:, tap : tap + 128], field[i + d, :, e * NZ : e * NZ + LANES], DOT_NN
                    )
                    total = part if total is None else total + part
            acc[i] = total
            return carry

        lax.fori_loop(0, BX, step, 0, unroll=2)

    def unflatten(source, write):
        def step(c, carry):
            flat[pl.ds(pl.multiple_of(c * 32, 32), 32), :] = source[c].astype(f32)
            return carry

        lax.fori_loop(0, C, step, 0, unroll=8)

        def step2(i, carry):
            tiles = [flat[pl.ds(i * BY + y, C, stride=32), :] for y in range(BY)]
            write(i, tiles)
            return carry

        lax.fori_loop(0, BX, step2, 0, unroll=4)

    def flatten(source, target):
        def step(c, carry):
            target[c] = source[pl.ds(pl.multiple_of(c * 32, 32), 32), :].astype(bf16)
            return carry

        lax.fori_loop(0, C, step, 0, unroll=8)

    def prepare_weights():
        row = lax.broadcasted_iota(jnp.int32, (C, 128), 0)
        column = lax.broadcasted_iota(jnp.int32, (C, 128), 1)
        place = [jnp.where(column == row + 32 * f, 1.0, 0.0).astype(bf16) for f in range(3)]
        for tap in range(9):
            total, back_total = None, None
            for f in range(3):
                part = dot(w_raw[tap * 3 + f], place[f], DOT_NN)
                total = part if total is None else total + part
                part = dot(w_raw[(8 - tap) * 3 + 2 - f], place[f], DOT_TN)
                back_total = part if back_total is None else back_total + part
            wf_ref[:, tap * 128 : tap * 128 + 128] = total.astype(bf16)
            wb_ref[:, tap * 128 : tap * 128 + 128] = back_total.astype(bf16)
        spread = jnp.where(column[:, :C] == row[:, :C], jnp.broadcast_to(bias_row[...], (C, C)), 0.0)
        bias_ref[...] = jnp.broadcast_to(jnp.sum(spread, axis=1, keepdims=True), (C, 128))

    load_x.wait()
    small[0].wait()
    small[1].wait()

    def write_x(i, tiles):
        tiles = [t.astype(bf16) for t in tiles]
        for y in range(BY):
            stk[i + 1, 32:64, (y + 1) * NZ : (y + 2) * NZ] = tiles[y]
        z_analyse(i, tiles)

    unflatten(xin, write_x)
    x_partials(sx)
    pl.semaphore_wait(barrier, awaited)
    for k in (6, 8):
        pl.semaphore_signal(ready, inc=1, device_id=group_y(k)[1], device_id_type=MESH)
    each(group_x, lambda k, t, peer: x_copy(t, peer, sx.at[t], rx, xs.at[0], xr.at[0]).start())
    rx[g] = sx[g]
    halo_start(stk, 0)

    zero_rim(stk)
    fill_ones(stk)
    for load in small[2:]:
        load.wait()
    prepare_weights()
    load_ct.wait()

    def write_ct(i, tiles):
        for y in range(BY):
            ct[i, :, y * NZ : (y + 1) * NZ] = tiles[y]

    unflatten(ctin, write_ct)
    for i in (0, 1, 10, 11):
        dx[i] = jnp.zeros((C, LANES), bf16)

    all_of(rx, 15, xs.at[0], xr.at[0]).wait_recv()
    y_blocks(rx, sy)
    pl.semaphore_wait(ready, 2)
    each(group_y, lambda k, t, peer: y_copy(t, peer, sy, ry, ys.at[0], yr.at[0, y_class(k)]).start())
    ry[q] = sy[...]

    halo_wait_recv(stk, 0)
    shift_rows(stk, True)
    convolve(stk, wf_ref)
    load_spec.wait()

    parts = y_analyse(ry, 0)
    for m in range(MODES):
        ct_modes[0, m] = parts[m]
    coefs[...] = to_columns(parts, GRID_SCALE)

    def mix(o, carry):
        mixed[pl.ds(o, 1), :] = jnp.sum(spec[o].astype(f32) * coefs[...], axis=0, keepdims=True)
        return carry

    lax.fori_loop(0, C, mix, 0, unroll=4)
    y_synthesise(mixed[...], MODE_SCALE, sz)
    each(group_x, lambda k, t, peer: x_copy(t, peer, sz.at[lax.rem(t, 2)], rz, zs.at[0], zr.at[0]).start())
    rz[g] = sz[h]
    all_of(rz, 15, zs.at[0], zr.at[0]).wait_recv()

    root = math.sqrt(2.0 / math.pi)

    def point(i, carry):
        modes = x_z_synthesise(a * 8 + i, rz, px_ref, zs_ref)
        tiles = []
        for y in range(BY):
            cells = slice(y * NZ, (y + 1) * NZ)
            v = acc[i, :, cells] + modes[y * C : (y + 1) * C] + bias_ref[...]
            square = v * v
            t = jnp.tanh(root * (v + 0.044715 * (square * v)))
            half = 0.5 * (1.0 + t)
            slope = half + 0.5 * v * (1.0 - t * t) * (root * (1.0 + 3 * 0.044715 * square))
            acc[i, :, cells] = v * half
            delta = (ct[i, :, cells] * slope).astype(bf16)
            dstk[i + 1, 32:64, (y + 1) * NZ : (y + 2) * NZ] = delta
            dx[i + 2, :, cells] = delta
            tiles.append(delta)
        z_analyse(i, tiles)
        return carry

    lax.fori_loop(0, BX, point, 0, unroll=True)

    x_partials(sxb)
    each(group_x, lambda k, t, peer: x_copy(t, peer, sxb.at[t], rxb, xs.at[1], xr.at[1]).start())
    rxb[g] = sxb[g]
    halo_start(dstk, 1)

    zero_rim(dstk)
    fill_ones(dstk)

    def planes(cut):
        return jnp.concatenate([cut(i) for i in range(10)], axis=1)

    idle = jnp.zeros((C, LANES), bf16)
    shifted = jnp.concatenate([planes(lambda i: dx[i + 2]), planes(lambda i: dx[i + 1]), planes(lambda i: dx[i]), planes(lambda i: idle)], axis=0)
    windows = jnp.concatenate(
        [planes(lambda i, e=e: stk[i, :, e * NZ : e * NZ + LANES]) for e in range(3)], axis=0
    )
    kgt = dot(windows, shifted, DOT_NT)
    columns = [jnp.transpose(kgt[128 * e : 128 * e + 128]) for e in range(3)]
    kgp = [columns[e][32 * d : 32 * d + 32] for e in range(3) for d in range(3)]

    for n in range(7):
        block = kgp[n]
        if n < 6:
            block = jnp.where(lane >= 96, pltpu.roll(kgp[7 + n // 3], 96 - 32 * (n % 3), 1), block)
        ks1[2 * n] = block[0:16].astype(bf16)
        ks1[2 * n + 1] = block[16:32].astype(bf16)
    def k1_start(k, t, peer):
        @pl.when(t < KG_SHARES)
        def _():
            x_copy(t, peer, ks1.at[t], kr1, k1s, k1r).start()

    each(group_x, k1_start)

    def spread(i, carry):
        for y in range(BY):
            oflat[pl.ds(i * BY + y, C, stride=32), :] = acc[i, :, y * NZ : (y + 1) * NZ]
        return carry

    lax.fori_loop(0, BX, spread, 0, unroll=4)
    flatten(oflat, obf)
    store_out = pltpu.make_async_copy(obf, out_hbm, dma_sem.at[3])
    store_out.start()

    all_of(rxb, 15, xs.at[1], xr.at[1]).wait_recv()
    y_blocks(rxb, syb)
    each(group_y, lambda k, t, peer: y_copy(t, peer, syb, ryb, ys.at[1], yr.at[1, y_class(k)]).start())
    ryb[q] = syb[...]

    halo_wait_recv(dstk, 1)
    shift_rows(dstk, False)
    @pl.when(g < KG_SHARES)
    def _():
        all_of(kr1, 15, k1s, k1r).wait_recv()
        kr1[g] = ks1[g]
        total = kr1[0].astype(f32)
        for i in range(1, 16):
            total = total + kr1[i].astype(f32)
        ks2[...] = total.astype(bf16)
        kr2[q] = total.astype(bf16)
        each(group_y, lambda k, t, peer: y_copy(t, peer, ks2, kr2, k2s, k2r).start())

    convolve(dstk, wb_ref)

    parts = y_analyse(ryb, 1)
    for m in range(MODES):
        ct_modes[1, m] = parts[m]
    mixed[...] = to_columns(parts, MODE_SCALE)

    def mix_back(o, carry):
        return carry + spec[o].astype(f32) * mixed[pl.ds(o, 1), :]

    back = lax.fori_loop(0, C, mix_back, jnp.zeros((C, 256), f32), unroll=4)
    y_synthesise(back, GRID_SCALE, szb)
    each(group_x, lambda k, t, peer: x_copy(t, peer, szb.at[lax.rem(t, 2)], rzb, zs.at[1], zr.at[1]).start())
    rzb[g] = szb[h]

    @pl.when(g < KG_SHARES)
    def _():
        all_of(kr2, 15, k2s, k2r).wait_recv()
        total = kr2[0].astype(f32)
        for i in range(1, 16):
            total = total + kr2[i].astype(f32)
        total = total * GRID_SCALE
        ks3[...] = total
        pltpu.make_async_copy(ks3, kr3.at[g], dma_sem.at[12]).start()
        each(group_x, lambda k, t, peer: x_copy(t, peer, ks3, kr3, k3s, k3r).start())

    coef_rows = ct_modes[0, q]
    coef_rows = coef_rows + pltpu.roll(coef_rows, 64, 1)
    coef_rows = (coef_rows + pltpu.roll(coef_rows, 32, 1)) * GRID_SCALE
    wide = jnp.transpose(ct_modes[1, q])
    back_columns = jnp.transpose(wide[0:32] + wide[32:64] + wide[64:96] + wide[96:128]) * MODE_SCALE
    for o in range(C):
        sg_ref[o] = (coef_rows * back_columns[:, o : o + 1])[:, 0:32]

    store_sg = pltpu.make_async_copy(sg_ref, sg_hbm, dma_sem.at[13])
    store_sg.start()

    store_out.wait()
    all_of(rzb, 15, zs.at[1], zr.at[1]).wait_recv()
    def last(i, carry):
        modes = x_z_synthesise(a * 8 + i, rzb, px_ref, zs_ref)
        for y in range(BY):
            cells = slice(y * NZ, (y + 1) * NZ)
            oflat[pl.ds(i * BY + y, C, stride=32), :] = acc[i, :, cells] + modes[y * C : (y + 1) * C]
        return carry

    lax.fori_loop(0, BX, last, 0, unroll=True)
    flatten(oflat, ibf)
    store_ig = pltpu.make_async_copy(ibf, ig_hbm, dma_sem.at[4])
    store_ig.start()

    for n in range(2):
        all_of((rx, rxb)[n], 15, xs.at[n], xr.at[n]).wait_send()
        all_of((rz, rzb)[n], 15, zs.at[n], zr.at[n]).wait_send()
        all_of((ry, ryb)[n], 15, ys.at[n], yr.at[n, 0]).wait_send()
    halo_wait_send(stk, 0)
    halo_wait_send(dstk, 1)
    def in_shares(has, has_not):
        pl.when(g < KG_SHARES)(has)
        pl.when(g >= KG_SHARES)(has_not)

    in_shares(
        lambda: all_of(kr1, KG_SHARES - 1, k1s, k1r).wait_send(),
        lambda: all_of(kr1, KG_SHARES, k1s, k1r).wait_send(),
    )

    @pl.when(g < KG_SHARES)
    def _():
        all_of(kr2, 15, k2s, k2r).wait_send()
        all_of(rx, 15, k3s, k3r).wait_send()
        pltpu.make_async_copy(ks3, kr3.at[g], dma_sem.at[12]).wait()

    store_sg.wait()
    in_shares(
        lambda: all_of(kr3, KG_SHARES - 1, k3s, k3r).wait_recv(),
        lambda: all_of(kr3, KG_SHARES, k3s, k3r).wait_recv(),
    )
    store_ig.wait()


def finish(
    kr_in, ig_in, out_in, sg_in, out_hbm, ig_hbm, sg_hbm, kg_hbm, bg_ref, kr, ig, out, sg, kg, load_sem, store_sem
):
    pairs = ((kr_in, kr), (ig_in, ig), (out_in, out), (sg_in, sg))
    loads = [pltpu.make_async_copy(src, dst, load_sem.at[n]) for n, (src, dst) in enumerate(pairs)]
    pairs = ((kg, kg_hbm), (ig, ig_hbm), (out, out_hbm), (sg, sg_hbm))
    stores = [pltpu.make_async_copy(src, dst, store_sem.at[n]) for n, (src, dst) in enumerate(pairs)]
    for load in loads:
        load.start()
    loads[0].wait()
    blocks = [jnp.concatenate([kr[2 * n], kr[2 * n + 1]], axis=0) for n in range(7)]
    for d in range(3):
        for e in range(3):
            for f in range(3):
                n, offset = e * 3 + d, 32 * f
                if n >= 7:
                    n, offset = (n - 7) * 3 + f, 96
                moved = blocks[n] if offset == 0 else pltpu.roll(blocks[n], 128 - offset, 1)
                kg[(d * 3 + e) * 3 + f] = moved[:, 0:32]
    bg_ref[...] = jnp.transpose(blocks[6])[96:97, :]
    stores[0].start()
    for load, store in zip(loads[1:], stores[1:]):
        load.wait()
        store.start()
    for store in stores:
        store.wait()


def layer(inputs, cotangent, weights, channel_bias, spectral):
    z_analysis, z_synthesis, y_table, x_table = tables()
    x = inputs.reshape(C, BX * BY, NZ)
    ct = cotangent.reshape(C, BX * BY, NZ)
    any_space = pl.BlockSpec(memory_space=pl.ANY)
    vmem = pl.BlockSpec(memory_space=pltpu.VMEM)
    dma = pltpu.SemaphoreType.DMA
    V = pltpu.VMEM
    mode_bufs = [
        V((16, 16, 128), f32), V((16, 16, 128), f32),
        V((2, 16, 128), bf16), V((16, 2, 16, 128), bf16),
        V((2, 16, 128), f32), V((16, 16, 128), f32),
    ]
    outputs, input_grad, spectral_grad, shares = pl.pallas_call(
        kernel,
        out_shape=(
            jax.ShapeDtypeStruct((C, BX * BY, NZ), bf16),
            jax.ShapeDtypeStruct((C, BX * BY, NZ), bf16),
            jax.ShapeDtypeStruct((C, 16, C), f32),
            jax.ShapeDtypeStruct((KG_SHARES, KG_ROWS, 128), f32),
        ),
        in_specs=[pl.BlockSpec(memory_space=pltpu.HBM)] * 9,
        out_specs=(any_space,) * 4,
        scratch_shapes=[
            V((27, C, C), bf16), V((1, C), f32), V((32, 128), bf16), V((48, 128), bf16),
            V((32, MODES, 128), f32), pltpu.SMEM((NX * MODES,), f32),
            V((C, 1152), bf16), V((C, 1152), bf16), V((C, 128), f32),
            V((C, 32, NZ), bf16), V((C, 32, NZ), bf16), V((C, C, 256), bf16),
            V((C * 32, NZ), f32), V((BX, C, LANES), f32), V((BX, C, LANES), f32),
            V((10, 128, WIDE), bf16), V((10, 128, WIDE), bf16), V((12, C, LANES), bf16),
            V((BX, 16, 128), f32),
            *mode_bufs,
            V((2, MODES, 16, 128), f32), V((C, 256), f32), V((C, 256), f32),

            *mode_bufs,
            V((KG_SHARES, KG_ROWS, 128), bf16), V((16, KG_ROWS, 128), bf16),
            V((KG_ROWS, 128), bf16), V((16, KG_ROWS, 128), bf16),
            V((KG_ROWS, 128), f32), V((C, 16, C), f32),
            V((C * 32, NZ), f32), V((C, 32, NZ), bf16), V((C, 32, NZ), bf16),
            pltpu.SemaphoreType.REGULAR, dma((14,)), dma((2, 8)), dma((2, 8)),
            *[dma((2,))] * 3, dma((2, 4)), *[dma((2,))] * 2,
            *[dma] * 6,
        ],
        compiler_params=pltpu.CompilerParams(
            collective_id=0, has_side_effects=True, vmem_limit_bytes=60 * 2**20
        ),
        cost_estimate=pl.CostEstimate(flops=700_000_000, bytes_accessed=4_000_000, transcendentals=131072),
    )(
        x, ct, spectral, weights.reshape(27, C, C),
        channel_bias.reshape(1, C),
        z_analysis, z_synthesis, y_table, x_table,
    )
    block = (C, BX * BY, NZ)
    outputs, input_grad, spectral_grad, kernel_grad, bias_grad = pl.pallas_call(
        finish,
        out_shape=(
            jax.ShapeDtypeStruct(block, bf16),
            jax.ShapeDtypeStruct(block, bf16),
            jax.ShapeDtypeStruct((C, 16, C), f32),
            jax.ShapeDtypeStruct((27, C, C), f32),
            jax.ShapeDtypeStruct((1, C), f32),
        ),
        in_specs=[any_space] * 4,
        out_specs=(any_space,) * 4 + (vmem,),
        scratch_shapes=[
            V(shares.shape, f32), V(block, bf16), V(block, bf16), V((C, 16, C), f32), V((27, C, C), f32),
            dma((4,)), dma((4,)),
        ],
        compiler_params=pltpu.CompilerParams(vmem_limit_bytes=60 * 2**20),
    )(shares, input_grad, outputs, spectral_grad)
    field = (C, BX, BY, NZ)
    return (
        outputs.reshape(field), input_grad.reshape(field), spectral_grad.transpose(0, 2, 1),
        kernel_grad.reshape(3, 3, 3, C, C), bias_grad.reshape(C),
    )


def solution(mesh):
    placed = (P(None, "gx", "gy", None), P(None, "gx", "gy", None), P(), P(), P())
    return jax.shard_map(
        layer,
        mesh=mesh,
        in_specs=placed,
        out_specs=(
            P(None, "gx", "gy", None),
            P(None, "gx", "gy", None),
            P(None, None, ("gx", "gy")),
            P(),
            P(),
        ),
        check_vma=False,
    )
```

```python
import functools
import math

import jax
import jax.numpy as jnp
import numpy as np
from jax import lax
from jax.experimental import pallas as pl
from jax.experimental.pallas import tpu as pltpu
from jax.sharding import PartitionSpec as P

MESH = pl.DeviceIdType.MESH
MODES = 16
C = 32
BX, BY, NZ = 8, 4, 128
NX, NY = 64, 128
LANES = BY * NZ
WIDE = (BY + 2) * NZ
NEIGHBOURS = [(i, j) for i in (-1, 0, 1) for j in (-1, 0, 1) if (i, j) != (0, 0)]
GRID_SCALE = 1.0 / math.sqrt(NX * NY * NZ)
MODE_SCALE = 1.0 / math.sqrt(MODES**3)
Y_CLASSES = ((1, 6), (6, 10), (10, 14), (14, 16))
KG_ROWS = 16
KG_SHARES = 14
f32, bf16 = jnp.float32, jnp.bfloat16
DOT_NT = (((1,), (1,)), ((), ()))
DOT_TN = (((0,), (0,)), ((), ()))
DOT_NN = (((1,), (0,)), ((), ()))


def basis(cells):
    rows = np.arange(MODES)
    frequency = np.where(rows < MODES // 2, rows, rows - MODES // 2 + 1)
    phase = frequency[:, None] * np.arange(cells)[None, :] % cells
    angles = phase * (2.0 * math.pi / cells)
    return np.where((rows < MODES // 2)[:, None], np.cos(angles), np.sin(angles)).astype(np.float32)


def split(array):
    high = array.astype(jnp.bfloat16)
    low = (array - high.astype(np.float32)).astype(jnp.bfloat16)
    return high, low


def tables():
    phi_x, phi_y, phi_z = basis(NX), basis(NY), basis(NZ)
    high, low = split(phi_z)
    z_analysis = np.concatenate([high, low], 0)
    z_synthesis = np.concatenate([high, high, low], 0)
    lanes = np.repeat(phi_y.reshape(MODES, 32, BY), C, axis=2)
    y_table = lanes.transpose(1, 0, 2)
    x_table = phi_x.T.reshape(-1)
    return z_analysis, z_synthesis, np.ascontiguousarray(y_table), np.ascontiguousarray(x_table)


def dot(a, b, dims):
    return lax.dot_general(a, b, dims, preferred_element_type=f32)


def x_z_synthesise(cell, recv, px_ref, zs_ref):
    values = [recv[p].astype(f32) for p in range(MODES)]
    planes = []
    for i in range(BX):
        total = px_ref[(cell + i) * 16] * values[0]
        for p in range(1, MODES):
            total = total + px_ref[(cell + i) * 16 + p] * values[p]
        planes.append(total)
    total = jnp.concatenate(planes, axis=1)
    high = total.astype(bf16)
    low = (total - high.astype(f32)).astype(bf16)
    return dot(jnp.concatenate([high, low, high], axis=0), zs_ref[...], DOT_TN)


def kernel(
    x_hbm, ct_hbm, spec_hbm, w_hbm, bias_hbm, za_hbm, zs_hbm, py_hbm, px_hbm,
    out_ref, ig_ref, sg_ref, kr3,
    w_raw, bias_row, za_ref, zs_ref, py_ref, px_ref, wf_ref, wb_ref, bias_ref,
    xin, ctin, spec, flat, ct, acc, stk, dstk, dx, tbuf,
    sx, rx, sy, ry, sz, rz, ct_modes, coefs, mixed,
    sxb, rxb, syb, ryb, szb, rzb,
    ks1, kr1, ks2, kr2, ks3,
    oflat,
    ready, dma_sem, halo_s, halo_r, xs, xr, ys, yr, zs, zr, k1s, k1r, k2s, k2r, k3s, k3r,
):
    a, b = lax.axis_index("gx"), lax.axis_index("gy")
    h, q = b // 16, lax.rem(b, 16)
    g = 2 * a + h
    partner = (3 - b // 8) * 8 + lax.rem(b, 8)

    def group_x(k):
        rank, other, core = k // 4, lax.rem(k // 2, 2), lax.rem(k, 2)
        steps = jnp.where(rank == 1, 3, jnp.where(rank == 0, 0, rank - 1))
        ta = 2 * lax.rem(a // 2 + steps, 4) + lax.rem(a + core, 2)
        th = lax.rem(h + other, 2)
        return 2 * ta + th, (ta, jnp.where(other == 0, b, partner))

    def group_y(k):
        rank, other = k // 2, lax.rem(k, 2)
        steps = jnp.where(lax.rem(rank, 2) == 1, (rank + 1) // 2, 8 - rank // 2)
        t = 8 * lax.rem(q // 8 + other, 2) + lax.rem(lax.rem(q, 8) + steps, 8)
        return t, (a, t + 16 * h)

    def each(members, action, count=15):
        def step(n, carry):
            action(count - n, *members(count - n))
            return carry

        lax.fori_loop(0, count, step, 0, unroll=True)

    def there(da, db):
        ok = None
        if da == 1:
            ok = a < 7
        if da == -1:
            ok = a > 0
        if db == 1:
            ok = (b < 31) if ok is None else ok & (b < 31)
        if db == -1:
            ok = (b > 0) if ok is None else ok & (b > 0)
        return ok

    barrier = pltpu.get_barrier_semaphore()

    def greet(k, t, peer):
        pl.semaphore_signal(barrier, inc=1, device_id=peer, device_id_type=MESH)

    each(group_x, greet)
    each(group_y, greet, 9)
    awaited = 24
    for da, db in NEIGHBOURS:
        if db == 0:
            continue

        @pl.when(there(da, db))
        def _():
            pl.semaphore_signal(barrier, inc=1, device_id=(a + da, b + db), device_id_type=MESH)

        awaited = awaited + jnp.where(there(da, db), 1, 0)

    load_x = pltpu.make_async_copy(x_hbm, xin, dma_sem.at[0])
    load_ct = pltpu.make_async_copy(ct_hbm, ctin, dma_sem.at[1])
    load_spec = pltpu.make_async_copy(
        spec_hbm.at[:, :, pl.ds(pl.multiple_of(g * 256, 256), 256)], spec, dma_sem.at[2]
    )
    load_x.start()
    small = [
        pltpu.make_async_copy(src, dst, dma_sem.at[5 + n])
        for n, (src, dst) in enumerate(
            ((za_hbm, za_ref), (px_hbm, px_ref), (w_hbm, w_raw), (bias_hbm, bias_row), (zs_hbm, zs_ref), (py_hbm, py_ref))
        )
    ]
    for load in small:
        load.start()
    load_ct.start()
    load_spec.start()

    def x_copy(t, peer, src, buf, ssem, rsem):
        return pltpu.make_async_remote_copy(
            src_ref=src, dst_ref=buf.at[g], send_sem=ssem, recv_sem=rsem,
            device_id=peer, device_id_type=MESH,
        )

    def y_copy(t, peer, src, buf, ssem, rsem):
        return pltpu.make_async_remote_copy(
            src_ref=src, dst_ref=buf.at[q], send_sem=ssem, recv_sem=rsem,
            device_id=peer, device_id_type=MESH,
        )

    def all_of(buf, count, ssem, rsem):
        return pltpu.make_async_remote_copy(
            src_ref=buf.at[pl.ds(0, count)], dst_ref=buf.at[pl.ds(0, count)], send_sem=ssem, recv_sem=rsem,
            device_id=group_y(1)[1], device_id_type=MESH,
        )

    def halo_copy(index, field, n, da, db):
        sx_ = pl.ds(8, 1) if da == 1 else pl.ds(1, 1) if da == -1 else pl.ds(1, 8)
        dx_ = pl.ds(0, 1) if da == 1 else pl.ds(9, 1) if da == -1 else pl.ds(1, 8)
        sl = pl.ds(512, 128) if db == 1 else pl.ds(128, 128) if db == -1 else pl.ds(128, 512)
        dl = pl.ds(0, 128) if db == 1 else pl.ds(640, 128) if db == -1 else pl.ds(128, 512)
        return pltpu.make_async_remote_copy(
            src_ref=field.at[sx_, pl.ds(32, 32), sl], dst_ref=field.at[dx_, pl.ds(32, 32), dl],
            send_sem=halo_s.at[n, index], recv_sem=halo_r.at[n, index],
            device_id=(a + da, b + db), device_id_type=MESH,
        )

    def halo_start(field, n):
        for index, (da, db) in enumerate(NEIGHBOURS):

            @pl.when(there(da, db))
            def _():
                halo_copy(index, field, n, da, db).start()

    def halo_wait_recv(field, n):
        for index, (da, db) in enumerate(NEIGHBOURS):

            @pl.when(there(-da, -db))
            def _():
                halo_copy(index, field, n, da, db).wait_recv()

    def halo_wait_send(field, n):
        for index, (da, db) in enumerate(NEIGHBOURS):

            @pl.when(there(da, db))
            def _():
                halo_copy(index, field, n, da, db).wait_send()

    def zero_rim(field):
        @pl.when(a == 0)
        def _():
            field[0, 32:64, :] = jnp.zeros((C, WIDE), bf16)

        @pl.when(a == 7)
        def _():
            field[9, 32:64, :] = jnp.zeros((C, WIDE), bf16)

        @pl.when(b == 0)
        def _():
            for i in range(10):
                field[i, 32:64, 0:128] = jnp.zeros((C, NZ), bf16)

        @pl.when(b == 31)
        def _():
            for i in range(10):
                field[i, 32:64, 640:768] = jnp.zeros((C, NZ), bf16)

    def z_analyse(i, tiles):
        rows = jnp.concatenate(tiles, axis=0)
        both = dot(za_ref[...], rows, DOT_NT)
        tbuf[i] = both[:16] + both[16:]

    def x_partials(buf):
        rows = [tbuf[i] for i in range(BX)]

        def step(p, carry):
            total = px_ref[(a * 8) * 16 + p] * rows[0]
            for i in range(1, BX):
                total = total + px_ref[(a * 8 + i) * 16 + p] * rows[i]
            buf[p] = total
            return carry

        lax.fori_loop(0, 16, step, 0, unroll=4)

    def y_blocks(recv, send):
        for half in range(2):
            total = recv[half]
            for i in range(1, 8):
                total = total + recv[2 * i + half]
            send[half] = total.astype(bf16)

    def block_of(member, half):
        return 16 * half + jnp.where(h == half, member, lax.rem(member + 8, 16))

    def y_analyse(recv, n):
        def step(k, carry):
            result = list(carry)
            block = group_y(k)[0]
            for half in range(2):
                value = recv[block, half].astype(f32)
                place = block_of(block, half)
                for m in range(MODES):
                    result[m] = result[m] + value * py_ref[place, pl.ds(m, 1), :]
            return tuple(result)

        result = step(0, tuple(jnp.zeros((16, 128), f32) for _ in range(MODES)))
        for near, (low, high) in enumerate(Y_CLASSES):
            all_of(recv, high - low, ys.at[n], yr.at[n, near]).wait_recv()
            result = lax.fori_loop(low, high, step, result, unroll=True)
        return result

    def y_class(k):
        return jnp.where(k < 6, 0, jnp.where(k < 10, 1, jnp.where(k < 14, 2, 3)))

    def to_columns(parts, scale):
        wide = jnp.transpose(jnp.concatenate(parts, axis=0))
        return (wide[0:32] + wide[32:64] + wide[64:96] + wide[96:128]) * scale

    def y_synthesise(modes, scale, send):
        tall = jnp.transpose(jnp.concatenate([modes * scale] * 4, axis=0))
        for half in range(2):
            place = block_of(q, half)
            total = py_ref[place, pl.ds(0, 1), :] * tall[0:16]
            for m in range(1, MODES):
                total = total + py_ref[place, pl.ds(m, 1), :] * tall[16 * m : 16 * m + 16]
            send[half] = total.astype(send.dtype)

    lane = lax.broadcasted_iota(jnp.int32, (C, NZ), 1)

    def shift_rows(field, ones):
        def step(i, carry):
            for y in range(BY + 2):
                cells = slice(y * NZ, (y + 1) * NZ)
                value = field[i, 32:64, cells].astype(f32)
                before = jnp.where(lane == 0, 0.0, pltpu.roll(value, 1, 1))
                after = jnp.where(lane == NZ - 1, 0.0, pltpu.roll(value, NZ - 1, 1))
                field[i, 0:32, cells] = before.astype(bf16)
                field[i, 64:96, cells] = after.astype(bf16)
            return carry

        lax.fori_loop(0, 10, step, 0, unroll=2)

    def fill_ones(field):
        def step(i, carry):
            field[i, 96:128, :] = jnp.ones((32, WIDE), bf16)
            return carry

        lax.fori_loop(0, 10, step, 0)

    def convolve(field, weights, shift=None):
        def step(i, carry):
            total = None
            for d in range(3):
                for e in range(3):
                    tap = (d * 3 + e) * 128
                    part = dot(
                        weights[:, tap : tap + 128], field[i + d, :, e * NZ : e * NZ + LANES], DOT_NN
                    )
                    total = part if total is None else total + part
            acc[i] = total if shift is None else total + shift
            return carry

        lax.fori_loop(0, BX, step, 0, unroll=2)

    def unflatten(source, write):
        def step(c, carry):
            flat[pl.ds(pl.multiple_of(c * 32, 32), 32), :] = source[c].astype(f32)
            return carry

        lax.fori_loop(0, C, step, 0, unroll=8)

        def step2(i, carry):
            tiles = [flat[pl.ds(i * BY + y, C, stride=32), :] for y in range(BY)]
            write(i, tiles)
            return carry

        lax.fori_loop(0, BX, step2, 0, unroll=4)

    def flatten(source, target):
        def step(c, carry):
            target[c] = source[pl.ds(pl.multiple_of(c * 32, 32), 32), :].astype(bf16)
            return carry

        lax.fori_loop(0, C, step, 0, unroll=8)

    def prepare_weights():
        row = lax.broadcasted_iota(jnp.int32, (C, 128), 0)
        column = lax.broadcasted_iota(jnp.int32, (C, 128), 1)
        place = [jnp.where(column == row + 32 * f, 1.0, 0.0).astype(bf16) for f in range(3)]
        for tap in range(9):
            total, back_total = None, None
            for f in range(3):
                part = dot(w_raw[tap * 3 + f], place[f], DOT_NN)
                total = part if total is None else total + part
                part = dot(w_raw[(8 - tap) * 3 + 2 - f], place[f], DOT_TN)
                back_total = part if back_total is None else back_total + part
            wf_ref[:, tap * 128 : tap * 128 + 128] = total.astype(bf16)
            wb_ref[:, tap * 128 : tap * 128 + 128] = back_total.astype(bf16)
        spread = jnp.where(column[:, :C] == row[:, :C], jnp.broadcast_to(bias_row[...], (C, C)), 0.0)
        bias_ref[...] = jnp.broadcast_to(jnp.sum(spread, axis=1, keepdims=True), (C, 128))

    load_x.wait()
    small[0].wait()
    small[1].wait()

    def write_x(i, tiles):
        tiles = [t.astype(bf16) for t in tiles]
        for y in range(BY):
            stk[i + 1, 32:64, (y + 1) * NZ : (y + 2) * NZ] = tiles[y]
        z_analyse(i, tiles)

    unflatten(xin, write_x)
    x_partials(sx)
    pl.semaphore_wait(barrier, awaited)
    for k in (6, 8):
        pl.semaphore_signal(ready, inc=1, device_id=group_y(k)[1], device_id_type=MESH)
    each(group_x, lambda k, t, peer: x_copy(t, peer, sx.at[t], rx, xs.at[0], xr.at[0]).start())
    rx[g] = sx[g]
    halo_start(stk, 0)

    zero_rim(stk)
    fill_ones(stk)
    for load in small[2:]:
        load.wait()
    prepare_weights()
    load_ct.wait()

    def write_ct(i, tiles):
        for y in range(BY):
            ct[i, :, y * NZ : (y + 1) * NZ] = tiles[y]

    unflatten(ctin, write_ct)
    for i in (0, 1, 10, 11):
        dx[i] = jnp.zeros((C, LANES), bf16)

    all_of(rx, 15, xs.at[0], xr.at[0]).wait_recv()
    y_blocks(rx, sy)
    pl.semaphore_wait(ready, 2)
    each(group_y, lambda k, t, peer: y_copy(t, peer, sy, ry, ys.at[0], yr.at[0, y_class(k)]).start())
    ry[q] = sy[...]

    halo_wait_recv(stk, 0)
    shift_rows(stk, True)
    convolve(stk, wf_ref, jnp.concatenate([bias_ref[...]] * BY, axis=1))
    load_spec.wait()

    parts = y_analyse(ry, 0)
    for m in range(MODES):
        ct_modes[0, m] = parts[m]
    coefs[...] = to_columns(parts, GRID_SCALE)

    def mix(o, carry):
        mixed[pl.ds(o, 1), :] = jnp.sum(spec[o].astype(f32) * coefs[...], axis=0, keepdims=True)
        return carry

    lax.fori_loop(0, C, mix, 0, unroll=4)
    y_synthesise(mixed[...], MODE_SCALE, sz)
    each(group_x, lambda k, t, peer: x_copy(t, peer, sz.at[lax.rem(t, 2)], rz, zs.at[0], zr.at[0]).start())
    rz[g] = sz[h]
    all_of(rz, 15, zs.at[0], zr.at[0]).wait_recv()

    root = math.sqrt(2.0 / math.pi)

    modes_all = x_z_synthesise(a * 8, rz, px_ref, zs_ref)

    def point(i):
        modes = modes_all[128 * i : 128 * i + 128]
        tiles = []
        for y in range(BY):
            cells = slice(y * NZ, (y + 1) * NZ)
            v = acc[i, :, cells] + modes[y * C : (y + 1) * C]
            square = v * v
            t = jnp.tanh(v * (square * (0.044715 * root) + root))
            half = 0.5 * t + 0.5
            slope = half * ((v * (square * (3 * 0.044715 * root) + root)) * (1.0 - t) + 1.0)
            acc[i, :, cells] = v * half
            delta = (ct[i, :, cells] * slope).astype(bf16)
            dstk[i + 1, 32:64, (y + 1) * NZ : (y + 2) * NZ] = delta
            dx[i + 2, :, cells] = delta
            tiles.append(delta)
        z_analyse(i, tiles)

    for i in range(BX):
        point(i)

    x_partials(sxb)
    each(group_x, lambda k, t, peer: x_copy(t, peer, sxb.at[t], rxb, xs.at[1], xr.at[1]).start())
    rxb[g] = sxb[g]
    halo_start(dstk, 1)

    zero_rim(dstk)
    fill_ones(dstk)

    def planes(cut):
        return jnp.concatenate([cut(i) for i in range(10)], axis=1)

    idle = jnp.zeros((C, LANES), bf16)
    shifted = jnp.concatenate([planes(lambda i: dx[i + 2]), planes(lambda i: dx[i + 1]), planes(lambda i: dx[i]), planes(lambda i: idle)], axis=0)
    windows = jnp.concatenate(
        [planes(lambda i, e=e: stk[i, : 128 if e == 1 else 96, e * NZ : e * NZ + LANES]) for e in range(3)], axis=0
    )
    kgt = dot(windows, shifted, DOT_NT)
    empty = jnp.zeros((32, 128), f32)
    kgt = [jnp.concatenate([kgt[0:96], empty], axis=0), kgt[96:224], jnp.concatenate([kgt[224:320], empty], axis=0)]
    columns = [jnp.transpose(kgt[e]) for e in range(3)]
    kgp = [columns[e][32 * d : 32 * d + 32] for e in range(3) for d in range(3)]

    for n in range(7):
        block = kgp[n]
        if n < 6:
            block = jnp.where(lane >= 96, pltpu.roll(kgp[7 + n // 3], 96 - 32 * (n % 3), 1), block)
        else:
            block = jnp.where(lane >= 96, kgp[4], block)
        ks1[2 * n] = block[0:16].astype(bf16)
        ks1[2 * n + 1] = block[16:32].astype(bf16)
    def k1_start(k, t, peer):
        @pl.when(t < KG_SHARES)
        def _():
            x_copy(t, peer, ks1.at[t], kr1, k1s, k1r).start()

    each(group_x, k1_start)

    def spread(i, carry):
        for y in range(BY):
            oflat[pl.ds(i * BY + y, C, stride=32), :] = acc[i, :, y * NZ : (y + 1) * NZ]
        return carry

    lax.fori_loop(0, BX, spread, 0, unroll=4)
    flatten(oflat, out_ref)

    all_of(rxb, 15, xs.at[1], xr.at[1]).wait_recv()
    y_blocks(rxb, syb)
    each(group_y, lambda k, t, peer: y_copy(t, peer, syb, ryb, ys.at[1], yr.at[1, y_class(k)]).start())
    ryb[q] = syb[...]

    halo_wait_recv(dstk, 1)
    shift_rows(dstk, False)
    @pl.when(g < KG_SHARES)
    def _():
        all_of(kr1, 15, k1s, k1r).wait_recv()
        kr1[g] = ks1[g]
        total = kr1[0].astype(f32)
        for i in range(1, 16):
            total = total + kr1[i].astype(f32)
        ks2[...] = total.astype(bf16)
        kr2[q] = total.astype(bf16)
        each(group_y, lambda k, t, peer: y_copy(t, peer, ks2, kr2, k2s, k2r).start())

    convolve(dstk, wb_ref)

    parts = y_analyse(ryb, 1)
    for m in range(MODES):
        ct_modes[1, m] = parts[m]
    mixed[...] = to_columns(parts, MODE_SCALE)

    def mix_back(o, carry):
        return carry + spec[o].astype(f32) * mixed[pl.ds(o, 1), :]

    back = lax.fori_loop(0, C, mix_back, jnp.zeros((C, 256), f32), unroll=4)
    y_synthesise(back, GRID_SCALE, szb)
    each(group_x, lambda k, t, peer: x_copy(t, peer, szb.at[lax.rem(t, 2)], rzb, zs.at[1], zr.at[1]).start())
    rzb[g] = szb[h]

    @pl.when(g < KG_SHARES)
    def _():
        all_of(kr2, 15, k2s, k2r).wait_recv()
        total = kr2[0].astype(f32)
        for i in range(1, 16):
            total = total + kr2[i].astype(f32)
        total = total * GRID_SCALE
        ks3[...] = total
        kr3[g] = total
        each(group_x, lambda k, t, peer: x_copy(t, peer, ks3, kr3, k3s, k3r).start())

    coef_rows = ct_modes[0, q]
    coef_rows = coef_rows + pltpu.roll(coef_rows, 64, 1)
    coef_rows = (coef_rows + pltpu.roll(coef_rows, 32, 1)) * GRID_SCALE
    wide = jnp.transpose(ct_modes[1, q])
    back_columns = jnp.transpose(wide[0:32] + wide[32:64] + wide[64:96] + wide[96:128]) * MODE_SCALE
    for o in range(C):
        sg_ref[o] = (coef_rows * back_columns[:, o : o + 1])[:, 0:32]

    all_of(rzb, 15, zs.at[1], zr.at[1]).wait_recv()
    modes_all = x_z_synthesise(a * 8, rzb, px_ref, zs_ref)

    def last(i):
        modes = modes_all[128 * i : 128 * i + 128]
        for y in range(BY):
            cells = slice(y * NZ, (y + 1) * NZ)
            oflat[pl.ds(i * BY + y, C, stride=32), :] = acc[i, :, cells] + modes[y * C : (y + 1) * C]

    for i in range(BX):
        last(i)
    flatten(oflat, ig_ref)

    for n in range(2):
        all_of((rx, rxb)[n], 15, xs.at[n], xr.at[n]).wait_send()
        all_of((rz, rzb)[n], 15, zs.at[n], zr.at[n]).wait_send()
        all_of((ry, ryb)[n], 15, ys.at[n], yr.at[n, 0]).wait_send()
    halo_wait_send(stk, 0)
    halo_wait_send(dstk, 1)
    def in_shares(has, has_not):
        pl.when(g < KG_SHARES)(has)
        pl.when(g >= KG_SHARES)(has_not)

    in_shares(
        lambda: all_of(kr1, KG_SHARES - 1, k1s, k1r).wait_send(),
        lambda: all_of(kr1, KG_SHARES, k1s, k1r).wait_send(),
    )

    @pl.when(g < KG_SHARES)
    def _():
        all_of(kr2, 15, k2s, k2r).wait_send()
        all_of(rx, 15, k3s, k3r).wait_send()

    in_shares(
        lambda: all_of(kr3, KG_SHARES - 1, k3s, k3r).wait_recv(),
        lambda: all_of(kr3, KG_SHARES, k3s, k3r).wait_recv(),
    )


def finish(kr, ig, out, sg, out_hbm, ig_hbm, sg_hbm, kg_hbm, bg_ref, kg, store_sem):
    pairs = ((ig, ig_hbm), (out, out_hbm), (sg, sg_hbm), (kg, kg_hbm))
    stores = [pltpu.make_async_copy(src, dst, store_sem.at[n]) for n, (src, dst) in enumerate(pairs)]
    for store in stores[:3]:
        store.start()
    blocks = [jnp.concatenate([kr[2 * n], kr[2 * n + 1]], axis=0) for n in range(7)]
    for d in range(3):
        for e in range(3):
            for f in range(3):
                n, offset = e * 3 + d, 32 * f
                if n >= 7:
                    n, offset = (n - 7) * 3 + f, 96
                moved = blocks[n] if offset == 0 else pltpu.roll(blocks[n], 128 - offset, 1)
                kg[(d * 3 + e) * 3 + f] = moved[:, 0:32]
    bg_ref[...] = jnp.transpose(blocks[6])[96:97, :]
    stores[3].start()
    for store in stores:
        store.wait()


def layer(inputs, cotangent, weights, channel_bias, spectral):
    z_analysis, z_synthesis, y_table, x_table = tables()
    x = inputs.reshape(C, BX * BY, NZ)
    ct = cotangent.reshape(C, BX * BY, NZ)
    any_space = pl.BlockSpec(memory_space=pl.ANY)
    vmem = pl.BlockSpec(memory_space=pltpu.VMEM)
    dma = pltpu.SemaphoreType.DMA
    V = pltpu.VMEM
    mode_bufs = [
        V((16, 16, 128), f32), V((16, 16, 128), f32),
        V((2, 16, 128), bf16), V((16, 2, 16, 128), bf16),
        V((2, 16, 128), bf16), V((16, 16, 128), bf16),
    ]
    block = (C, BX * BY, NZ)
    operands = (
        x, ct, spectral, weights.reshape(27, C, C), channel_bias.reshape(1, C),
        z_analysis, z_synthesis, y_table, x_table,
    )
    results = pl.pallas_call(
        kernel,
        out_shape=(V(block, bf16), V(block, bf16), V((C, 16, C), f32), V((KG_SHARES, KG_ROWS, 128), f32)),
        in_specs=[pl.BlockSpec(memory_space=pltpu.HBM)] * 9,
        out_specs=(vmem,) * 4,
        scratch_shapes=[
            V((27, C, C), bf16), V((1, C), f32), V((32, 128), bf16), V((48, 128), bf16),
            V((32, MODES, 128), f32), pltpu.SMEM((NX * MODES,), f32),
            V((C, 1152), bf16), V((C, 1152), bf16), V((C, 128), f32),
            V((C, 32, NZ), bf16), V((C, 32, NZ), bf16), V((C, C, 256), bf16),
            V((C * 32, NZ), f32), V((BX, C, LANES), f32), V((BX, C, LANES), f32),
            V((10, 128, WIDE), bf16), V((10, 128, WIDE), bf16), V((12, C, LANES), bf16),
            V((BX, 16, 128), f32),
            *mode_bufs,
            V((2, MODES, 16, 128), f32), V((C, 256), f32), V((C, 256), f32),

            *mode_bufs,
            V((KG_SHARES, KG_ROWS, 128), bf16), V((16, KG_ROWS, 128), bf16),
            V((KG_ROWS, 128), bf16), V((16, KG_ROWS, 128), bf16),
            V((KG_ROWS, 128), f32),
            V((C * 32, NZ), f32),
            pltpu.SemaphoreType.REGULAR, dma((11,)), dma((2, 8)), dma((2, 8)),
            *[dma((2,))] * 3, dma((2, 4)), *[dma((2,))] * 2,
            *[dma] * 6,
        ],
        compiler_params=pltpu.CompilerParams(
            collective_id=0, has_side_effects=True, vmem_limit_bytes=40 * 2**20
        ),
        cost_estimate=pl.CostEstimate(flops=700_000_000, bytes_accessed=4_000_000, transcendentals=131072),
    )(*[pltpu.with_memory_space_constraint(jnp.asarray(operand), pltpu.HBM) for operand in operands])
    outputs, input_grad, spectral_grad, shares = [
        pltpu.with_memory_space_constraint(result, pltpu.VMEM) for result in results
    ]
    outputs, input_grad, spectral_grad, kernel_grad, bias_grad = pl.pallas_call(
        finish,
        out_shape=(
            jax.ShapeDtypeStruct(block, bf16),
            jax.ShapeDtypeStruct(block, bf16),
            jax.ShapeDtypeStruct((C, 16, C), f32),
            jax.ShapeDtypeStruct((27, C, C), f32),
            jax.ShapeDtypeStruct((1, C), f32),
        ),
        in_specs=[vmem] * 4,
        out_specs=(any_space,) * 4 + (vmem,),
        scratch_shapes=[
            V((27, C, C), f32), dma((4,)),
        ],
        compiler_params=pltpu.CompilerParams(vmem_limit_bytes=16 * 2**20),
    )(shares, input_grad, outputs, spectral_grad)
    field = (C, BX, BY, NZ)
    return (
        outputs.reshape(field), input_grad.reshape(field), spectral_grad.transpose(0, 2, 1),
        kernel_grad.reshape(3, 3, 3, C, C), bias_grad.reshape(C),
    )


def solution(mesh):
    placed = (P(None, "gx", "gy", None), P(None, "gx", "gy", None), P(), P(), P())
    return jax.shard_map(
        layer,
        mesh=mesh,
        in_specs=placed,
        out_specs=(
            P(None, "gx", "gy", None),
            P(None, "gx", "gy", None),
            P(None, None, ("gx", "gy")),
            P(),
            P(),
        ),
        check_vma=False,
    )
```

```python
import functools
import math

import jax
import jax.numpy as jnp
import numpy as np
from jax import lax
from jax.experimental import pallas as pl
from jax.experimental.pallas import tpu as pltpu
from jax.sharding import PartitionSpec as P

MESH = pl.DeviceIdType.MESH
MODES = 16
C = 32
BX, BY, NZ = 8, 4, 128
NX, NY = 64, 128
LANES = BY * NZ
WIDE = (BY + 2) * NZ
NEIGHBOURS = [(i, j) for i in (-1, 0, 1) for j in (-1, 0, 1) if (i, j) != (0, 0)]
GRID_SCALE = 1.0 / math.sqrt(NX * NY * NZ)
MODE_SCALE = 1.0 / math.sqrt(MODES**3)
Y_CLASSES = ((1, 6), (6, 10), (10, 14), (14, 16))
KG_ROWS = 16
KG_SHARES = 14
f32, bf16 = jnp.float32, jnp.bfloat16
DOT_NT = (((1,), (1,)), ((), ()))
DOT_TN = (((0,), (0,)), ((), ()))
DOT_NN = (((1,), (0,)), ((), ()))


def basis(cells):
    rows = np.arange(MODES)
    frequency = np.where(rows < MODES // 2, rows, rows - MODES // 2 + 1)
    phase = frequency[:, None] * np.arange(cells)[None, :] % cells
    angles = phase * (2.0 * math.pi / cells)
    return np.where((rows < MODES // 2)[:, None], np.cos(angles), np.sin(angles)).astype(np.float32)


def split(array):
    high = array.astype(jnp.bfloat16)
    low = (array - high.astype(np.float32)).astype(jnp.bfloat16)
    return high, low


def tables():
    phi_x, phi_y, phi_z = basis(NX), basis(NY), basis(NZ)
    high, low = split(phi_z)
    z_analysis = np.concatenate([high, low], 0)
    z_synthesis = np.concatenate([high, high, low], 0)
    lanes = np.repeat(phi_y.reshape(MODES, 32, BY), C, axis=2)
    y_table = lanes.transpose(1, 0, 2)
    x_table = phi_x.T.reshape(-1)
    return z_analysis, z_synthesis, np.ascontiguousarray(y_table), np.ascontiguousarray(x_table)


def dot(a, b, dims):
    return lax.dot_general(a, b, dims, preferred_element_type=f32)


def x_z_synthesise(cell, recv, px_ref, zs_ref):
    values = [recv[p].astype(f32) for p in range(MODES)]
    planes = []
    for i in range(BX):
        total = px_ref[(cell + i) * 16] * values[0]
        for p in range(1, MODES):
            total = total + px_ref[(cell + i) * 16 + p] * values[p]
        planes.append(total)
    total = jnp.concatenate(planes, axis=1)
    high = total.astype(bf16)
    low = (total - high.astype(f32)).astype(bf16)
    return dot(jnp.concatenate([high, low, high], axis=0), zs_ref[...], DOT_TN)


def kernel(
    x_hbm, ct_hbm, spec_hbm, w_hbm, bias_hbm, za_hbm, zs_hbm, py_hbm, px_hbm,
    out_ref, ig_ref, sg_ref, kr3,
    w_raw, bias_row, za_ref, zs_ref, py_ref, px_ref, wf_ref, wb_ref, bias_ref,
    xin, ctin, spec, flat, ct, acc, stk, dstk, dx, tbuf,
    sx, rx, sy, ry, sz, rz, ct_modes, coefs, mixed,
    sxb, rxb, syb, ryb, szb, rzb,
    ks1, kr1, ks2, kr2, ks3,
    oflat, flat2, by_input,
    ready, dma_sem, halo_s, halo_r, xs, xr, ys, yr, zs, zr, k1s, k1r, k2s, k2r, k3s, k3r,
):
    a, b = lax.axis_index("gx"), lax.axis_index("gy")
    h, q = b // 16, lax.rem(b, 16)
    g = 2 * a + h
    partner = (3 - b // 8) * 8 + lax.rem(b, 8)

    load_x = pltpu.make_async_copy(x_hbm, xin, dma_sem.at[0])
    load_x.start()

    def group_x(k):
        rank, other, core = k // 4, lax.rem(k // 2, 2), lax.rem(k, 2)
        steps = jnp.where(rank == 1, 3, jnp.where(rank == 0, 0, rank - 1))
        ta = 2 * lax.rem(a // 2 + steps, 4) + lax.rem(a + core, 2)
        th = lax.rem(h + other, 2)
        return 2 * ta + th, (ta, jnp.where(other == 0, b, partner))

    def group_y(k):
        rank, other = k // 2, lax.rem(k, 2)
        steps = jnp.where(lax.rem(rank, 2) == 1, (rank + 1) // 2, 8 - rank // 2)
        t = 8 * lax.rem(q // 8 + other, 2) + lax.rem(lax.rem(q, 8) + steps, 8)
        return t, (a, t + 16 * h)

    def each(members, action, count=15):
        def step(n, carry):
            action(count - n, *members(count - n))
            return carry

        lax.fori_loop(0, count, step, 0, unroll=True)

    def there(da, db):
        ok = None
        if da == 1:
            ok = a < 7
        if da == -1:
            ok = a > 0
        if db == 1:
            ok = (b < 31) if ok is None else ok & (b < 31)
        if db == -1:
            ok = (b > 0) if ok is None else ok & (b > 0)
        return ok

    barrier = pltpu.get_barrier_semaphore()

    def greet(k, t, peer):
        pl.semaphore_signal(barrier, inc=1, device_id=peer, device_id_type=MESH)

    each(group_x, greet)
    each(group_y, greet, 9)
    awaited = 24
    for da, db in NEIGHBOURS:
        if db == 0:
            continue

        @pl.when(there(da, db))
        def _():
            pl.semaphore_signal(barrier, inc=1, device_id=(a + da, b + db), device_id_type=MESH)

        awaited = awaited + jnp.where(there(da, db), 1, 0)

    load_ct = pltpu.make_async_copy(ct_hbm, ctin, dma_sem.at[1])
    load_spec = pltpu.make_async_copy(
        spec_hbm.at[:, :, pl.ds(pl.multiple_of(g * 256, 256), 256)], spec, dma_sem.at[2]
    )
    small = [
        pltpu.make_async_copy(src, dst, dma_sem.at[5 + n])
        for n, (src, dst) in enumerate(
            ((za_hbm, za_ref), (px_hbm, px_ref), (w_hbm, w_raw), (bias_hbm, bias_row), (zs_hbm, zs_ref), (py_hbm, py_ref))
        )
    ]
    for load in small:
        load.start()
    load_ct.start()
    load_spec.start()

    def x_copy(t, peer, src, buf, ssem, rsem):
        return pltpu.make_async_remote_copy(
            src_ref=src, dst_ref=buf.at[g], send_sem=ssem, recv_sem=rsem,
            device_id=peer, device_id_type=MESH,
        )

    def y_copy(t, peer, src, buf, ssem, rsem):
        return pltpu.make_async_remote_copy(
            src_ref=src, dst_ref=buf.at[q], send_sem=ssem, recv_sem=rsem,
            device_id=peer, device_id_type=MESH,
        )

    def all_of(buf, count, ssem, rsem):
        return pltpu.make_async_remote_copy(
            src_ref=buf.at[pl.ds(0, count)], dst_ref=buf.at[pl.ds(0, count)], send_sem=ssem, recv_sem=rsem,
            device_id=group_y(1)[1], device_id_type=MESH,
        )

    def halo_copy(index, field, n, da, db):
        sx_ = pl.ds(8, 1) if da == 1 else pl.ds(1, 1) if da == -1 else pl.ds(1, 8)
        dx_ = pl.ds(0, 1) if da == 1 else pl.ds(9, 1) if da == -1 else pl.ds(1, 8)
        sl = pl.ds(512, 128) if db == 1 else pl.ds(128, 128) if db == -1 else pl.ds(128, 512)
        dl = pl.ds(0, 128) if db == 1 else pl.ds(640, 128) if db == -1 else pl.ds(128, 512)
        return pltpu.make_async_remote_copy(
            src_ref=field.at[sx_, pl.ds(32, 32), sl], dst_ref=field.at[dx_, pl.ds(32, 32), dl],
            send_sem=halo_s.at[n, index], recv_sem=halo_r.at[n, index],
            device_id=(a + da, b + db), device_id_type=MESH,
        )

    def halo_start(field, n):
        for index, (da, db) in enumerate(NEIGHBOURS):

            @pl.when(there(da, db))
            def _():
                halo_copy(index, field, n, da, db).start()

    def halo_wait_recv(field, n):
        for index, (da, db) in enumerate(NEIGHBOURS):

            @pl.when(there(-da, -db))
            def _():
                halo_copy(index, field, n, da, db).wait_recv()

    def halo_wait_send(field, n):
        for index, (da, db) in enumerate(NEIGHBOURS):

            @pl.when(there(da, db))
            def _():
                halo_copy(index, field, n, da, db).wait_send()

    def zero_rim(field):
        @pl.when(a == 0)
        def _():
            field[0, 32:64, :] = jnp.zeros((C, WIDE), bf16)

        @pl.when(a == 7)
        def _():
            field[9, 32:64, :] = jnp.zeros((C, WIDE), bf16)

        @pl.when(b == 0)
        def _():
            for i in range(10):
                field[i, 32:64, 0:128] = jnp.zeros((C, NZ), bf16)

        @pl.when(b == 31)
        def _():
            for i in range(10):
                field[i, 32:64, 640:768] = jnp.zeros((C, NZ), bf16)

    def z_analyse(i, tiles):
        rows = jnp.concatenate(tiles, axis=0)
        both = dot(za_ref[...], rows, DOT_NT)
        tbuf[i] = both[:16] + both[16:]

    def x_partials(buf):
        rows = [tbuf[i] for i in range(BX)]

        def step(p, carry):
            total = px_ref[(a * 8) * 16 + p] * rows[0]
            for i in range(1, BX):
                total = total + px_ref[(a * 8 + i) * 16 + p] * rows[i]
            buf[p] = total
            return carry

        lax.fori_loop(0, 16, step, 0, unroll=4)

    def y_blocks(recv, send):
        for half in range(2):
            total = recv[half]
            for i in range(1, 8):
                total = total + recv[2 * i + half]
            send[half] = total.astype(bf16)

    def block_of(member, half):
        return 16 * half + jnp.where(h == half, member, lax.rem(member + 8, 16))

    def y_analyse(recv, n):
        def step(k, carry):
            result = list(carry)
            block = group_y(k)[0]
            for half in range(2):
                value = recv[block, half].astype(f32)
                place = block_of(block, half)
                for m in range(MODES):
                    result[m] = result[m] + value * py_ref[place, pl.ds(m, 1), :]
            return tuple(result)

        result = step(0, tuple(jnp.zeros((16, 128), f32) for _ in range(MODES)))
        for near, (low, high) in enumerate(Y_CLASSES):
            all_of(recv, high - low, ys.at[n], yr.at[n, near]).wait_recv()
            result = lax.fori_loop(low, high, step, result, unroll=True)
        return result

    def y_class(k):
        return jnp.where(k < 6, 0, jnp.where(k < 10, 1, jnp.where(k < 14, 2, 3)))

    def to_columns(parts, scale):
        wide = jnp.transpose(jnp.concatenate(parts, axis=0))
        return (wide[0:32] + wide[32:64] + wide[64:96] + wide[96:128]) * scale

    def y_synthesise(modes, scale, send):
        tall = jnp.transpose(jnp.concatenate([modes * scale] * 4, axis=0))
        for half in range(2):
            place = block_of(q, half)
            total = py_ref[place, pl.ds(0, 1), :] * tall[0:16]
            for m in range(1, MODES):
                total = total + py_ref[place, pl.ds(m, 1), :] * tall[16 * m : 16 * m + 16]
            send[half] = total.astype(send.dtype)

    lane = lax.broadcasted_iota(jnp.int32, (C, NZ), 1)

    def shift_rows(field, ones):
        def step(i, carry):
            for y in range(BY + 2):
                cells = slice(y * NZ, (y + 1) * NZ)
                value = field[i, 32:64, cells].astype(f32)
                before = jnp.where(lane == 0, 0.0, pltpu.roll(value, 1, 1))
                after = jnp.where(lane == NZ - 1, 0.0, pltpu.roll(value, NZ - 1, 1))
                field[i, 0:32, cells] = before.astype(bf16)
                field[i, 64:96, cells] = after.astype(bf16)
            return carry

        lax.fori_loop(0, 10, step, 0, unroll=2)

    def fill_ones(field):
        def step(i, carry):
            field[i, 96:128, :] = jnp.ones((32, WIDE), bf16)
            return carry

        lax.fori_loop(0, 10, step, 0)

    def convolve(field, weights, shift=None):
        def step(i, carry):
            total = None
            for d in range(3):
                for e in range(3):
                    tap = (d * 3 + e) * 128
                    part = dot(
                        weights[:, tap : tap + 128], field[i + d, :, e * NZ : e * NZ + LANES], DOT_NN
                    )
                    total = part if total is None else total + part
            acc[i] = total if shift is None else total + shift
            return carry

        lax.fori_loop(0, BX, step, 0, unroll=2)

    def unflatten(source, write):
        def step(c, carry):
            flat[pl.ds(pl.multiple_of(c * 32, 32), 32), :] = source[c].astype(f32)
            return carry

        lax.fori_loop(0, C, step, 0, unroll=8)

        def step2(i, carry):
            tiles = [flat[pl.ds(i * BY + y, C, stride=32), :] for y in range(BY)]
            write(i, tiles)
            return carry

        lax.fori_loop(0, BX, step2, 0, unroll=4)

    def flatten(source, target):
        def step(c, carry):
            target[c] = source[pl.ds(pl.multiple_of(c * 32, 32), 32), :].astype(bf16)
            return carry

        lax.fori_loop(0, C, step, 0, unroll=8)

    def prepare_weights():
        row = lax.broadcasted_iota(jnp.int32, (C, 128), 0)
        column = lax.broadcasted_iota(jnp.int32, (C, 128), 1)
        place = [jnp.where(column == row + 32 * f, 1.0, 0.0).astype(bf16) for f in range(3)]
        for tap in range(9):
            total, back_total = None, None
            for f in range(3):
                part = dot(w_raw[tap * 3 + f], place[f], DOT_NN)
                total = part if total is None else total + part
                part = dot(w_raw[(8 - tap) * 3 + 2 - f], place[f], DOT_TN)
                back_total = part if back_total is None else back_total + part
            wf_ref[:, tap * 128 : tap * 128 + 128] = total.astype(bf16)
            wb_ref[:, tap * 128 : tap * 128 + 128] = back_total.astype(bf16)
        spread = jnp.where(column[:, :C] == row[:, :C], jnp.broadcast_to(bias_row[...], (C, C)), 0.0)
        bias_ref[...] = jnp.broadcast_to(jnp.sum(spread, axis=1, keepdims=True), (C, 128))

    load_x.wait()
    small[0].wait()
    small[1].wait()

    def write_x(i, tiles):
        tiles = [t.astype(bf16) for t in tiles]
        for y in range(BY):
            stk[i + 1, 32:64, (y + 1) * NZ : (y + 2) * NZ] = tiles[y]
        z_analyse(i, tiles)

    unflatten(xin, write_x)
    x_partials(sx)
    pl.semaphore_wait(barrier, awaited)
    for k in (6, 8):
        pl.semaphore_signal(ready, inc=1, device_id=group_y(k)[1], device_id_type=MESH)
    each(group_x, lambda k, t, peer: x_copy(t, peer, sx.at[t], rx, xs.at[0], xr.at[0]).start())
    rx[g] = sx[g]
    halo_start(stk, 0)

    zero_rim(stk)
    fill_ones(stk)
    for load in small[2:]:
        load.wait()
    prepare_weights()
    load_ct.wait()

    def write_ct(i, tiles):
        for y in range(BY):
            ct[i, :, y * NZ : (y + 1) * NZ] = tiles[y]

    unflatten(ctin, write_ct)
    for i in (0, 1, 10, 11):
        dx[i] = jnp.zeros((C, LANES), bf16)

    all_of(rx, 15, xs.at[0], xr.at[0]).wait_recv()
    y_blocks(rx, sy)
    pl.semaphore_wait(ready, 2)
    each(group_y, lambda k, t, peer: y_copy(t, peer, sy, ry, ys.at[0], yr.at[0, y_class(k)]).start())
    ry[q] = sy[...]

    halo_wait_recv(stk, 0)
    shift_rows(stk, True)
    convolve(stk, wf_ref, jnp.concatenate([bias_ref[...]] * BY, axis=1))
    load_spec.wait()

    def widen(o, carry):
        for n in range(2):
            flat2[n, pl.ds(pl.multiple_of(o * 32, 32), 32), :] = spec[o, :, 128 * n : 128 * n + 128].astype(f32)
        return carry

    lax.fori_loop(0, C, widen, 0, unroll=4)

    def gather(c, carry):
        for n in range(2):
            by_input[c, :, 128 * n : 128 * n + 128] = flat2[n, pl.ds(c, C, stride=32), :]
        return carry

    lax.fori_loop(0, C, gather, 0, unroll=4)

    parts = y_analyse(ry, 0)
    for m in range(MODES):
        ct_modes[0, m] = parts[m]
    coefs[...] = to_columns(parts, GRID_SCALE)

    def mix(c, carry):
        return carry + by_input[c] * coefs[pl.ds(c, 1), :]

    y_synthesise(lax.fori_loop(0, C, mix, jnp.zeros((C, 256), f32), unroll=4), MODE_SCALE, sz)
    each(group_x, lambda k, t, peer: x_copy(t, peer, sz.at[lax.rem(t, 2)], rz, zs.at[0], zr.at[0]).start())
    rz[g] = sz[h]
    all_of(rz, 15, zs.at[0], zr.at[0]).wait_recv()

    root = math.sqrt(2.0 / math.pi)

    modes_all = x_z_synthesise(a * 8, rz, px_ref, zs_ref)

    def point(i):
        modes = modes_all[128 * i : 128 * i + 128]
        tiles = []
        for y in range(BY):
            cells = slice(y * NZ, (y + 1) * NZ)
            v = acc[i, :, cells] + modes[y * C : (y + 1) * C]
            square = v * v
            t = jnp.tanh(v * (square * (0.044715 * root) + root))
            half = 0.5 * t + 0.5
            slope = half * ((v * (square * (3 * 0.044715 * root) + root)) * (1.0 - t) + 1.0)
            acc[i, :, cells] = v * half
            delta = (ct[i, :, cells] * slope).astype(bf16)
            dstk[i + 1, 32:64, (y + 1) * NZ : (y + 2) * NZ] = delta
            dx[i + 2, :, cells] = delta
            tiles.append(delta)
        z_analyse(i, tiles)

    for i in range(BX):
        point(i)

    x_partials(sxb)
    each(group_x, lambda k, t, peer: x_copy(t, peer, sxb.at[t], rxb, xs.at[1], xr.at[1]).start())
    rxb[g] = sxb[g]
    halo_start(dstk, 1)

    zero_rim(dstk)
    fill_ones(dstk)

    def planes(cut):
        return jnp.concatenate([cut(i) for i in range(10)], axis=1)

    idle = jnp.zeros((C, LANES), bf16)
    shifted = [planes(lambda i, d=d: dx[i + 2 - d]) for d in range(3)] + [planes(lambda i: idle)]
    windows = [planes(lambda i, e=e: stk[i, : 112 if e == 1 else 96, e * NZ : e * NZ + LANES]) for e in range(3)]
    kgt = dot(jnp.concatenate(windows, axis=0), jnp.concatenate(shifted, axis=0), DOT_NT)
    empty = jnp.zeros((32, 128), f32)
    kgt = [
        jnp.concatenate([kgt[0:96], empty], axis=0),
        jnp.concatenate([kgt[96:208], empty[:16]], axis=0),
        jnp.concatenate([kgt[208:304], empty], axis=0),
    ]
    columns = [jnp.transpose(kgt[e]) for e in range(3)]
    kgp = [columns[e][32 * d : 32 * d + 32] for e in range(3) for d in range(3)]

    for n in range(7):
        block = kgp[n]
        if n < 6:
            block = jnp.where(lane >= 96, pltpu.roll(kgp[7 + n // 3], 96 - 32 * (n % 3), 1), block)
        else:
            block = jnp.where(lane >= 96, kgp[4], block)
        ks1[2 * n] = block[0:16].astype(bf16)
        ks1[2 * n + 1] = block[16:32].astype(bf16)
    def k1_start(k, t, peer):
        @pl.when(t < KG_SHARES)
        def _():
            x_copy(t, peer, ks1.at[t], kr1, k1s, k1r).start()

    each(group_x, k1_start)

    def spread(i, carry):
        for y in range(BY):
            oflat[pl.ds(i * BY + y, C, stride=32), :] = acc[i, :, y * NZ : (y + 1) * NZ]
        return carry

    lax.fori_loop(0, BX, spread, 0, unroll=4)
    flatten(oflat, out_ref)

    all_of(rxb, 15, xs.at[1], xr.at[1]).wait_recv()
    y_blocks(rxb, syb)
    each(group_y, lambda k, t, peer: y_copy(t, peer, syb, ryb, ys.at[1], yr.at[1, y_class(k)]).start())
    ryb[q] = syb[...]

    halo_wait_recv(dstk, 1)
    shift_rows(dstk, False)
    @pl.when(g < KG_SHARES)
    def _():
        all_of(kr1, 15, k1s, k1r).wait_recv()
        kr1[g] = ks1[g]
        total = kr1[0].astype(f32)
        for i in range(1, 16):
            total = total + kr1[i].astype(f32)
        ks2[...] = total.astype(bf16)
        kr2[q] = total.astype(bf16)
        each(group_y, lambda k, t, peer: y_copy(t, peer, ks2, kr2, k2s, k2r).start())

    convolve(dstk, wb_ref)

    parts = y_analyse(ryb, 1)
    for m in range(MODES):
        ct_modes[1, m] = parts[m]
    mixed[...] = to_columns(parts, MODE_SCALE)

    def mix_back(o, carry):
        return carry + spec[o].astype(f32) * mixed[pl.ds(o, 1), :]

    back = lax.fori_loop(0, C, mix_back, jnp.zeros((C, 256), f32), unroll=4)
    y_synthesise(back, GRID_SCALE, szb)
    each(group_x, lambda k, t, peer: x_copy(t, peer, szb.at[lax.rem(t, 2)], rzb, zs.at[1], zr.at[1]).start())
    rzb[g] = szb[h]

    @pl.when(g < KG_SHARES)
    def _():
        all_of(kr2, 15, k2s, k2r).wait_recv()
        total = kr2[0].astype(f32)
        for i in range(1, 16):
            total = total + kr2[i].astype(f32)
        total = total * GRID_SCALE
        ks3[...] = total
        kr3[g] = total
        each(group_x, lambda k, t, peer: x_copy(t, peer, ks3, kr3, k3s, k3r).start())

    coef_rows = ct_modes[0, q]
    coef_rows = coef_rows + pltpu.roll(coef_rows, 64, 1)
    coef_rows = (coef_rows + pltpu.roll(coef_rows, 32, 1)) * GRID_SCALE
    wide = jnp.transpose(ct_modes[1, q])
    back_columns = jnp.transpose(wide[0:32] + wide[32:64] + wide[64:96] + wide[96:128]) * MODE_SCALE
    for o in range(C):
        sg_ref[o] = (coef_rows * back_columns[:, o : o + 1])[:, 0:32]

    all_of(rzb, 15, zs.at[1], zr.at[1]).wait_recv()
    modes_all = x_z_synthesise(a * 8, rzb, px_ref, zs_ref)

    def last(i):
        modes = modes_all[128 * i : 128 * i + 128]
        for y in range(BY):
            cells = slice(y * NZ, (y + 1) * NZ)
            oflat[pl.ds(i * BY + y, C, stride=32), :] = acc[i, :, cells] + modes[y * C : (y + 1) * C]

    for i in range(BX):
        last(i)
    flatten(oflat, ig_ref)

    for n in range(2):
        all_of((rx, rxb)[n], 15, xs.at[n], xr.at[n]).wait_send()
        all_of((rz, rzb)[n], 15, zs.at[n], zr.at[n]).wait_send()
        all_of((ry, ryb)[n], 15, ys.at[n], yr.at[n, 0]).wait_send()
    halo_wait_send(stk, 0)
    halo_wait_send(dstk, 1)
    def in_shares(has, has_not):
        pl.when(g < KG_SHARES)(has)
        pl.when(g >= KG_SHARES)(has_not)

    in_shares(
        lambda: all_of(kr1, KG_SHARES - 1, k1s, k1r).wait_send(),
        lambda: all_of(kr1, KG_SHARES, k1s, k1r).wait_send(),
    )

    @pl.when(g < KG_SHARES)
    def _():
        all_of(kr2, 15, k2s, k2r).wait_send()
        all_of(rx, 15, k3s, k3r).wait_send()

    in_shares(
        lambda: all_of(kr3, KG_SHARES - 1, k3s, k3r).wait_recv(),
        lambda: all_of(kr3, KG_SHARES, k3s, k3r).wait_recv(),
    )


def finish(kr, ig, out, sg, out_hbm, ig_hbm, sg_hbm, kg_hbm, bg_hbm, kg, bg, store_sem):
    pairs = ((ig, ig_hbm), (out, out_hbm), (sg, sg_hbm), (bg, bg_hbm), (kg, kg_hbm))
    stores = [pltpu.make_async_copy(src, dst, store_sem.at[n]) for n, (src, dst) in enumerate(pairs)]
    for store in stores[:3]:
        store.start()
    blocks = [jnp.concatenate([kr[2 * n], kr[2 * n + 1]], axis=0) for n in range(7)]
    bg[...] = jnp.transpose(blocks[6])[96:97, :]
    stores[3].start()
    for d in range(3):
        for e in range(3):
            for f in range(3):
                n, offset = e * 3 + d, 32 * f
                if n >= 7:
                    n, offset = (n - 7) * 3 + f, 96
                moved = blocks[n] if offset == 0 else pltpu.roll(blocks[n], 128 - offset, 1)
                kg[(d * 3 + e) * 3 + f] = moved[:, 0:32]
    stores[4].start()
    for store in stores:
        store.wait()


def layer(inputs, cotangent, weights, channel_bias, spectral):
    z_analysis, z_synthesis, y_table, x_table = tables()
    x = inputs.reshape(C, BX * BY, NZ)
    ct = cotangent.reshape(C, BX * BY, NZ)
    any_space = pl.BlockSpec(memory_space=pl.ANY)
    vmem = pl.BlockSpec(memory_space=pltpu.VMEM)
    dma = pltpu.SemaphoreType.DMA
    V = pltpu.VMEM
    mode_bufs = [
        V((16, 16, 128), f32), V((16, 16, 128), f32),
        V((2, 16, 128), bf16), V((16, 2, 16, 128), bf16),
        V((2, 16, 128), bf16), V((16, 16, 128), bf16),
    ]
    block = (C, BX * BY, NZ)
    operands = (
        x, ct, spectral, weights.reshape(27, C, C), channel_bias.reshape(1, C),
        z_analysis, z_synthesis, y_table, x_table,
    )
    results = pl.pallas_call(
        kernel,
        out_shape=(V(block, bf16), V(block, bf16), V((C, 16, C), f32), V((KG_SHARES, KG_ROWS, 128), f32)),
        in_specs=[pl.BlockSpec(memory_space=pltpu.HBM)] * 9,
        out_specs=(vmem,) * 4,
        scratch_shapes=[
            V((27, C, C), bf16), V((1, C), f32), V((32, 128), bf16), V((48, 128), bf16),
            V((32, MODES, 128), f32), pltpu.SMEM((NX * MODES,), f32),
            V((C, 1152), bf16), V((C, 1152), bf16), V((C, 128), f32),
            V((C, 32, NZ), bf16), V((C, 32, NZ), bf16), V((C, C, 256), bf16),
            V((C * 32, NZ), f32), V((BX, C, LANES), f32), V((BX, C, LANES), f32),
            V((10, 128, WIDE), bf16), V((10, 128, WIDE), bf16), V((12, C, LANES), bf16),
            V((BX, 16, 128), f32),
            *mode_bufs,
            V((2, MODES, 16, 128), f32), V((C, 256), f32), V((C, 256), f32),

            *mode_bufs,
            V((KG_SHARES, KG_ROWS, 128), bf16), V((16, KG_ROWS, 128), bf16),
            V((KG_ROWS, 128), bf16), V((16, KG_ROWS, 128), bf16),
            V((KG_ROWS, 128), f32),
            V((C * 32, NZ), f32), V((2, C * C, 128), f32), V((C, C, 256), f32),
            pltpu.SemaphoreType.REGULAR, dma((11,)), dma((2, 8)), dma((2, 8)),
            *[dma((2,))] * 3, dma((2, 4)), *[dma((2,))] * 2,
            *[dma] * 6,
        ],
        compiler_params=pltpu.CompilerParams(
            collective_id=0, has_side_effects=True, vmem_limit_bytes=40 * 2**20
        ),
        cost_estimate=pl.CostEstimate(flops=700_000_000, bytes_accessed=4_000_000, transcendentals=131072),
    )(*[pltpu.with_memory_space_constraint(jnp.asarray(operand), pltpu.HBM) for operand in operands])
    outputs, input_grad, spectral_grad, shares = [
        pltpu.with_memory_space_constraint(result, pltpu.VMEM) for result in results
    ]
    outputs, input_grad, spectral_grad, kernel_grad, bias_grad = pl.pallas_call(
        finish,
        out_shape=(
            jax.ShapeDtypeStruct(block, bf16),
            jax.ShapeDtypeStruct(block, bf16),
            jax.ShapeDtypeStruct((C, 16, C), f32),
            jax.ShapeDtypeStruct((27, C, C), f32),
            jax.ShapeDtypeStruct((1, C), f32),
        ),
        in_specs=[vmem] * 4,
        out_specs=(any_space,) * 5,
        scratch_shapes=[
            V((27, C, C), f32), V((1, C), f32), dma((5,)),
        ],
        compiler_params=pltpu.CompilerParams(vmem_limit_bytes=16 * 2**20),
    )(shares, input_grad, outputs, spectral_grad)
    field = (C, BX, BY, NZ)
    return (
        outputs.reshape(field), input_grad.reshape(field), spectral_grad.transpose(0, 2, 1),
        kernel_grad.reshape(3, 3, 3, C, C), bias_grad.reshape(C),
    )


def solution(mesh):
    placed = (P(None, "gx", "gy", None), P(None, "gx", "gy", None), P(), P(), P())
    return jax.shard_map(
        layer,
        mesh=mesh,
        in_specs=placed,
        out_specs=(
            P(None, "gx", "gy", None),
            P(None, "gx", "gy", None),
            P(None, None, ("gx", "gy")),
            P(),
            P(),
        ),
        check_vma=False,
    )
```

```python
import functools
import math

import jax
import jax.numpy as jnp
import numpy as np
from jax import lax
from jax.experimental import pallas as pl
from jax.experimental.pallas import tpu as pltpu
from jax.sharding import PartitionSpec as P

MESH = pl.DeviceIdType.MESH
MODES = 16
C = 32
BX, BY, NZ = 8, 4, 128
NX, NY = 64, 128
LANES = BY * NZ
WIDE = (BY + 2) * NZ
NEIGHBOURS = [(i, j) for i in (-1, 0, 1) for j in (-1, 0, 1) if (i, j) != (0, 0)]
GRID_SCALE = 1.0 / math.sqrt(NX * NY * NZ)
MODE_SCALE = 1.0 / math.sqrt(MODES**3)
Y_CLASSES = ((1, 6), (6, 10), (10, 14), (14, 16))
KG_ROWS = 32
KG_SHARES = 7
f32, bf16 = jnp.float32, jnp.bfloat16
DOT_NT = (((1,), (1,)), ((), ()))
DOT_TN = (((0,), (0,)), ((), ()))
DOT_NN = (((1,), (0,)), ((), ()))


def basis(cells):
    rows = np.arange(MODES)
    frequency = np.where(rows < MODES // 2, rows, rows - MODES // 2 + 1)
    phase = frequency[:, None] * np.arange(cells)[None, :] % cells
    angles = phase * (2.0 * math.pi / cells)
    return np.where((rows < MODES // 2)[:, None], np.cos(angles), np.sin(angles)).astype(np.float32)


def split(array):
    high = array.astype(jnp.bfloat16)
    low = (array - high.astype(np.float32)).astype(jnp.bfloat16)
    return high, low


def tables():
    phi_x, phi_y, phi_z = basis(NX), basis(NY), basis(NZ)
    high, low = split(phi_z)
    z_analysis = np.concatenate([high, low], 0)
    z_synthesis = np.concatenate([high, high, low], 0)
    lanes = np.repeat(phi_y.reshape(MODES, 32, BY), C, axis=2)
    y_table = lanes.transpose(1, 0, 2)
    x_table = phi_x.T.reshape(-1)
    return z_analysis, z_synthesis, np.ascontiguousarray(y_table), np.ascontiguousarray(x_table)


def dot(a, b, dims):
    return lax.dot_general(a, b, dims, preferred_element_type=f32)


def x_z_synthesise(cell, recv, px_ref, zs_ref):
    values = [recv[p].astype(f32) for p in range(MODES)]
    planes = []
    for i in range(BX):
        total = px_ref[(cell + i) * 16] * values[0]
        for p in range(1, MODES):
            total = total + px_ref[(cell + i) * 16 + p] * values[p]
        planes.append(total)
    total = jnp.concatenate(planes, axis=1)
    high = total.astype(bf16)
    low = (total - high.astype(f32)).astype(bf16)
    return dot(jnp.concatenate([high, low, high], axis=0), zs_ref[...], DOT_TN)


def kernel(
    x_hbm, ct_hbm, spec_hbm, w_hbm, bias_hbm, za_hbm, zs_hbm, py_hbm, px_hbm,
    out_ref, ig_ref, sg_ref, kr3,
    w_raw, bias_row, za_ref, zs_ref, py_ref, px_ref, wf_ref, wb_ref, bias_ref,
    xin, ctin, spec, flat, ct, acc, stk, dstk, dx, tbuf,
    sx, rx, sy, ry, sz, rz, ct_modes, coefs, mixed,
    sxb, rxb, syb, ryb, szb, rzb,
    ks1, kr1, ks2, kr2, ks3,
    oflat, flat2, by_input,
    ready, dma_sem, halo_s, halo_r, xs, xr, ys, yr, zs, zr, k1s, k1r, k2s, k2r, k3s, k3r,
):
    a, b = lax.axis_index("gx"), lax.axis_index("gy")
    h, q = b // 16, lax.rem(b, 16)
    g = 2 * a + h
    partner = (3 - b // 8) * 8 + lax.rem(b, 8)

    load_x = pltpu.make_async_copy(x_hbm, xin, dma_sem.at[0])
    load_x.start()

    def group_x(k):
        rank, other, core = k // 4, lax.rem(k // 2, 2), lax.rem(k, 2)
        steps = jnp.where(rank == 1, 3, jnp.where(rank == 0, 0, rank - 1))
        ta = 2 * lax.rem(a // 2 + steps, 4) + lax.rem(a + core, 2)
        th = lax.rem(h + other, 2)
        return 2 * ta + th, (ta, jnp.where(other == 0, b, partner))

    def group_y(k):
        rank, other = k // 2, lax.rem(k, 2)
        steps = jnp.where(lax.rem(rank, 2) == 1, (rank + 1) // 2, 8 - rank // 2)
        t = 8 * lax.rem(q // 8 + other, 2) + lax.rem(lax.rem(q, 8) + steps, 8)
        return t, (a, t + 16 * h)

    def each(members, action, count=15):
        def step(n, carry):
            action(count - n, *members(count - n))
            return carry

        lax.fori_loop(0, count, step, 0, unroll=True)

    def there(da, db):
        ok = None
        if da == 1:
            ok = a < 7
        if da == -1:
            ok = a > 0
        if db == 1:
            ok = (b < 31) if ok is None else ok & (b < 31)
        if db == -1:
            ok = (b > 0) if ok is None else ok & (b > 0)
        return ok

    barrier = pltpu.get_barrier_semaphore()

    def greet(k, t, peer):
        pl.semaphore_signal(barrier, inc=1, device_id=peer, device_id_type=MESH)

    each(group_x, greet)
    each(group_y, greet, 9)
    awaited = 24
    for da, db in NEIGHBOURS:
        if db == 0:
            continue

        @pl.when(there(da, db))
        def _():
            pl.semaphore_signal(barrier, inc=1, device_id=(a + da, b + db), device_id_type=MESH)

        awaited = awaited + jnp.where(there(da, db), 1, 0)

    load_ct = pltpu.make_async_copy(ct_hbm, ctin, dma_sem.at[1])
    load_spec = pltpu.make_async_copy(
        spec_hbm.at[:, :, pl.ds(pl.multiple_of(g * 256, 256), 256)], spec, dma_sem.at[2]
    )
    small = [
        pltpu.make_async_copy(src, dst, dma_sem.at[5 + n])
        for n, (src, dst) in enumerate(
            ((za_hbm, za_ref), (px_hbm, px_ref), (w_hbm, w_raw), (bias_hbm, bias_row), (zs_hbm, zs_ref), (py_hbm, py_ref))
        )
    ]
    for load in small:
        load.start()
    load_ct.start()
    load_spec.start()

    def x_copy(t, peer, src, buf, ssem, rsem):
        return pltpu.make_async_remote_copy(
            src_ref=src, dst_ref=buf.at[g], send_sem=ssem, recv_sem=rsem,
            device_id=peer, device_id_type=MESH,
        )

    def y_copy(t, peer, src, buf, ssem, rsem):
        return pltpu.make_async_remote_copy(
            src_ref=src, dst_ref=buf.at[q], send_sem=ssem, recv_sem=rsem,
            device_id=peer, device_id_type=MESH,
        )

    def all_of(buf, count, ssem, rsem):
        return pltpu.make_async_remote_copy(
            src_ref=buf.at[pl.ds(0, count)], dst_ref=buf.at[pl.ds(0, count)], send_sem=ssem, recv_sem=rsem,
            device_id=group_y(1)[1], device_id_type=MESH,
        )

    def halo_copy(index, field, n, da, db):
        sx_ = pl.ds(8, 1) if da == 1 else pl.ds(1, 1) if da == -1 else pl.ds(1, 8)
        dx_ = pl.ds(0, 1) if da == 1 else pl.ds(9, 1) if da == -1 else pl.ds(1, 8)
        sl = pl.ds(512, 128) if db == 1 else pl.ds(128, 128) if db == -1 else pl.ds(128, 512)
        dl = pl.ds(0, 128) if db == 1 else pl.ds(640, 128) if db == -1 else pl.ds(128, 512)
        return pltpu.make_async_remote_copy(
            src_ref=field.at[sx_, pl.ds(32, 32), sl], dst_ref=field.at[dx_, pl.ds(32, 32), dl],
            send_sem=halo_s.at[n, index], recv_sem=halo_r.at[n, index],
            device_id=(a + da, b + db), device_id_type=MESH,
        )

    def halo_start(field, n):
        for index, (da, db) in enumerate(NEIGHBOURS):

            @pl.when(there(da, db))
            def _():
                halo_copy(index, field, n, da, db).start()

    def halo_wait_recv(field, n):
        for index, (da, db) in enumerate(NEIGHBOURS):

            @pl.when(there(-da, -db))
            def _():
                halo_copy(index, field, n, da, db).wait_recv()

    def halo_wait_send(field, n):
        for index, (da, db) in enumerate(NEIGHBOURS):

            @pl.when(there(da, db))
            def _():
                halo_copy(index, field, n, da, db).wait_send()

    def zero_rim(field):
        @pl.when(a == 0)
        def _():
            field[0, 32:64, :] = jnp.zeros((C, WIDE), bf16)

        @pl.when(a == 7)
        def _():
            field[9, 32:64, :] = jnp.zeros((C, WIDE), bf16)

        @pl.when(b == 0)
        def _():
            for i in range(10):
                field[i, 32:64, 0:128] = jnp.zeros((C, NZ), bf16)

        @pl.when(b == 31)
        def _():
            for i in range(10):
                field[i, 32:64, 640:768] = jnp.zeros((C, NZ), bf16)

    def z_analyse(i, tiles):
        rows = jnp.concatenate(tiles, axis=0)
        both = dot(za_ref[...], rows, DOT_NT)
        tbuf[i] = both[:16] + both[16:]

    def x_partials(buf):
        rows = [tbuf[i] for i in range(BX)]

        def step(p, carry):
            total = px_ref[(a * 8) * 16 + p] * rows[0]
            for i in range(1, BX):
                total = total + px_ref[(a * 8 + i) * 16 + p] * rows[i]
            buf[p] = total
            return carry

        lax.fori_loop(0, 16, step, 0, unroll=4)

    def y_blocks(recv, send):
        for half in range(2):
            total = recv[half]
            for i in range(1, 8):
                total = total + recv[2 * i + half]
            send[half] = total.astype(bf16)

    def block_of(member, half):
        return 16 * half + jnp.where(h == half, member, lax.rem(member + 8, 16))

    def y_analyse(recv, n):
        def step(k, carry):
            result = list(carry)
            block = group_y(k)[0]
            for half in range(2):
                value = recv[block, half].astype(f32)
                place = block_of(block, half)
                for m in range(MODES):
                    result[m] = result[m] + value * py_ref[place, pl.ds(m, 1), :]
            return tuple(result)

        result = step(0, tuple(jnp.zeros((16, 128), f32) for _ in range(MODES)))
        for near, (low, high) in enumerate(Y_CLASSES):
            all_of(recv, high - low, ys.at[n], yr.at[n, near]).wait_recv()
            result = lax.fori_loop(low, high, step, result, unroll=True)
        return result

    def y_class(k):
        return jnp.where(k < 6, 0, jnp.where(k < 10, 1, jnp.where(k < 14, 2, 3)))

    def to_columns(parts, scale):
        wide = jnp.transpose(jnp.concatenate(parts, axis=0))
        return (wide[0:32] + wide[32:64] + wide[64:96] + wide[96:128]) * scale

    def y_synthesise(modes, scale, send):
        tall = jnp.transpose(jnp.concatenate([modes * scale] * 4, axis=0))
        for half in range(2):
            place = block_of(q, half)
            total = py_ref[place, pl.ds(0, 1), :] * tall[0:16]
            for m in range(1, MODES):
                total = total + py_ref[place, pl.ds(m, 1), :] * tall[16 * m : 16 * m + 16]
            send[half] = total.astype(send.dtype)

    lane = lax.broadcasted_iota(jnp.int32, (C, NZ), 1)

    def shift_rows(field, ones):
        def step(i, carry):
            for y in range(BY + 2):
                cells = slice(y * NZ, (y + 1) * NZ)
                value = field[i, 32:64, cells].astype(f32)
                before = jnp.where(lane == 0, 0.0, pltpu.roll(value, 1, 1))
                after = jnp.where(lane == NZ - 1, 0.0, pltpu.roll(value, NZ - 1, 1))
                field[i, 0:32, cells] = before.astype(bf16)
                field[i, 64:96, cells] = after.astype(bf16)
            return carry

        lax.fori_loop(0, 10, step, 0, unroll=2)

    def fill_ones(field):
        def step(i, carry):
            field[i, 96:128, :] = jnp.ones((32, WIDE), bf16)
            return carry

        lax.fori_loop(0, 10, step, 0)

    def convolve(field, weights, shift=None):
        def step(i, carry):
            total = None
            for d in range(3):
                for e in range(3):
                    tap = (d * 3 + e) * 128
                    part = dot(
                        weights[:, tap : tap + 128], field[i + d, :, e * NZ : e * NZ + LANES], DOT_NN
                    )
                    total = part if total is None else total + part
            acc[i] = total if shift is None else total + shift
            return carry

        lax.fori_loop(0, BX, step, 0, unroll=2)

    def unflatten(source, write):
        def step(c, carry):
            flat[pl.ds(pl.multiple_of(c * 32, 32), 32), :] = source[c].astype(f32)
            return carry

        lax.fori_loop(0, C, step, 0, unroll=8)

        def step2(i, carry):
            tiles = [flat[pl.ds(i * BY + y, C, stride=32), :] for y in range(BY)]
            write(i, tiles)
            return carry

        lax.fori_loop(0, BX, step2, 0, unroll=4)

    def flatten(source, target):
        def step(c, carry):
            target[c] = source[pl.ds(pl.multiple_of(c * 32, 32), 32), :].astype(bf16)
            return carry

        lax.fori_loop(0, C, step, 0, unroll=8)

    def prepare_weights():
        row = lax.broadcasted_iota(jnp.int32, (C, 128), 0)
        column = lax.broadcasted_iota(jnp.int32, (C, 128), 1)
        place = [jnp.where(column == row + 32 * f, 1.0, 0.0).astype(bf16) for f in range(3)]
        for tap in range(9):
            total, back_total = None, None
            for f in range(3):
                part = dot(w_raw[tap * 3 + f], place[f], DOT_NN)
                total = part if total is None else total + part
                part = dot(w_raw[(8 - tap) * 3 + 2 - f], place[f], DOT_TN)
                back_total = part if back_total is None else back_total + part
            wf_ref[:, tap * 128 : tap * 128 + 128] = total.astype(bf16)
            wb_ref[:, tap * 128 : tap * 128 + 128] = back_total.astype(bf16)
        spread = jnp.where(column[:, :C] == row[:, :C], jnp.broadcast_to(bias_row[...], (C, C)), 0.0)
        bias_ref[...] = jnp.broadcast_to(jnp.sum(spread, axis=1, keepdims=True), (C, 128))

    load_x.wait()
    small[0].wait()
    small[1].wait()

    def write_x(i, tiles):
        tiles = [t.astype(bf16) for t in tiles]
        for y in range(BY):
            stk[i + 1, 32:64, (y + 1) * NZ : (y + 2) * NZ] = tiles[y]
        z_analyse(i, tiles)

    unflatten(xin, write_x)
    x_partials(sx)
    pl.semaphore_wait(barrier, awaited)
    for k in (6, 8):
        pl.semaphore_signal(ready, inc=1, device_id=group_y(k)[1], device_id_type=MESH)
    each(group_x, lambda k, t, peer: x_copy(t, peer, sx.at[t], rx, xs.at[0], xr.at[0]).start())
    rx[g] = sx[g]
    halo_start(stk, 0)

    zero_rim(stk)
    fill_ones(stk)
    for load in small[2:]:
        load.wait()
    prepare_weights()
    load_ct.wait()

    def write_ct(i, tiles):
        for y in range(BY):
            ct[i, :, y * NZ : (y + 1) * NZ] = tiles[y]

    unflatten(ctin, write_ct)
    for i in (0, 1, 10, 11):
        dx[i] = jnp.zeros((C, LANES), bf16)

    all_of(rx, 15, xs.at[0], xr.at[0]).wait_recv()
    y_blocks(rx, sy)
    pl.semaphore_wait(ready, 2)
    each(group_y, lambda k, t, peer: y_copy(t, peer, sy, ry, ys.at[0], yr.at[0, y_class(k)]).start())
    ry[q] = sy[...]

    halo_wait_recv(stk, 0)
    shift_rows(stk, True)
    convolve(stk, wf_ref, jnp.concatenate([bias_ref[...]] * BY, axis=1))
    load_spec.wait()

    def widen(o, carry):
        for n in range(2):
            flat2[n, pl.ds(pl.multiple_of(o * 32, 32), 32), :] = spec[o, :, 128 * n : 128 * n + 128].astype(f32)
        return carry

    lax.fori_loop(0, C, widen, 0, unroll=4)

    def gather(c, carry):
        for n in range(2):
            by_input[c, :, 128 * n : 128 * n + 128] = flat2[n, pl.ds(c, C, stride=32), :]
        return carry

    lax.fori_loop(0, C, gather, 0, unroll=4)

    parts = y_analyse(ry, 0)
    for m in range(MODES):
        ct_modes[0, m] = parts[m]
    coefs[...] = to_columns(parts, GRID_SCALE)

    def mix(c, carry):
        return carry + by_input[c] * coefs[pl.ds(c, 1), :]

    y_synthesise(lax.fori_loop(0, C, mix, jnp.zeros((C, 256), f32), unroll=4), MODE_SCALE, sz)
    each(group_x, lambda k, t, peer: x_copy(t, peer, sz.at[lax.rem(t, 2)], rz, zs.at[0], zr.at[0]).start())
    rz[g] = sz[h]
    all_of(rz, 15, zs.at[0], zr.at[0]).wait_recv()

    root = math.sqrt(2.0 / math.pi)

    modes_all = x_z_synthesise(a * 8, rz, px_ref, zs_ref)

    def point(i):
        modes = modes_all[128 * i : 128 * i + 128]
        tiles = []
        for y in range(BY):
            cells = slice(y * NZ, (y + 1) * NZ)
            v = acc[i, :, cells] + modes[y * C : (y + 1) * C]
            square = v * v
            t = jnp.tanh(v * (square * (0.044715 * root) + root))
            half = 0.5 * t + 0.5
            slope = half * ((v * (square * (3 * 0.044715 * root) + root)) * (1.0 - t) + 1.0)
            acc[i, :, cells] = v * half
            delta = (ct[i, :, cells] * slope).astype(bf16)
            dstk[i + 1, 32:64, (y + 1) * NZ : (y + 2) * NZ] = delta
            dx[i + 2, :, cells] = delta
            tiles.append(delta)
        z_analyse(i, tiles)

    for i in range(BX):
        point(i)

    x_partials(sxb)
    each(group_x, lambda k, t, peer: x_copy(t, peer, sxb.at[t], rxb, xs.at[1], xr.at[1]).start())
    rxb[g] = sxb[g]

    def planes(cut):
        return jnp.concatenate([cut(i) for i in range(10)], axis=1)

    idle = jnp.zeros((C, LANES), bf16)
    shifted = [planes(lambda i, d=d: dx[i + 2 - d]) for d in range(3)] + [planes(lambda i: idle)]
    windows = [planes(lambda i, e=e: stk[i, : 112 if e == 1 else 96, e * NZ : e * NZ + LANES]) for e in range(3)]
    kgt = dot(jnp.concatenate(windows, axis=0), jnp.concatenate(shifted, axis=0), DOT_NT)
    empty = jnp.zeros((32, 128), f32)
    kgt = [
        jnp.concatenate([kgt[0:96], empty], axis=0),
        jnp.concatenate([kgt[96:208], empty[:16]], axis=0),
        jnp.concatenate([kgt[208:304], empty], axis=0),
    ]
    columns = [jnp.transpose(kgt[e]) for e in range(3)]
    kgp = [columns[e][32 * d : 32 * d + 32] for e in range(3) for d in range(3)]

    for n in range(7):
        block = kgp[n]
        if n < 6:
            block = jnp.where(lane >= 96, pltpu.roll(kgp[7 + n // 3], 96 - 32 * (n % 3), 1), block)
        else:
            block = jnp.where(lane >= 96, kgp[4], block)
        ks1[n] = block.astype(bf16)
    def share_of(t):
        return t // 2 + lax.rem(t, 2), (lax.rem(t // 2, 2) == 0) & (t // 2 + lax.rem(t, 2) < KG_SHARES)

    share, holds = share_of(g)

    def k1_start(k, t, peer):
        target, takes = share_of(t)

        @pl.when(takes)
        def _():
            x_copy(t, peer, ks1.at[target], kr1, k1s, k1r).start()

    each(group_x, k1_start)

    halo_start(dstk, 1)

    zero_rim(dstk)
    fill_ones(dstk)
    def spread(i, carry):
        for y in range(BY):
            oflat[pl.ds(i * BY + y, C, stride=32), :] = acc[i, :, y * NZ : (y + 1) * NZ]
        return carry

    lax.fori_loop(0, BX, spread, 0, unroll=4)
    flatten(oflat, out_ref)

    all_of(rxb, 15, xs.at[1], xr.at[1]).wait_recv()
    y_blocks(rxb, syb)
    each(group_y, lambda k, t, peer: y_copy(t, peer, syb, ryb, ys.at[1], yr.at[1, y_class(k)]).start())
    ryb[q] = syb[...]

    @pl.when(holds)
    def _():
        all_of(kr1, 15, k1s, k1r).wait_recv()
        kr1[g] = ks1[share]
        total = kr1[0].astype(f32)
        for i in range(1, 16):
            total = total + kr1[i].astype(f32)
        ks2[...] = total.astype(bf16)
        kr2[q] = total.astype(bf16)
        each(group_y, lambda k, t, peer: y_copy(t, peer, ks2, kr2, k2s, k2r).start())

    halo_wait_recv(dstk, 1)
    shift_rows(dstk, False)
    convolve(dstk, wb_ref)

    parts = y_analyse(ryb, 1)
    for m in range(MODES):
        ct_modes[1, m] = parts[m]
    mixed[...] = to_columns(parts, MODE_SCALE)

    def mix_back(o, carry):
        return carry + spec[o].astype(f32) * mixed[pl.ds(o, 1), :]

    back = lax.fori_loop(0, C, mix_back, jnp.zeros((C, 256), f32), unroll=4)
    y_synthesise(back, GRID_SCALE, szb)
    each(group_x, lambda k, t, peer: x_copy(t, peer, szb.at[lax.rem(t, 2)], rzb, zs.at[1], zr.at[1]).start())
    rzb[g] = szb[h]

    def share_copy(peer):
        return pltpu.make_async_remote_copy(
            src_ref=ks3, dst_ref=kr3.at[share], send_sem=k3s, recv_sem=k3r, device_id=peer, device_id_type=MESH
        )

    @pl.when(holds)
    def _():
        all_of(kr2, 15, k2s, k2r).wait_recv()
        total = kr2[0].astype(f32)
        for i in range(1, 16):
            total = total + kr2[i].astype(f32)
        total = total * GRID_SCALE
        ks3[...] = total.astype(bf16)
        kr3[share] = total.astype(bf16)
        each(group_x, lambda k, t, peer: share_copy(peer).start())

    coef_rows = ct_modes[0, q]
    coef_rows = coef_rows + pltpu.roll(coef_rows, 64, 1)
    coef_rows = (coef_rows + pltpu.roll(coef_rows, 32, 1)) * GRID_SCALE
    wide = jnp.transpose(ct_modes[1, q])
    back_columns = jnp.transpose(wide[0:32] + wide[32:64] + wide[64:96] + wide[96:128]) * MODE_SCALE
    for o in range(C):
        sg_ref[o] = (coef_rows * back_columns[:, o : o + 1])[:, 0:32]

    all_of(rzb, 15, zs.at[1], zr.at[1]).wait_recv()
    modes_all = x_z_synthesise(a * 8, rzb, px_ref, zs_ref)

    def last(i):
        modes = modes_all[128 * i : 128 * i + 128]
        for y in range(BY):
            cells = slice(y * NZ, (y + 1) * NZ)
            oflat[pl.ds(i * BY + y, C, stride=32), :] = acc[i, :, cells] + modes[y * C : (y + 1) * C]

    for i in range(BX):
        last(i)
    flatten(oflat, ig_ref)

    for n in range(2):
        all_of((rx, rxb)[n], 15, xs.at[n], xr.at[n]).wait_send()
        all_of((rz, rzb)[n], 15, zs.at[n], zr.at[n]).wait_send()
        all_of((ry, ryb)[n], 15, ys.at[n], yr.at[n, 0]).wait_send()
    halo_wait_send(stk, 0)
    halo_wait_send(dstk, 1)
    def in_shares(has, has_not):
        pl.when(holds)(has)
        pl.when(jnp.logical_not(holds))(has_not)

    in_shares(
        lambda: all_of(kr1, KG_SHARES - 1, k1s, k1r).wait_send(),
        lambda: all_of(kr1, KG_SHARES, k1s, k1r).wait_send(),
    )

    @pl.when(holds)
    def _():
        all_of(kr2, 15, k2s, k2r).wait_send()
        all_of(kr1, 15, k3s, k3r).wait_send()

    in_shares(
        lambda: all_of(kr3, KG_SHARES - 1, k3s, k3r).wait_recv(),
        lambda: all_of(kr3, KG_SHARES, k3s, k3r).wait_recv(),
    )


def finish(kr, ig, out, sg, out_hbm, ig_hbm, sg_hbm, kg_hbm, bg_hbm, kg, bg, store_sem):
    pairs = ((ig, ig_hbm), (out, out_hbm), (sg, sg_hbm), (bg, bg_hbm), (kg, kg_hbm))
    stores = [pltpu.make_async_copy(src, dst, store_sem.at[n]) for n, (src, dst) in enumerate(pairs)]
    for store in stores[:3]:
        store.start()
    blocks = [kr[n].astype(f32) for n in range(KG_SHARES)]
    bg[...] = jnp.transpose(blocks[6])[96:97, :]
    stores[3].start()
    for d in range(3):
        for e in range(3):
            for f in range(3):
                n, offset = e * 3 + d, 32 * f
                if n >= 7:
                    n, offset = (n - 7) * 3 + f, 96
                moved = blocks[n] if offset == 0 else pltpu.roll(blocks[n], 128 - offset, 1)
                kg[(d * 3 + e) * 3 + f] = moved[:, 0:32]
    stores[4].start()
    for store in stores:
        store.wait()


def layer(inputs, cotangent, weights, channel_bias, spectral):
    z_analysis, z_synthesis, y_table, x_table = tables()
    x = inputs.reshape(C, BX * BY, NZ)
    ct = cotangent.reshape(C, BX * BY, NZ)
    any_space = pl.BlockSpec(memory_space=pl.ANY)
    vmem = pl.BlockSpec(memory_space=pltpu.VMEM)
    dma = pltpu.SemaphoreType.DMA
    V = pltpu.VMEM
    mode_bufs = [
        V((16, 16, 128), f32), V((16, 16, 128), f32),
        V((2, 16, 128), bf16), V((16, 2, 16, 128), bf16),
        V((2, 16, 128), bf16), V((16, 16, 128), bf16),
    ]
    block = (C, BX * BY, NZ)
    operands = (
        x, ct, spectral, weights.reshape(27, C, C), channel_bias.reshape(1, C),
        z_analysis, z_synthesis, y_table, x_table,
    )
    results = pl.pallas_call(
        kernel,
        out_shape=(V(block, bf16), V(block, bf16), V((C, 16, C), f32), V((KG_SHARES, KG_ROWS, 128), bf16)),
        in_specs=[pl.BlockSpec(memory_space=pltpu.HBM)] * 9,
        out_specs=(vmem,) * 4,
        scratch_shapes=[
            V((27, C, C), bf16), V((1, C), f32), V((32, 128), bf16), V((48, 128), bf16),
            V((32, MODES, 128), f32), pltpu.SMEM((NX * MODES,), f32),
            V((C, 1152), bf16), V((C, 1152), bf16), V((C, 128), f32),
            V((C, 32, NZ), bf16), V((C, 32, NZ), bf16), V((C, C, 256), bf16),
            V((C * 32, NZ), f32), V((BX, C, LANES), f32), V((BX, C, LANES), f32),
            V((10, 128, WIDE), bf16), V((10, 128, WIDE), bf16), V((12, C, LANES), bf16),
            V((BX, 16, 128), f32),
            *mode_bufs,
            V((2, MODES, 16, 128), f32), V((C, 256), f32), V((C, 256), f32),

            *mode_bufs,
            V((KG_SHARES, KG_ROWS, 128), bf16), V((16, KG_ROWS, 128), bf16),
            V((KG_ROWS, 128), bf16), V((16, KG_ROWS, 128), bf16),
            V((KG_ROWS, 128), bf16),
            V((C * 32, NZ), f32), V((2, C * C, 128), f32), V((C, C, 256), f32),
            pltpu.SemaphoreType.REGULAR, dma((11,)), dma((2, 8)), dma((2, 8)),
            *[dma((2,))] * 3, dma((2, 4)), *[dma((2,))] * 2,
            *[dma] * 6,
        ],
        compiler_params=pltpu.CompilerParams(
            collective_id=0, has_side_effects=True, vmem_limit_bytes=40 * 2**20
        ),
        cost_estimate=pl.CostEstimate(flops=700_000_000, bytes_accessed=4_000_000, transcendentals=131072),
    )(*[pltpu.with_memory_space_constraint(jnp.asarray(operand), pltpu.HBM) for operand in operands])
    outputs, input_grad, spectral_grad, shares = [
        pltpu.with_memory_space_constraint(result, pltpu.VMEM) for result in results
    ]
    outputs, input_grad, spectral_grad, kernel_grad, bias_grad = pl.pallas_call(
        finish,
        out_shape=(
            jax.ShapeDtypeStruct(block, bf16),
            jax.ShapeDtypeStruct(block, bf16),
            jax.ShapeDtypeStruct((C, 16, C), f32),
            jax.ShapeDtypeStruct((27, C, C), f32),
            jax.ShapeDtypeStruct((1, C), f32),
        ),
        in_specs=[vmem] * 4,
        out_specs=(any_space,) * 5,
        scratch_shapes=[
            V((27, C, C), f32), V((1, C), f32), dma((5,)),
        ],
        compiler_params=pltpu.CompilerParams(vmem_limit_bytes=16 * 2**20),
    )(shares, input_grad, outputs, spectral_grad)
    field = (C, BX, BY, NZ)
    return (
        outputs.reshape(field), input_grad.reshape(field), spectral_grad.transpose(0, 2, 1),
        kernel_grad.reshape(3, 3, 3, C, C), bias_grad.reshape(C),
    )


def solution(mesh):
    placed = (P(None, "gx", "gy", None), P(None, "gx", "gy", None), P(), P(), P())
    return jax.shard_map(
        layer,
        mesh=mesh,
        in_specs=placed,
        out_specs=(
            P(None, "gx", "gy", None),
            P(None, "gx", "gy", None),
            P(None, None, ("gx", "gy")),
            P(),
            P(),
        ),
        check_vma=False,
    )
```

```python
import functools
import math

import jax
import jax.numpy as jnp
import numpy as np
from jax import lax
from jax.experimental import pallas as pl
from jax.experimental.pallas import tpu as pltpu
from jax.sharding import PartitionSpec as P

MESH = pl.DeviceIdType.MESH
MODES = 16
C = 32
BX, BY, NZ = 8, 4, 128
NX, NY = 64, 128
LANES = BY * NZ
WIDE = (BY + 2) * NZ
NEIGHBOURS = [(i, j) for i in (-1, 0, 1) for j in (-1, 0, 1) if (i, j) != (0, 0)]
GRID_SCALE = 1.0 / math.sqrt(NX * NY * NZ)
MODE_SCALE = 1.0 / math.sqrt(MODES**3)
Y_CLASSES = ((1, 6), (6, 10), (10, 14), (14, 16))
KG_ROWS = 32
KG_SHARES = 7
f32, bf16 = jnp.float32, jnp.bfloat16
DOT_NT = (((1,), (1,)), ((), ()))
DOT_TN = (((0,), (0,)), ((), ()))
DOT_NN = (((1,), (0,)), ((), ()))


def basis(cells):
    rows = np.arange(MODES)
    frequency = np.where(rows < MODES // 2, rows, rows - MODES // 2 + 1)
    phase = frequency[:, None] * np.arange(cells)[None, :] % cells
    angles = phase * (2.0 * math.pi / cells)
    return np.where((rows < MODES // 2)[:, None], np.cos(angles), np.sin(angles)).astype(np.float32)


def split(array):
    high = array.astype(jnp.bfloat16)
    low = (array - high.astype(np.float32)).astype(jnp.bfloat16)
    return high, low


def tables():
    phi_x, phi_y, phi_z = basis(NX), basis(NY), basis(NZ)
    high, low = split(phi_z)
    z_analysis = np.concatenate([high, low], 0)
    z_synthesis = np.concatenate([high, high, low], 0)
    lanes = np.repeat(phi_y.reshape(MODES, 32, BY), C, axis=2)
    y_table = lanes.transpose(1, 0, 2)
    y_table_back = y_table.reshape(32, MODES, BY, C).transpose(0, 1, 3, 2).reshape(32, MODES, BY * C)
    x_table = phi_x.T.reshape(-1)
    y_scale = np.exp2(np.arange(NY) * 0.6180339887 % 1.0).reshape(32, BY)
    x_scale = np.exp2(np.arange(8 * BY) * 0.6180339887 % 1.0).reshape(8, BY)
    scales = np.repeat(np.concatenate([y_scale, x_scale, 1.0 / x_scale]), C, axis=1).astype(np.float32)
    y_analysis = (y_table / np.repeat(y_scale, C, axis=1)[:, None, :]).astype(np.float32)
    return z_analysis, z_synthesis, np.ascontiguousarray(y_table), np.ascontiguousarray(y_table_back), np.ascontiguousarray(x_table), scales, y_analysis


def dot(a, b, dims):
    return lax.dot_general(a, b, dims, preferred_element_type=f32)


def x_z_synthesise(cell, recv, px_ref, zs_ref):
    values = [recv[p].astype(f32) for p in range(MODES)]
    planes = []
    for i in range(BX):
        total = px_ref[(cell + i) * 16] * values[0]
        for p in range(1, MODES):
            total = total + px_ref[(cell + i) * 16 + p] * values[p]
        planes.append(total)
    total = jnp.concatenate(planes, axis=1)
    high = total.astype(bf16)
    low = (total - high.astype(f32)).astype(bf16)
    return dot(jnp.concatenate([high, low, high], axis=0), zs_ref[...], DOT_TN)


def kernel(
    x_hbm, ct_hbm, spec_hbm, w_hbm, bias_hbm, za_hbm, zs_hbm, py_hbm, px_hbm, pb_hbm, sc_hbm, pa_hbm,
    out_ref, ig_ref, sg_ref, kr3,
    w_raw, bias_row, za_ref, zs_ref, py_ref, px_ref, pb_ref, sc_ref, pa_ref, wide_ref, wf_ref, wb_ref, bias_ref,
    xin, ctin, spec, flat, ct, acc, stk, dstk, dx, tbuf,
    sx, rx, sy, ry, sz, rz, ct_modes, coefs, mixed,
    sxb, rxb, syb, ryb, szb, rzb,
    ks1, kr1, ks2, kr2, ks3,
    oflat, flat2, by_input,
    ready, dma_sem, halo_s, halo_r, xs, xr, ys, yr, zs, zr, k1s, k1r, k2s, k2r, k3s, k3r,
):
    a, b = lax.axis_index("gx"), lax.axis_index("gy")
    h, q = b // 16, lax.rem(b, 16)
    g = 2 * a + h
    partner = (3 - b // 8) * 8 + lax.rem(b, 8)

    load_x = pltpu.make_async_copy(x_hbm, xin, dma_sem.at[0])
    load_x.start()

    def group_x(k):
        rank, other, core = k // 4, lax.rem(k // 2, 2), lax.rem(k, 2)
        steps = jnp.where(rank == 1, 3, jnp.where(rank == 0, 0, rank - 1))
        ta = 2 * lax.rem(a // 2 + steps, 4) + lax.rem(a + core, 2)
        th = lax.rem(h + other, 2)
        return 2 * ta + th, (ta, jnp.where(other == 0, b, partner))

    def group_y(k):
        rank, other = k // 2, lax.rem(k, 2)
        steps = jnp.where(lax.rem(rank, 2) == 1, (rank + 1) // 2, 8 - rank // 2)
        t = 8 * lax.rem(q // 8 + other, 2) + lax.rem(lax.rem(q, 8) + steps, 8)
        return t, (a, t + 16 * h)

    def each(members, action, count=15):
        def step(n, carry):
            action(count - n, *members(count - n))
            return carry

        lax.fori_loop(0, count, step, 0, unroll=True)

    def there(da, db):
        ok = None
        if da == 1:
            ok = a < 7
        if da == -1:
            ok = a > 0
        if db == 1:
            ok = (b < 31) if ok is None else ok & (b < 31)
        if db == -1:
            ok = (b > 0) if ok is None else ok & (b > 0)
        return ok

    barrier = pltpu.get_barrier_semaphore()

    def greet(k, t, peer):
        pl.semaphore_signal(barrier, inc=1, device_id=peer, device_id_type=MESH)

    each(group_x, greet)
    each(group_y, greet, 9)
    awaited = 24
    for da, db in NEIGHBOURS:
        if db == 0:
            continue

        @pl.when(there(da, db))
        def _():
            pl.semaphore_signal(barrier, inc=1, device_id=(a + da, b + db), device_id_type=MESH)

        awaited = awaited + jnp.where(there(da, db), 1, 0)

    load_ct = pltpu.make_async_copy(ct_hbm, ctin, dma_sem.at[1])
    load_spec = pltpu.make_async_copy(
        spec_hbm.at[:, :, pl.ds(pl.multiple_of(g * 256, 256), 256)], spec, dma_sem.at[2]
    )
    small = [
        pltpu.make_async_copy(src, dst, dma_sem.at[5 + n])
        for n, (src, dst) in enumerate(
            ((za_hbm, za_ref), (px_hbm, px_ref), (sc_hbm, sc_ref), (pa_hbm, pa_ref), (w_hbm, w_raw), (bias_hbm, bias_row), (zs_hbm, zs_ref), (py_hbm, py_ref), (pb_hbm, pb_ref))
        )
    ]
    for load in small:
        load.start()
    load_ct.start()
    load_spec.start()

    def x_copy(t, peer, src, buf, ssem, rsem):
        return pltpu.make_async_remote_copy(
            src_ref=src, dst_ref=buf.at[g], send_sem=ssem, recv_sem=rsem,
            device_id=peer, device_id_type=MESH,
        )

    def y_copy(t, peer, src, buf, ssem, rsem):
        return pltpu.make_async_remote_copy(
            src_ref=src, dst_ref=buf.at[q], send_sem=ssem, recv_sem=rsem,
            device_id=peer, device_id_type=MESH,
        )

    def all_of(buf, count, ssem, rsem):
        return pltpu.make_async_remote_copy(
            src_ref=buf.at[pl.ds(0, count)], dst_ref=buf.at[pl.ds(0, count)], send_sem=ssem, recv_sem=rsem,
            device_id=group_y(1)[1], device_id_type=MESH,
        )

    def halo_copy(index, field, n, da, db):
        sx_ = pl.ds(8, 1) if da == 1 else pl.ds(1, 1) if da == -1 else pl.ds(1, 8)
        dx_ = pl.ds(0, 1) if da == 1 else pl.ds(9, 1) if da == -1 else pl.ds(1, 8)
        sl = pl.ds(512, 128) if db == 1 else pl.ds(128, 128) if db == -1 else pl.ds(128, 512)
        dl = pl.ds(0, 128) if db == 1 else pl.ds(640, 128) if db == -1 else pl.ds(128, 512)
        return pltpu.make_async_remote_copy(
            src_ref=field.at[sx_, pl.ds(32, 32), sl], dst_ref=field.at[dx_, pl.ds(32, 32), dl],
            send_sem=halo_s.at[n, index], recv_sem=halo_r.at[n, index],
            device_id=(a + da, b + db), device_id_type=MESH,
        )

    def halo_start(field, n):
        for index, (da, db) in enumerate(NEIGHBOURS):

            @pl.when(there(da, db))
            def _():
                halo_copy(index, field, n, da, db).start()

    def halo_wait_recv(field, n):
        for index, (da, db) in enumerate(NEIGHBOURS):

            @pl.when(there(-da, -db))
            def _():
                halo_copy(index, field, n, da, db).wait_recv()

    def halo_wait_send(field, n):
        for index, (da, db) in enumerate(NEIGHBOURS):

            @pl.when(there(da, db))
            def _():
                halo_copy(index, field, n, da, db).wait_send()

    def zero_rim(field):
        @pl.when(a == 0)
        def _():
            field[0, 32:64, :] = jnp.zeros((C, WIDE), bf16)

        @pl.when(a == 7)
        def _():
            field[9, 32:64, :] = jnp.zeros((C, WIDE), bf16)

        @pl.when(b == 0)
        def _():
            for i in range(10):
                field[i, 32:64, 0:128] = jnp.zeros((C, NZ), bf16)

        @pl.when(b == 31)
        def _():
            for i in range(10):
                field[i, 32:64, 640:768] = jnp.zeros((C, NZ), bf16)

    def z_analyse(i, tiles):
        rows = jnp.concatenate(tiles, axis=0)
        both = dot(za_ref[...], rows, DOT_NT)
        tbuf[i] = both[:16] + both[16:]

    def x_partials(buf):
        rows = [tbuf[i] for i in range(BX)]

        def step(p, carry):
            total = px_ref[(a * 8) * 16 + p] * rows[0]
            for i in range(1, BX):
                total = total + px_ref[(a * 8 + i) * 16 + p] * rows[i]
            buf[p] = (total * sc_ref[pl.ds(32 + a, 1), :]).astype(bf16)
            return carry

        lax.fori_loop(0, 16, step, 0, unroll=4)

    def y_blocks(recv, send):
        for half in range(2):
            total = recv[half].astype(f32) * sc_ref[40:41, :]
            for i in range(1, 8):
                total = total + recv[2 * i + half].astype(f32) * sc_ref[40 + i : 41 + i, :]
            send[half] = (total * sc_ref[pl.ds(block_of(q, half), 1), :]).astype(bf16)

    def block_of(member, half):
        return 16 * half + jnp.where(h == half, member, lax.rem(member + 8, 16))

    def y_analyse(recv, n):
        def step(k, carry):
            result = list(carry)
            block = group_y(k)[0]
            for half in range(2):
                value = recv[block, half].astype(f32)
                place = block_of(block, half)
                for m in range(MODES):
                    result[m] = result[m] + value * pa_ref[place, pl.ds(m, 1), :]
            return tuple(result)

        result = step(0, tuple(jnp.zeros((16, 128), f32) for _ in range(MODES)))
        for near, (low, high) in enumerate(Y_CLASSES):
            all_of(recv, high - low, ys.at[n], yr.at[n, near]).wait_recv()
            result = lax.fori_loop(low, high, step, result, unroll=True)
        return result

    def y_class(k):
        return jnp.where(k < 6, 0, jnp.where(k < 10, 1, jnp.where(k < 14, 2, 3)))

    def to_columns(parts, scale):
        wide = jnp.transpose(jnp.concatenate(parts, axis=0))
        return (wide[0:32] + wide[32:64] + wide[64:96] + wide[96:128]) * scale

    def y_synthesise(modes, scale, send):
        y_project(jnp.transpose(jnp.concatenate([modes * scale] * 4, axis=0)), py_ref, send)

    def y_synthesise_back(modes, scale, send):
        for n in range(2):
            for j in range(BY):
                wide_ref[n, pl.ds(j, C, stride=BY), :] = modes[:, 128 * n : 128 * n + 128] * scale
        tall = jnp.concatenate([jnp.transpose(wide_ref[n]) for n in range(2)], axis=0)
        y_project(tall, pb_ref, send)

    def y_project(tall, table, send):
        for half in range(2):
            place = block_of(q, half)
            total = table[place, pl.ds(0, 1), :] * tall[0:16]
            for m in range(1, MODES):
                total = total + table[place, pl.ds(m, 1), :] * tall[16 * m : 16 * m + 16]
            send[half] = total.astype(send.dtype)

    lane = lax.broadcasted_iota(jnp.int32, (C, NZ), 1)

    def shift_rows(field, ones):
        def step(i, carry):
            for y in range(BY + 2):
                cells = slice(y * NZ, (y + 1) * NZ)
                value = field[i, 32:64, cells].astype(f32)
                before = jnp.where(lane == 0, 0.0, pltpu.roll(value, 1, 1))
                after = jnp.where(lane == NZ - 1, 0.0, pltpu.roll(value, NZ - 1, 1))
                field[i, 0:32, cells] = before.astype(bf16)
                field[i, 64:96, cells] = after.astype(bf16)
            return carry

        lax.fori_loop(0, 10, step, 0, unroll=2)

    def fill_ones(field):
        def step(i, carry):
            field[i, 96:128, :] = jnp.ones((32, WIDE), bf16)
            return carry

        lax.fori_loop(0, 10, step, 0)

    def convolve(field, weights, shift=None):
        def step(i, carry):
            total = None
            for d in range(3):
                for e in range(3):
                    tap = (d * 3 + e) * 128
                    part = dot(
                        weights[:, tap : tap + 128], field[i + d, :, e * NZ : e * NZ + LANES], DOT_NN
                    )
                    total = part if total is None else total + part
            acc[i] = total if shift is None else total + shift
            return carry

        lax.fori_loop(0, BX, step, 0, unroll=2)

    def unflatten(source, write):
        def step(c, carry):
            flat[pl.ds(pl.multiple_of(c * 32, 32), 32), :] = source[c].astype(f32)
            return carry

        lax.fori_loop(0, C, step, 0, unroll=8)

        def step2(i, carry):
            tiles = [flat[pl.ds(i * BY + y, C, stride=32), :] for y in range(BY)]
            write(i, tiles)
            return carry

        lax.fori_loop(0, BX, step2, 0, unroll=4)

    def flatten(source, target):
        def step(c, carry):
            target[c] = source[pl.ds(pl.multiple_of(c * 32, 32), 32), :].astype(bf16)
            return carry

        lax.fori_loop(0, C, step, 0, unroll=8)

    def prepare_weights():
        row = lax.broadcasted_iota(jnp.int32, (C, 128), 0)
        column = lax.broadcasted_iota(jnp.int32, (C, 128), 1)
        place = [jnp.where(column == row + 32 * f, 1.0, 0.0).astype(bf16) for f in range(3)]
        for tap in range(9):
            total, back_total = None, None
            for f in range(3):
                part = dot(w_raw[tap * 3 + f], place[f], DOT_NN)
                total = part if total is None else total + part
                part = dot(w_raw[(8 - tap) * 3 + 2 - f], place[f], DOT_TN)
                back_total = part if back_total is None else back_total + part
            wf_ref[:, tap * 128 : tap * 128 + 128] = total.astype(bf16)
            wb_ref[:, tap * 128 : tap * 128 + 128] = back_total.astype(bf16)
        spread = jnp.where(column[:, :C] == row[:, :C], jnp.broadcast_to(bias_row[...], (C, C)), 0.0)
        bias_ref[...] = jnp.broadcast_to(jnp.sum(spread, axis=1, keepdims=True), (C, 128))

    load_x.wait()
    small[0].wait()
    small[1].wait()
    small[2].wait()

    def write_x(i, tiles):
        tiles = [t.astype(bf16) for t in tiles]
        for y in range(BY):
            stk[i + 1, 32:64, (y + 1) * NZ : (y + 2) * NZ] = tiles[y]
        z_analyse(i, tiles)

    unflatten(xin, write_x)
    x_partials(sx)
    pl.semaphore_wait(barrier, awaited)
    for k in (6, 8):
        pl.semaphore_signal(ready, inc=1, device_id=group_y(k)[1], device_id_type=MESH)
    each(group_x, lambda k, t, peer: x_copy(t, peer, sx.at[t], rx, xs.at[0], xr.at[0]).start())
    rx[g] = sx[g]
    halo_start(stk, 0)

    zero_rim(stk)
    fill_ones(stk)
    for load in small[3:]:
        load.wait()
    prepare_weights()
    load_ct.wait()

    def write_ct(i, tiles):
        for y in range(BY):
            ct[i, :, y * NZ : (y + 1) * NZ] = tiles[y]

    unflatten(ctin, write_ct)
    for i in (0, 1, 10, 11):
        dx[i] = jnp.zeros((C, LANES), bf16)

    all_of(rx, 15, xs.at[0], xr.at[0]).wait_recv()
    y_blocks(rx, sy)
    pl.semaphore_wait(ready, 2)
    each(group_y, lambda k, t, peer: y_copy(t, peer, sy, ry, ys.at[0], yr.at[0, y_class(k)]).start())
    ry[q] = sy[...]

    halo_wait_recv(stk, 0)
    shift_rows(stk, True)
    convolve(stk, wf_ref, jnp.concatenate([bias_ref[...]] * BY, axis=1))
    load_spec.wait()

    def widen(o, carry):
        for n in range(2):
            flat2[n, pl.ds(pl.multiple_of(o * 32, 32), 32), :] = spec[o, :, 128 * n : 128 * n + 128].astype(f32)
        return carry

    lax.fori_loop(0, C, widen, 0, unroll=4)

    def gather(c, carry):
        for n in range(2):
            by_input[c, :, 128 * n : 128 * n + 128] = flat2[n, pl.ds(c, C, stride=32), :]
        return carry

    lax.fori_loop(0, C, gather, 0, unroll=4)

    parts = y_analyse(ry, 0)
    for m in range(MODES):
        ct_modes[0, m] = parts[m]
    coefs[...] = to_columns(parts, GRID_SCALE)

    def mix(c, carry):
        return carry + by_input[c] * coefs[pl.ds(c, 1), :]

    y_synthesise(lax.fori_loop(0, C, mix, jnp.zeros((C, 256), f32), unroll=4), MODE_SCALE, sz)
    each(group_x, lambda k, t, peer: x_copy(t, peer, sz.at[lax.rem(t, 2)], rz, zs.at[0], zr.at[0]).start())
    rz[g] = sz[h]
    all_of(rz, 15, zs.at[0], zr.at[0]).wait_recv()

    root = math.sqrt(2.0 / math.pi)

    modes_all = x_z_synthesise(a * 8, rz, px_ref, zs_ref)

    def point(i):
        modes = modes_all[128 * i : 128 * i + 128]
        tiles = []
        for y in range(BY):
            cells = slice(y * NZ, (y + 1) * NZ)
            v = acc[i, :, cells] + modes[y * C : (y + 1) * C]
            square = v * v
            t = jnp.tanh(v * (square * (0.044715 * root) + root))
            half = 0.5 * t + 0.5
            slope = half * ((v * (square * (3 * 0.044715 * root) + root)) * (1.0 - t) + 1.0)
            acc[i, :, cells] = v * half
            delta = (ct[i, :, cells] * slope).astype(bf16)
            dstk[i + 1, 32:64, (y + 1) * NZ : (y + 2) * NZ] = delta
            dx[i + 2, :, cells] = delta
            tiles.append(delta)
        z_analyse(i, tiles)

    for i in range(BX):
        point(i)

    x_partials(sxb)
    each(group_x, lambda k, t, peer: x_copy(t, peer, sxb.at[t], rxb, xs.at[1], xr.at[1]).start())
    rxb[g] = sxb[g]

    def planes(cut):
        return jnp.concatenate([cut(i) for i in range(10)], axis=1)

    idle = jnp.zeros((C, LANES), bf16)
    shifted = [planes(lambda i, d=d: dx[i + 2 - d]) for d in range(3)] + [planes(lambda i: idle)]
    windows = [planes(lambda i, e=e: stk[i, : 112 if e == 1 else 96, e * NZ : e * NZ + LANES]) for e in range(3)]
    kgt = dot(jnp.concatenate(windows, axis=0), jnp.concatenate(shifted, axis=0), DOT_NT)
    empty = jnp.zeros((32, 128), f32)
    kgt = [
        jnp.concatenate([kgt[0:96], empty], axis=0),
        jnp.concatenate([kgt[96:208], empty[:16]], axis=0),
        jnp.concatenate([kgt[208:304], empty], axis=0),
    ]
    columns = [jnp.transpose(kgt[e]) for e in range(3)]
    kgp = [columns[e][32 * d : 32 * d + 32] for e in range(3) for d in range(3)]

    for n in range(7):
        block = kgp[n]
        if n < 6:
            block = jnp.where(lane >= 96, pltpu.roll(kgp[7 + n // 3], 96 - 32 * (n % 3), 1), block)
        else:
            block = jnp.where(lane >= 96, kgp[4], block)
        ks1[n] = block.astype(bf16)
    def share_of(t):
        return t // 2 + lax.rem(t, 2), (lax.rem(t // 2, 2) == 0) & (t // 2 + lax.rem(t, 2) < KG_SHARES)

    share, holds = share_of(g)

    def k1_start(k, t, peer):
        target, takes = share_of(t)

        @pl.when(takes)
        def _():
            x_copy(t, peer, ks1.at[target], kr1, k1s, k1r).start()

    each(group_x, k1_start)

    halo_start(dstk, 1)

    zero_rim(dstk)
    fill_ones(dstk)
    def spread(i, carry):
        for y in range(BY):
            oflat[pl.ds(i * BY + y, C, stride=32), :] = acc[i, :, y * NZ : (y + 1) * NZ]
        return carry

    lax.fori_loop(0, BX, spread, 0, unroll=4)
    flatten(oflat, out_ref)

    all_of(rxb, 15, xs.at[1], xr.at[1]).wait_recv()
    y_blocks(rxb, syb)
    each(group_y, lambda k, t, peer: y_copy(t, peer, syb, ryb, ys.at[1], yr.at[1, y_class(k)]).start())
    ryb[q] = syb[...]

    @pl.when(holds)
    def _():
        all_of(kr1, 15, k1s, k1r).wait_recv()
        kr1[g] = ks1[share]
        total = kr1[0].astype(f32)
        for i in range(1, 16):
            total = total + kr1[i].astype(f32)
        ks2[...] = total.astype(bf16)
        kr2[q] = total.astype(bf16)
        each(group_y, lambda k, t, peer: y_copy(t, peer, ks2, kr2, k2s, k2r).start())

    halo_wait_recv(dstk, 1)
    shift_rows(dstk, False)
    convolve(dstk, wb_ref)

    parts = y_analyse(ryb, 1)
    for m in range(MODES):
        ct_modes[1, m] = parts[m]
    mixed[...] = to_columns(parts, MODE_SCALE)

    def mix_back(o, carry):
        return carry + spec[o].astype(f32) * mixed[pl.ds(o, 1), :]

    back = lax.fori_loop(0, C, mix_back, jnp.zeros((C, 256), f32), unroll=4)
    y_synthesise_back(back, GRID_SCALE, szb)
    each(group_x, lambda k, t, peer: x_copy(t, peer, szb.at[lax.rem(t, 2)], rzb, zs.at[1], zr.at[1]).start())
    rzb[g] = szb[h]

    def share_copy(peer):
        return pltpu.make_async_remote_copy(
            src_ref=ks3, dst_ref=kr3.at[share], send_sem=k3s, recv_sem=k3r, device_id=peer, device_id_type=MESH
        )

    @pl.when(holds)
    def _():
        all_of(kr2, 15, k2s, k2r).wait_recv()
        total = kr2[0].astype(f32)
        for i in range(1, 16):
            total = total + kr2[i].astype(f32)
        total = total * GRID_SCALE
        ks3[...] = total.astype(bf16)
        kr3[share] = total.astype(bf16)
        each(group_x, lambda k, t, peer: share_copy(peer).start())

    coef_rows = ct_modes[0, q]
    coef_rows = coef_rows + pltpu.roll(coef_rows, 64, 1)
    coef_rows = (coef_rows + pltpu.roll(coef_rows, 32, 1)) * GRID_SCALE
    wide = jnp.transpose(ct_modes[1, q])
    back_columns = jnp.transpose(wide[0:32] + wide[32:64] + wide[64:96] + wide[96:128]) * MODE_SCALE
    for o in range(C):
        sg_ref[o] = (coef_rows * back_columns[:, o : o + 1])[:, 0:32]

    lax.fori_loop(0, BX, spread, 0, unroll=4)
    all_of(rzb, 15, zs.at[1], zr.at[1]).wait_recv()
    modes_all = x_z_synthesise(a * 8, rzb, px_ref, zs_ref)
    upper = lax.broadcasted_iota(jnp.int32, (128, NZ), 0) % 8 < 4
    for part in range(2):
        even, odd = [], []
        for i in (4 * part, 4 * part + 2):
            first, second = modes_all[128 * i : 128 * i + 128], modes_all[128 * i + 128 : 128 * i + 256]
            even.append(jnp.where(upper, first, pltpu.roll(second, 4, 0)))
            odd.append(jnp.where(upper, pltpu.roll(first, 124, 0), second))
        for n in range(16):
            for c, rows in ((2 * n, even), (2 * n + 1, odd)):
                cells = slice(c * 32 + 16 * part, c * 32 + 16 * part + 16)
                value = jnp.concatenate([r[8 * n : 8 * n + 8] for r in rows], axis=0) + oflat[cells, :]
                ig_ref[c, 16 * part : 16 * part + 16, :] = value.astype(bf16)

    for n in range(2):
        all_of((rx, rxb)[n], 15, xs.at[n], xr.at[n]).wait_send()
        all_of((rz, rzb)[n], 15, zs.at[n], zr.at[n]).wait_send()
        all_of((ry, ryb)[n], 15, ys.at[n], yr.at[n, 0]).wait_send()
    halo_wait_send(stk, 0)
    halo_wait_send(dstk, 1)
    def in_shares(has, has_not):
        pl.when(holds)(has)
        pl.when(jnp.logical_not(holds))(has_not)

    in_shares(
        lambda: all_of(kr1, KG_SHARES - 1, k1s, k1r).wait_send(),
        lambda: all_of(kr1, KG_SHARES, k1s, k1r).wait_send(),
    )

    @pl.when(holds)
    def _():
        all_of(kr2, 15, k2s, k2r).wait_send()
        all_of(kr1, 15, k3s, k3r).wait_send()

    in_shares(
        lambda: all_of(kr3, KG_SHARES - 1, k3s, k3r).wait_recv(),
        lambda: all_of(kr3, KG_SHARES, k3s, k3r).wait_recv(),
    )


def finish(kr, ig, out, sg, out_hbm, ig_hbm, sg_hbm, kg_hbm, bg_hbm, kg, bg, store_sem):
    pairs = ((ig, ig_hbm), (out, out_hbm), (sg, sg_hbm), (bg, bg_hbm)) + tuple(
        (kg.at[pl.ds(9 * d, 9)], kg_hbm.at[pl.ds(9 * d, 9)]) for d in range(3)
    )
    stores = [pltpu.make_async_copy(src, dst, store_sem.at[n]) for n, (src, dst) in enumerate(pairs)]
    for store in stores[:3]:
        store.start()
    blocks = [kr[n].astype(f32) for n in range(KG_SHARES)]
    bg[...] = jnp.transpose(blocks[6])[96:97, :]
    stores[3].start()
    for d in range(3):
        for e in range(3):
            for f in range(3):
                n, offset = e * 3 + d, 32 * f
                if n >= 7:
                    n, offset = (n - 7) * 3 + f, 96
                moved = blocks[n] if offset == 0 else pltpu.roll(blocks[n], 128 - offset, 1)
                kg[(d * 3 + e) * 3 + f] = moved[:, 0:32]
        stores[4 + d].start()
    for store in stores:
        store.wait()


def layer(inputs, cotangent, weights, channel_bias, spectral):
    z_analysis, z_synthesis, y_table, y_table_back, x_table, scales, y_analysis = tables()
    x = inputs.reshape(C, BX * BY, NZ)
    ct = cotangent.reshape(C, BX * BY, NZ)
    any_space = pl.BlockSpec(memory_space=pl.ANY)
    vmem = pl.BlockSpec(memory_space=pltpu.VMEM)
    dma = pltpu.SemaphoreType.DMA
    V = pltpu.VMEM
    mode_bufs = [
        V((16, 16, 128), bf16), V((16, 16, 128), bf16),
        V((2, 16, 128), bf16), V((16, 2, 16, 128), bf16),
        V((2, 16, 128), bf16), V((16, 16, 128), bf16),
    ]
    block = (C, BX * BY, NZ)
    operands = (
        x, ct, spectral, weights.reshape(27, C, C), channel_bias.reshape(1, C),
        z_analysis, z_synthesis, y_table, x_table, y_table_back, scales, y_analysis,
    )
    results = pl.pallas_call(
        kernel,
        out_shape=(V(block, bf16), V(block, bf16), V((C, 16, C), f32), V((KG_SHARES, KG_ROWS, 128), bf16)),
        in_specs=[pl.BlockSpec(memory_space=pltpu.HBM)] * 12,
        out_specs=(vmem,) * 4,
        scratch_shapes=[
            V((27, C, C), bf16), V((1, C), f32), V((32, 128), bf16), V((48, 128), bf16),
            V((32, MODES, 128), f32), pltpu.SMEM((NX * MODES,), f32),
            V((32, MODES, 128), f32), V((48, 128), f32), V((32, MODES, 128), f32), V((2, 128, 128), f32),
            V((C, 1152), bf16), V((C, 1152), bf16), V((C, 128), f32),
            V((C, 32, NZ), bf16), V((C, 32, NZ), bf16), V((C, C, 256), bf16),
            V((C * 32, NZ), f32), V((BX, C, LANES), f32), V((BX, C, LANES), f32),
            V((10, 128, WIDE), bf16), V((10, 128, WIDE), bf16), V((12, C, LANES), bf16),
            V((BX, 16, 128), f32),
            *mode_bufs,
            V((2, MODES, 16, 128), f32), V((C, 256), f32), V((C, 256), f32),

            *mode_bufs,
            V((KG_SHARES, KG_ROWS, 128), bf16), V((16, KG_ROWS, 128), bf16),
            V((KG_ROWS, 128), bf16), V((16, KG_ROWS, 128), bf16),
            V((KG_ROWS, 128), bf16),
            V((C * 32, NZ), f32), V((2, C * C, 128), f32), V((C, C, 256), f32),
            pltpu.SemaphoreType.REGULAR, dma((14,)), dma((2, 8)), dma((2, 8)),
            *[dma((2,))] * 3, dma((2, 4)), *[dma((2,))] * 2,
            *[dma] * 6,
        ],
        compiler_params=pltpu.CompilerParams(
            collective_id=0, has_side_effects=True, vmem_limit_bytes=40 * 2**20
        ),
        cost_estimate=pl.CostEstimate(flops=700_000_000, bytes_accessed=4_000_000, transcendentals=131072),
    )(*[pltpu.with_memory_space_constraint(jnp.asarray(operand), pltpu.HBM) for operand in operands])
    outputs, input_grad, spectral_grad, shares = [
        pltpu.with_memory_space_constraint(result, pltpu.VMEM) for result in results
    ]
    outputs, input_grad, spectral_grad, kernel_grad, bias_grad = pl.pallas_call(
        finish,
        out_shape=(
            jax.ShapeDtypeStruct(block, bf16),
            jax.ShapeDtypeStruct(block, bf16),
            jax.ShapeDtypeStruct((C, 16, C), f32),
            jax.ShapeDtypeStruct((27, C, C), f32),
            jax.ShapeDtypeStruct((1, C), f32),
        ),
        in_specs=[vmem] * 4,
        out_specs=(any_space,) * 5,
        scratch_shapes=[
            V((27, C, C), f32), V((1, C), f32), dma((7,)),
        ],
        compiler_params=pltpu.CompilerParams(vmem_limit_bytes=16 * 2**20),
    )(shares, input_grad, outputs, spectral_grad)
    field = (C, BX, BY, NZ)
    return (
        outputs.reshape(field), input_grad.reshape(field), spectral_grad.transpose(0, 2, 1),
        kernel_grad.reshape(3, 3, 3, C, C), bias_grad.reshape(C),
    )


def solution(mesh):
    placed = (P(None, "gx", "gy", None), P(None, "gx", "gy", None), P(), P(), P())
    return jax.shard_map(
        layer,
        mesh=mesh,
        in_specs=placed,
        out_specs=(
            P(None, "gx", "gy", None),
            P(None, "gx", "gy", None),
            P(None, None, ("gx", "gy")),
            P(),
            P(),
        ),
        check_vma=False,
    )
```

```python
import functools
import math

import jax
import jax.numpy as jnp
import numpy as np
from jax import lax
from jax.experimental import pallas as pl
from jax.experimental.pallas import tpu as pltpu
from jax.sharding import PartitionSpec as P

MESH = pl.DeviceIdType.MESH
MODES = 16
C = 32
BX, BY, NZ = 8, 4, 128
NX, NY = 64, 128
LANES = BY * NZ
WIDE = (BY + 2) * NZ
NEIGHBOURS = [(i, j) for i in (-1, 0, 1) for j in (-1, 0, 1) if (i, j) != (0, 0)]
GRID_SCALE = 1.0 / math.sqrt(NX * NY * NZ)
MODE_SCALE = 1.0 / math.sqrt(MODES**3)
Y_CLASSES = ((1, 6), (6, 10), (10, 14), (14, 16))
KG_ROWS = 32
KG_SHARES = 7
f32, bf16 = jnp.float32, jnp.bfloat16
DOT_NT = (((1,), (1,)), ((), ()))
DOT_TN = (((0,), (0,)), ((), ()))
DOT_NN = (((1,), (0,)), ((), ()))


def basis(cells):
    rows = np.arange(MODES)
    frequency = np.where(rows < MODES // 2, rows, rows - MODES // 2 + 1)
    phase = frequency[:, None] * np.arange(cells)[None, :] % cells
    angles = phase * (2.0 * math.pi / cells)
    return np.where((rows < MODES // 2)[:, None], np.cos(angles), np.sin(angles)).astype(np.float32)


def split(array):
    high = array.astype(jnp.bfloat16)
    low = (array - high.astype(np.float32)).astype(jnp.bfloat16)
    return high, low


def tables():
    phi_x, phi_y, phi_z = basis(NX), basis(NY), basis(NZ)
    high, low = split(phi_z)
    z_analysis = np.concatenate([high, low], 0)
    z_synthesis = np.concatenate([high, high, low], 0)
    lanes = np.repeat(phi_y.reshape(MODES, 32, BY), C, axis=2)
    y_table = lanes.transpose(1, 0, 2)
    y_table_back = y_table.reshape(32, MODES, BY, C).transpose(0, 1, 3, 2).reshape(32, MODES, BY * C)
    x_table = phi_x.T.reshape(-1)
    y_scale = np.exp2(np.arange(NY) * 0.6180339887 % 1.0).reshape(32, BY)
    x_scale = np.exp2(np.arange(8 * BY) * 0.6180339887 % 1.0).reshape(8, BY)
    scales = np.repeat(np.concatenate([y_scale, x_scale, 1.0 / x_scale]), C, axis=1).astype(np.float32)
    y_analysis = (y_table / np.repeat(y_scale, C, axis=1)[:, None, :]).astype(np.float32)
    return z_analysis, z_synthesis, np.ascontiguousarray(y_table), np.ascontiguousarray(y_table_back), np.ascontiguousarray(x_table), scales, y_analysis


def dot(a, b, dims):
    return lax.dot_general(a, b, dims, preferred_element_type=f32)


def x_z_synthesise(cell, recv, px_ref, zs_ref):
    values = [recv[p].astype(f32) for p in range(MODES)]
    planes = []
    for i in range(BX):
        total = px_ref[(cell + i) * 16] * values[0]
        for p in range(1, MODES):
            total = total + px_ref[(cell + i) * 16 + p] * values[p]
        planes.append(total)
    total = jnp.concatenate(planes, axis=1)
    high = total.astype(bf16)
    low = (total - high.astype(f32)).astype(bf16)
    return dot(jnp.concatenate([high, low, high], axis=0), zs_ref[...], DOT_TN)


def kernel(
    x_hbm, ct_hbm, spec_hbm, w_hbm, bias_hbm, za_hbm, zs_hbm, py_hbm, px_hbm, pb_hbm, sc_hbm, pa_hbm,
    out_ref, ig_ref, sg_ref, kr3,
    w_raw, bias_row, za_ref, zs_ref, py_ref, px_ref, pb_ref, sc_ref, pa_ref, wide_ref, wf_ref, wb_ref, bias_ref,
    xin, ctin, spec, flat, ct, acc, stk, dstk, dx, tbuf,
    sx, rx, sy, ry, sz, rz, ct_modes, coefs, mixed,
    sxb, rxb, syb, ryb, szb, rzb,
    ks1, kr1, ks2, kr2, ks3,
    oflat, flat2, by_input,
    ready, dma_sem, halo_s, halo_r, xs, xr, ys, yr, zs, zr, k1s, k1r, k2s, k2r, k3s, k3r,
):
    a, b = lax.axis_index("gx"), lax.axis_index("gy")
    h, q = b // 16, lax.rem(b, 16)
    g = 2 * a + h
    partner = (3 - b // 8) * 8 + lax.rem(b, 8)

    load_x = pltpu.make_async_copy(x_hbm, xin, dma_sem.at[0])
    load_x.start()

    def group_x(k):
        rank, other, core = k // 4, lax.rem(k // 2, 2), lax.rem(k, 2)
        steps = jnp.where(rank == 1, 3, jnp.where(rank == 0, 0, rank - 1))
        ta = 2 * lax.rem(a // 2 + steps, 4) + lax.rem(a + core, 2)
        th = lax.rem(h + other, 2)
        return 2 * ta + th, (ta, jnp.where(other == 0, b, partner))

    def group_y(k):
        rank, other = k // 2, lax.rem(k, 2)
        steps = jnp.where(lax.rem(rank, 2) == 1, (rank + 1) // 2, 8 - rank // 2)
        t = 8 * lax.rem(q // 8 + other, 2) + lax.rem(lax.rem(q, 8) + steps, 8)
        return t, (a, t + 16 * h)

    def each(members, action, count=15):
        def step(n, carry):
            action(count - n, *members(count - n))
            return carry

        lax.fori_loop(0, count, step, 0, unroll=True)

    def there(da, db):
        ok = None
        if da == 1:
            ok = a < 7
        if da == -1:
            ok = a > 0
        if db == 1:
            ok = (b < 31) if ok is None else ok & (b < 31)
        if db == -1:
            ok = (b > 0) if ok is None else ok & (b > 0)
        return ok

    barrier = pltpu.get_barrier_semaphore()

    def greet(k, t, peer):
        pl.semaphore_signal(barrier, inc=1, device_id=peer, device_id_type=MESH)

    each(group_x, greet)
    each(group_y, greet, 9)
    awaited = 24
    for da, db in NEIGHBOURS:
        if db == 0:
            continue

        @pl.when(there(da, db))
        def _():
            pl.semaphore_signal(barrier, inc=1, device_id=(a + da, b + db), device_id_type=MESH)

        awaited = awaited + jnp.where(there(da, db), 1, 0)

    load_ct = pltpu.make_async_copy(ct_hbm, ctin, dma_sem.at[1])
    load_spec = pltpu.make_async_copy(
        spec_hbm.at[:, :, pl.ds(pl.multiple_of(g * 256, 256), 256)], spec, dma_sem.at[2]
    )
    small = [
        pltpu.make_async_copy(src, dst, dma_sem.at[5 + n])
        for n, (src, dst) in enumerate(
            ((za_hbm, za_ref), (px_hbm, px_ref), (sc_hbm, sc_ref), (pa_hbm, pa_ref), (w_hbm, w_raw), (bias_hbm, bias_row), (zs_hbm, zs_ref), (py_hbm, py_ref), (pb_hbm, pb_ref))
        )
    ]
    for load in small:
        load.start()
    load_ct.start()
    load_spec.start()

    def x_copy(t, peer, src, buf, ssem, rsem):
        return pltpu.make_async_remote_copy(
            src_ref=src, dst_ref=buf.at[g], send_sem=ssem, recv_sem=rsem,
            device_id=peer, device_id_type=MESH,
        )

    def y_copy(t, peer, src, buf, ssem, rsem):
        return pltpu.make_async_remote_copy(
            src_ref=src, dst_ref=buf.at[q], send_sem=ssem, recv_sem=rsem,
            device_id=peer, device_id_type=MESH,
        )

    def all_of(buf, count, ssem, rsem):
        return pltpu.make_async_remote_copy(
            src_ref=buf.at[pl.ds(0, count)], dst_ref=buf.at[pl.ds(0, count)], send_sem=ssem, recv_sem=rsem,
            device_id=group_y(1)[1], device_id_type=MESH,
        )

    def halo_copy(index, field, n, da, db):
        sx_ = pl.ds(8, 1) if da == 1 else pl.ds(1, 1) if da == -1 else pl.ds(1, 8)
        dx_ = pl.ds(0, 1) if da == 1 else pl.ds(9, 1) if da == -1 else pl.ds(1, 8)
        sl = pl.ds(512, 128) if db == 1 else pl.ds(128, 128) if db == -1 else pl.ds(128, 512)
        dl = pl.ds(0, 128) if db == 1 else pl.ds(640, 128) if db == -1 else pl.ds(128, 512)
        return pltpu.make_async_remote_copy(
            src_ref=field.at[sx_, pl.ds(32, 32), sl], dst_ref=field.at[dx_, pl.ds(32, 32), dl],
            send_sem=halo_s.at[n, index], recv_sem=halo_r.at[n, index],
            device_id=(a + da, b + db), device_id_type=MESH,
        )

    def halo_start(field, n):
        for index, (da, db) in enumerate(NEIGHBOURS):

            @pl.when(there(da, db))
            def _():
                halo_copy(index, field, n, da, db).start()

    def halo_wait_recv(field, n):
        for index, (da, db) in enumerate(NEIGHBOURS):

            @pl.when(there(-da, -db))
            def _():
                halo_copy(index, field, n, da, db).wait_recv()

    def halo_wait_send(field, n):
        for index, (da, db) in enumerate(NEIGHBOURS):

            @pl.when(there(da, db))
            def _():
                halo_copy(index, field, n, da, db).wait_send()

    def zero_rim(field):
        @pl.when(a == 0)
        def _():
            field[0, 32:64, :] = jnp.zeros((C, WIDE), bf16)

        @pl.when(a == 7)
        def _():
            field[9, 32:64, :] = jnp.zeros((C, WIDE), bf16)

        @pl.when(b == 0)
        def _():
            for i in range(10):
                field[i, 32:64, 0:128] = jnp.zeros((C, NZ), bf16)

        @pl.when(b == 31)
        def _():
            for i in range(10):
                field[i, 32:64, 640:768] = jnp.zeros((C, NZ), bf16)

    def z_analyse(i, tiles):
        rows = jnp.concatenate(tiles, axis=0)
        both = dot(za_ref[...], rows, DOT_NT)
        tbuf[i] = both[:16] + both[16:]

    def x_partials(buf):
        rows = [tbuf[i] for i in range(BX)]

        def step(p, carry):
            total = px_ref[(a * 8) * 16 + p] * rows[0]
            for i in range(1, BX):
                total = total + px_ref[(a * 8 + i) * 16 + p] * rows[i]
            buf[p] = (total * sc_ref[pl.ds(32 + a, 1), :]).astype(bf16)
            return carry

        lax.fori_loop(0, 16, step, 0, unroll=4)

    def y_blocks(recv, send):
        for half in range(2):
            total = recv[half].astype(f32) * sc_ref[40:41, :]
            for i in range(1, 8):
                total = total + recv[2 * i + half].astype(f32) * sc_ref[40 + i : 41 + i, :]
            send[half] = (total * sc_ref[pl.ds(block_of(q, half), 1), :]).astype(bf16)

    def block_of(member, half):
        return 16 * half + jnp.where(h == half, member, lax.rem(member + 8, 16))

    def y_analyse(recv, n):
        def step(k, carry):
            result = list(carry)
            block = group_y(k)[0]
            for half in range(2):
                value = recv[block, half].astype(f32)
                place = block_of(block, half)
                for m in range(MODES):
                    result[m] = result[m] + value * pa_ref[place, pl.ds(m, 1), :]
            return tuple(result)

        result = step(0, tuple(jnp.zeros((16, 128), f32) for _ in range(MODES)))
        for near, (low, high) in enumerate(Y_CLASSES):
            all_of(recv, high - low, ys.at[n], yr.at[n, near]).wait_recv()
            result = lax.fori_loop(low, high, step, result, unroll=True)
        return result

    def y_class(k):
        return jnp.where(k < 6, 0, jnp.where(k < 10, 1, jnp.where(k < 14, 2, 3)))

    def to_columns(parts, scale):
        wide = jnp.transpose(jnp.concatenate(parts, axis=0))
        return (wide[0:32] + wide[32:64] + wide[64:96] + wide[96:128]) * scale

    def y_synthesise(modes, scale, send):
        y_project(jnp.transpose(jnp.concatenate([modes * scale] * 4, axis=0)), py_ref, send)

    def y_synthesise_back(modes, scale, send):
        for n in range(2):
            for j in range(BY):
                wide_ref[n, pl.ds(j, C, stride=BY), :] = modes[:, 128 * n : 128 * n + 128] * scale
        tall = jnp.concatenate([jnp.transpose(wide_ref[n, 0:128, :]) for n in range(2)], axis=0)
        y_project(tall, pb_ref, send)

    def y_project(tall, table, send):
        for half in range(2):
            place = block_of(q, half)
            total = table[place, pl.ds(0, 1), :] * tall[0:16]
            for m in range(1, MODES):
                total = total + table[place, pl.ds(m, 1), :] * tall[16 * m : 16 * m + 16]
            send[half] = total.astype(send.dtype)

    lane = lax.broadcasted_iota(jnp.int32, (C, NZ), 1)

    def shift_rows(field, ones):
        def step(i, carry):
            for y in range(BY + 2):
                cells = slice(y * NZ, (y + 1) * NZ)
                value = field[i, 32:64, cells].astype(f32)
                before = jnp.where(lane == 0, 0.0, pltpu.roll(value, 1, 1))
                after = jnp.where(lane == NZ - 1, 0.0, pltpu.roll(value, NZ - 1, 1))
                field[i, 0:32, cells] = before.astype(bf16)
                field[i, 64:96, cells] = after.astype(bf16)
            return carry

        lax.fori_loop(0, 10, step, 0, unroll=2)

    def fill_ones(field):
        def step(i, carry):
            field[i, 96:128, :] = jnp.ones((32, WIDE), bf16)
            return carry

        lax.fori_loop(0, 10, step, 0)

    def convolve(field, weights, shift=None):
        def step(i, carry):
            total = None
            for d in range(3):
                for e in range(3):
                    tap = (d * 3 + e) * 128
                    part = dot(
                        weights[:, tap : tap + 128], field[i + d, :, e * NZ : e * NZ + LANES], DOT_NN
                    )
                    total = part if total is None else total + part
            acc[i] = total if shift is None else total + shift
            return carry

        lax.fori_loop(0, BX, step, 0, unroll=2)

    def unflatten(source, write):
        def step(c, carry):
            flat[pl.ds(pl.multiple_of(c * 32, 32), 32), :] = source[c].astype(f32)
            return carry

        lax.fori_loop(0, C, step, 0, unroll=8)

        def step2(i, carry):
            tiles = [flat[pl.ds(i * BY + y, C, stride=32), :] for y in range(BY)]
            write(i, tiles)
            return carry

        lax.fori_loop(0, BX, step2, 0, unroll=4)

    def flatten(source, target):
        def step(c, carry):
            target[c] = source[pl.ds(pl.multiple_of(c * 32, 32), 32), :].astype(bf16)
            return carry

        lax.fori_loop(0, C, step, 0, unroll=8)

    def prepare_weights():
        row = lax.broadcasted_iota(jnp.int32, (C, 128), 0)
        column = lax.broadcasted_iota(jnp.int32, (C, 128), 1)
        place = [jnp.where(column == row + 32 * f, 1.0, 0.0).astype(bf16) for f in range(3)]
        for tap in range(9):
            total, back_total = None, None
            for f in range(3):
                part = dot(w_raw[tap * 3 + f], place[f], DOT_NN)
                total = part if total is None else total + part
                part = dot(w_raw[(8 - tap) * 3 + 2 - f], place[f], DOT_TN)
                back_total = part if back_total is None else back_total + part
            wf_ref[:, tap * 128 : tap * 128 + 128] = total.astype(bf16)
            wb_ref[:, tap * 128 : tap * 128 + 128] = back_total.astype(bf16)
        spread = jnp.where(column[:, :C] == row[:, :C], jnp.broadcast_to(bias_row[...], (C, C)), 0.0)
        bias_ref[...] = jnp.broadcast_to(jnp.sum(spread, axis=1, keepdims=True), (C, 128))

    load_x.wait()
    small[0].wait()
    small[1].wait()
    small[2].wait()

    def write_x(i, tiles):
        tiles = [t.astype(bf16) for t in tiles]
        for y in range(BY):
            stk[i + 1, 32:64, (y + 1) * NZ : (y + 2) * NZ] = tiles[y]
        z_analyse(i, tiles)

    unflatten(xin, write_x)
    x_partials(sx)
    pl.semaphore_wait(barrier, awaited)
    for k in (6, 8):
        pl.semaphore_signal(ready, inc=1, device_id=group_y(k)[1], device_id_type=MESH)
    each(group_x, lambda k, t, peer: x_copy(t, peer, sx.at[t], rx, xs.at[0], xr.at[0]).start())
    rx[g] = sx[g]
    halo_start(stk, 0)

    zero_rim(stk)
    fill_ones(stk)
    for load in small[3:]:
        load.wait()
    prepare_weights()
    load_ct.wait()

    def write_ct(i, tiles):
        for y in range(BY):
            ct[i, :, y * NZ : (y + 1) * NZ] = tiles[y]

    unflatten(ctin, write_ct)
    for i in (0, 1, 10, 11):
        dx[i] = jnp.zeros((C, LANES), bf16)

    all_of(rx, 15, xs.at[0], xr.at[0]).wait_recv()
    y_blocks(rx, sy)
    pl.semaphore_wait(ready, 2)
    each(group_y, lambda k, t, peer: y_copy(t, peer, sy, ry, ys.at[0], yr.at[0, y_class(k)]).start())
    ry[q] = sy[...]

    halo_wait_recv(stk, 0)
    shift_rows(stk, True)
    convolve(stk, wf_ref, jnp.concatenate([bias_ref[...]] * BY, axis=1))
    load_spec.wait()

    def widen(o, carry):
        for n in range(2):
            flat2[n, pl.ds(pl.multiple_of(o * 32, 32), 32), :] = spec[o, :, 128 * n : 128 * n + 128].astype(f32)
        return carry

    lax.fori_loop(0, C, widen, 0, unroll=4)

    def gather(c, carry):
        for n in range(2):
            by_input[c, :, 128 * n : 128 * n + 128] = flat2[n, pl.ds(c, C, stride=32), :]
        return carry

    lax.fori_loop(0, C, gather, 0, unroll=4)

    parts = y_analyse(ry, 0)
    for m in range(MODES):
        ct_modes[0, m] = parts[m]
    coefs[...] = to_columns(parts, GRID_SCALE)

    def mix(c, carry):
        return carry + by_input[c] * coefs[pl.ds(c, 1), :]

    y_synthesise(lax.fori_loop(0, C, mix, jnp.zeros((C, 256), f32), unroll=4), MODE_SCALE, sz)
    each(group_x, lambda k, t, peer: x_copy(t, peer, sz.at[lax.rem(t, 2)], rz, zs.at[0], zr.at[0]).start())
    rz[g] = sz[h]
    all_of(rz, 15, zs.at[0], zr.at[0]).wait_recv()

    root = math.sqrt(2.0 / math.pi)

    modes_all = x_z_synthesise(a * 8, rz, px_ref, zs_ref)

    def point(i):
        modes = modes_all[128 * i : 128 * i + 128]
        tiles = []
        for y in range(BY):
            cells = slice(y * NZ, (y + 1) * NZ)
            v = acc[i, :, cells] + modes[y * C : (y + 1) * C]
            square = v * v
            t = jnp.tanh(v * (square * (0.044715 * root) + root))
            half = 0.5 * t + 0.5
            slope = half * ((v * (square * (3 * 0.044715 * root) + root)) * (1.0 - t) + 1.0)
            acc[i, :, cells] = v * half
            delta = (ct[i, :, cells] * slope).astype(bf16)
            dstk[i + 1, 32:64, (y + 1) * NZ : (y + 2) * NZ] = delta
            dx[i + 2, :, cells] = delta
            tiles.append(delta)
        z_analyse(i, tiles)

    for i in range(BX):
        point(i)

    x_partials(sxb)
    each(group_x, lambda k, t, peer: x_copy(t, peer, sxb.at[t], rxb, xs.at[1], xr.at[1]).start())
    rxb[g] = sxb[g]

    def planes(cut):
        return jnp.concatenate([cut(i) for i in range(10)], axis=1)

    idle = jnp.zeros((C, LANES), bf16)
    shifted = [planes(lambda i, d=d: dx[i + 2 - d]) for d in range(3)] + [planes(lambda i: idle)]
    windows = [planes(lambda i, e=e: stk[i, : 112 if e == 1 else 96, e * NZ : e * NZ + LANES]) for e in range(3)]
    kgt = dot(jnp.concatenate(windows, axis=0), jnp.concatenate(shifted, axis=0), DOT_NT)
    empty = jnp.zeros((32, 128), f32)
    kgt = [
        jnp.concatenate([kgt[0:96], empty], axis=0),
        jnp.concatenate([kgt[96:208], empty[:16]], axis=0),
        jnp.concatenate([kgt[208:304], empty], axis=0),
    ]
    columns = [jnp.transpose(kgt[e]) for e in range(3)]
    kgp = [columns[e][32 * d : 32 * d + 32] for e in range(3) for d in range(3)]

    for n in range(7):
        block = kgp[n]
        if n < 6:
            block = jnp.where(lane >= 96, pltpu.roll(kgp[7 + n // 3], 96 - 32 * (n % 3), 1), block)
        else:
            block = jnp.where(lane >= 96, kgp[4], block)
        ks1[n] = block.astype(bf16)
    def share_of(t):
        return t // 2 + lax.rem(t, 2), (lax.rem(t // 2, 2) == 0) & (t // 2 + lax.rem(t, 2) < KG_SHARES)

    share, holds = share_of(g)

    def k1_start(k, t, peer):
        target, takes = share_of(t)

        @pl.when(takes)
        def _():
            x_copy(t, peer, ks1.at[target], kr1, k1s, k1r).start()

    each(group_x, k1_start)

    halo_start(dstk, 1)

    zero_rim(dstk)
    fill_ones(dstk)
    def spread(i, carry):
        for y in range(BY):
            oflat[pl.ds(i * BY + y, C, stride=32), :] = acc[i, :, y * NZ : (y + 1) * NZ]
        return carry

    lax.fori_loop(0, BX, spread, 0, unroll=4)
    flatten(oflat, out_ref)

    all_of(rxb, 15, xs.at[1], xr.at[1]).wait_recv()
    y_blocks(rxb, syb)
    each(group_y, lambda k, t, peer: y_copy(t, peer, syb, ryb, ys.at[1], yr.at[1, y_class(k)]).start())
    ryb[q] = syb[...]

    @pl.when(holds)
    def _():
        all_of(kr1, 15, k1s, k1r).wait_recv()
        kr1[g] = ks1[share]
        total = kr1[0].astype(f32)
        for i in range(1, 16):
            total = total + kr1[i].astype(f32)
        ks2[...] = total.astype(bf16)
        kr2[q] = total.astype(bf16)
        each(group_y, lambda k, t, peer: y_copy(t, peer, ks2, kr2, k2s, k2r).start())

    halo_wait_recv(dstk, 1)
    shift_rows(dstk, False)
    convolve(dstk, wb_ref)

    parts = y_analyse(ryb, 1)
    for m in range(MODES):
        ct_modes[1, m] = parts[m]
    mixed[...] = to_columns(parts, MODE_SCALE)

    def mix_back(o, carry):
        return carry + spec[o].astype(f32) * mixed[pl.ds(o, 1), :]

    back = lax.fori_loop(0, C, mix_back, jnp.zeros((C, 256), f32), unroll=4)
    y_synthesise_back(back, GRID_SCALE, szb)
    each(group_x, lambda k, t, peer: x_copy(t, peer, szb.at[lax.rem(t, 2)], rzb, zs.at[1], zr.at[1]).start())
    rzb[g] = szb[h]

    def share_copy(peer):
        return pltpu.make_async_remote_copy(
            src_ref=ks3, dst_ref=kr3.at[share], send_sem=k3s, recv_sem=k3r, device_id=peer, device_id_type=MESH
        )

    @pl.when(holds)
    def _():
        all_of(kr2, 15, k2s, k2r).wait_recv()
        total = kr2[0].astype(f32)
        for i in range(1, 16):
            total = total + kr2[i].astype(f32)
        total = total * GRID_SCALE
        ks3[...] = total.astype(bf16)
        kr3[share] = total.astype(bf16)
        each(group_x, lambda k, t, peer: share_copy(peer).start())

    coef_rows = ct_modes[0, q]
    coef_rows = coef_rows + pltpu.roll(coef_rows, 64, 1)
    coef_rows = (coef_rows + pltpu.roll(coef_rows, 32, 1)) * GRID_SCALE
    wide = jnp.transpose(ct_modes[1, q])
    back_columns = jnp.transpose(wide[0:32] + wide[32:64] + wide[64:96] + wide[96:128]) * MODE_SCALE
    for o in range(C):
        sg_ref[o] = (coef_rows * back_columns[:, o : o + 1])[:, 0:32]

    lax.fori_loop(0, BX, spread, 0, unroll=4)
    all_of(rzb, 15, zs.at[1], zr.at[1]).wait_recv()
    modes_all = x_z_synthesise(a * 8, rzb, px_ref, zs_ref)
    upper = lax.broadcasted_iota(jnp.int32, (128, NZ), 0) % 8 < 4
    for part in range(2):
        even, odd = [], []
        for i in (4 * part, 4 * part + 2):
            first, second = modes_all[128 * i : 128 * i + 128], modes_all[128 * i + 128 : 128 * i + 256]
            even.append(jnp.where(upper, first, pltpu.roll(second, 4, 0)))
            odd.append(jnp.where(upper, pltpu.roll(first, 124, 0), second))
        for n in range(16):
            for c, rows in ((2 * n, even), (2 * n + 1, odd)):
                cells = slice(c * 32 + 16 * part, c * 32 + 16 * part + 16)
                value = jnp.concatenate([r[8 * n : 8 * n + 8] for r in rows], axis=0) + oflat[cells, :]
                ig_ref[c, 16 * part : 16 * part + 16, :] = value.astype(bf16)

    for n in range(2):
        all_of((rx, rxb)[n], 15, xs.at[n], xr.at[n]).wait_send()
        all_of((rz, rzb)[n], 15, zs.at[n], zr.at[n]).wait_send()
        all_of((ry, ryb)[n], 15, ys.at[n], yr.at[n, 0]).wait_send()
    halo_wait_send(stk, 0)
    halo_wait_send(dstk, 1)
    def in_shares(has, has_not):
        pl.when(holds)(has)
        pl.when(jnp.logical_not(holds))(has_not)

    in_shares(
        lambda: all_of(kr1, KG_SHARES - 1, k1s, k1r).wait_send(),
        lambda: all_of(kr1, KG_SHARES, k1s, k1r).wait_send(),
    )

    @pl.when(holds)
    def _():
        all_of(kr2, 15, k2s, k2r).wait_send()
        all_of(kr1, 15, k3s, k3r).wait_send()

    in_shares(
        lambda: all_of(kr3, KG_SHARES - 1, k3s, k3r).wait_recv(),
        lambda: all_of(kr3, KG_SHARES, k3s, k3r).wait_recv(),
    )


def finish(kr, ig, out, sg, out_hbm, ig_hbm, sg_hbm, kg_hbm, bg_hbm, kg, bg, store_sem):
    pairs = ((ig, ig_hbm), (out, out_hbm), (sg, sg_hbm), (bg, bg_hbm)) + tuple(
        (kg.at[pl.ds(9 * d, 9)], kg_hbm.at[pl.ds(9 * d, 9)]) for d in range(3)
    )
    stores = [pltpu.make_async_copy(src, dst, store_sem.at[n]) for n, (src, dst) in enumerate(pairs)]
    for store in stores[:3]:
        store.start()
    blocks = [kr[n].astype(f32) for n in range(KG_SHARES)]
    bg[...] = jnp.transpose(blocks[6])[96:97, :]
    stores[3].start()
    for d in range(3):
        for e in range(3):
            for f in range(3):
                n, offset = e * 3 + d, 32 * f
                if n >= 7:
                    n, offset = (n - 7) * 3 + f, 96
                moved = blocks[n] if offset == 0 else pltpu.roll(blocks[n], 128 - offset, 1)
                kg[(d * 3 + e) * 3 + f] = moved[:, 0:32]
        stores[4 + d].start()
    for store in stores:
        store.wait()


def layer(inputs, cotangent, weights, channel_bias, spectral):
    z_analysis, z_synthesis, y_table, y_table_back, x_table, scales, y_analysis = tables()
    x = inputs.reshape(C, BX * BY, NZ)
    ct = cotangent.reshape(C, BX * BY, NZ)
    any_space = pl.BlockSpec(memory_space=pl.ANY)
    vmem = pl.BlockSpec(memory_space=pltpu.VMEM)
    dma = pltpu.SemaphoreType.DMA
    V = pltpu.VMEM
    mode_bufs = [
        V((16, 16, 128), bf16), V((16, 16, 128), bf16),
        V((2, 16, 128), bf16), V((16, 2, 16, 128), bf16),
        V((2, 16, 128), bf16), V((16, 16, 128), bf16),
    ]
    block = (C, BX * BY, NZ)
    operands = (
        x, ct, spectral, weights.reshape(27, C, C), channel_bias.reshape(1, C),
        z_analysis, z_synthesis, y_table, x_table, y_table_back, scales, y_analysis,
    )
    results = pl.pallas_call(
        kernel,
        out_shape=(V(block, bf16), V(block, bf16), V((C, 16, C), f32), V((KG_SHARES, KG_ROWS, 128), bf16)),
        in_specs=[pl.BlockSpec(memory_space=pltpu.HBM)] * 12,
        out_specs=(vmem,) * 4,
        scratch_shapes=[
            V((27, C, C), bf16), V((1, C), f32), V((32, 128), bf16), V((48, 128), bf16),
            V((32, MODES, 128), f32), pltpu.SMEM((NX * MODES,), f32),
            V((32, MODES, 128), f32), V((48, 128), f32), V((32, MODES, 128), f32), V((2, 136, 128), f32),
            V((C, 1152), bf16), V((C, 1152), bf16), V((C, 128), f32),
            V((C, 32, NZ), bf16), V((C, 32, NZ), bf16), V((C, C, 256), bf16),
            V((C * 32 + 32, NZ), f32), V((BX, C, LANES), f32), V((BX, C, LANES), f32),
            V((10, 128, WIDE), bf16), V((10, 128, WIDE), bf16), V((12, C, LANES), bf16),
            V((BX, 16, 128), f32),
            *mode_bufs,
            V((2, MODES, 16, 128), f32), V((C, 256), f32), V((C, 256), f32),

            *mode_bufs,
            V((KG_SHARES, KG_ROWS, 128), bf16), V((16, KG_ROWS, 128), bf16),
            V((KG_ROWS, 128), bf16), V((16, KG_ROWS, 128), bf16),
            V((KG_ROWS, 128), bf16),
            V((C * 32 + 32, NZ), f32), V((2, C * C + 32, 128), f32), V((C, C, 256), f32),
            pltpu.SemaphoreType.REGULAR, dma((14,)), dma((2, 8)), dma((2, 8)),
            *[dma((2,))] * 3, dma((2, 4)), *[dma((2,))] * 2,
            *[dma] * 6,
        ],
        compiler_params=pltpu.CompilerParams(
            collective_id=0, has_side_effects=True, vmem_limit_bytes=40 * 2**20
        ),
        cost_estimate=pl.CostEstimate(flops=700_000_000, bytes_accessed=4_000_000, transcendentals=131072),
    )(*[pltpu.with_memory_space_constraint(jnp.asarray(operand), pltpu.HBM) for operand in operands])
    outputs, input_grad, spectral_grad, shares = [
        pltpu.with_memory_space_constraint(result, pltpu.VMEM) for result in results
    ]
    outputs, input_grad, spectral_grad, kernel_grad, bias_grad = pl.pallas_call(
        finish,
        out_shape=(
            jax.ShapeDtypeStruct(block, bf16),
            jax.ShapeDtypeStruct(block, bf16),
            jax.ShapeDtypeStruct((C, 16, C), f32),
            jax.ShapeDtypeStruct((27, C, C), f32),
            jax.ShapeDtypeStruct((1, C), f32),
        ),
        in_specs=[vmem] * 4,
        out_specs=(any_space,) * 5,
        scratch_shapes=[
            V((27, C, C), f32), V((1, C), f32), dma((7,)),
        ],
        compiler_params=pltpu.CompilerParams(vmem_limit_bytes=16 * 2**20),
    )(shares, input_grad, outputs, spectral_grad)
    field = (C, BX, BY, NZ)
    return (
        outputs.reshape(field), input_grad.reshape(field), spectral_grad.transpose(0, 2, 1),
        kernel_grad.reshape(3, 3, 3, C, C), bias_grad.reshape(C),
    )


def solution(mesh):
    placed = (P(None, "gx", "gy", None), P(None, "gx", "gy", None), P(), P(), P())
    return jax.shard_map(
        layer,
        mesh=mesh,
        in_specs=placed,
        out_specs=(
            P(None, "gx", "gy", None),
            P(None, "gx", "gy", None),
            P(None, None, ("gx", "gy")),
            P(),
            P(),
        ),
        check_vma=False,
    )
```
